128 devices in a mesh: slab: 128 (over x, z, y, core).
Axes of the slice: x: 4, y: 4, z: 4, core: 2. Of those that a mesh axis runs over, the one named last changes fastest.
Arguments:
- velocity: float32 [3, 1024, 32, 128], P(None, 'slab'), may hold values from -6 to 6
- node_coords: float32 [16384, 3, 128], P('slab'), may hold values from 0 to 1
- node_force: float32 [16384, 3, 128], P('slab'), may hold values from -12 to 12
- block_slab: int32 [16384, 1], P('slab'), may hold values from 0 to 127; in each aligned block of 128 rows (0 to 127, 128 to 255, ...) at most 2 rows name the same one
- block_offset: int32 [16384, 2], P('slab'), may hold values from 1 to 25
Outputs:
- new_velocity: float32 [3, 1024, 32, 128], P(None, 'slab')
- node_velocity: float32 [16384, 3, 128], P('slab')
The draws below stay inside these ranges and needn't reach their ends.
Inputs may be any that keep to these rules, and one draw needn't show every extreme that they name: `block_slab`: among the 128 blocks of one device at most 2 name the same slab, and in every draw some device has exactly 2 blocks in one slab.
All inputs are finite; a program needn't handle non-finite values.
Results may differ from the reference program's by a relative error of at most 0.0003.
Values sent between devices are 32-bit elements; how exact they have to be, the bound alone decides.
No kernel may reach another device: no remote copies, remote signals or barrier semaphores. Data moves between devices by JAX's collectives and lax.ppermute only.
A program may use at most 128 MiB of HBM per device.

```python
import math
import jax
import jax.numpy as jnp
import numpy as np
from jax import lax

CX = 8
NY = 32
NZ = 128
BS = 128
BLK_DEV = 128
SUBSTEPS = 3
CAP = 2
NX = 1024
BLOCKS = 16384
N_SLAB = 128


def plant(values, own_key, low, largest):
    index_at = [jax.random.randint(jax.random.fold_in(own_key, axis), (), 0, length) for axis, length in enumerate(values.shape)]
    longest = values.shape.index(max(values.shape))
    neighbour = index_at[:longest] + [(index_at[longest] + 1) % values.shape[longest]] + index_at[longest + 1:]
    return values.at[tuple(index_at)].set(low).at[tuple(neighbour)].set(largest)


def steps_of(own_key, shape, cuts, low, high):
    loudness = 1.0
    for axis_at, blocks in cuts:
        heights = jax.random.uniform(jax.random.fold_in(jax.random.fold_in(own_key, 6), axis_at), (blocks,), jnp.float32, low / len(cuts), high / len(cuts))
        loudness = loudness * jnp.repeat(jnp.exp(heights), shape[axis_at] // blocks).reshape((-1,) + (1,) * (len(shape) - 1 - axis_at))
    return loudness


def deal_out(rng, own, number, rows, amount, top, bound, slope):
    sequence = jax.random.permutation(rng, amount)
    crowded, usual = load_shares(amount, rows * top, bound, slope, True), load_shares(amount, rows * top, bound, slope, False)
    places = jnp.arange(amount)

    def named(sizes, offset_by):
        used = int((sizes > 0).sum())
        fixed = max(1, used // 4)
        passed = fixed + (places - fixed + offset_by * (used - fixed)) % max(1, amount - fixed)
        return jnp.zeros((amount,), jnp.int32).at[sequence[jnp.where(places < fixed, places, passed)]].set(jnp.asarray(sizes, jnp.int32))

    sizes = jnp.where(number % 4 == 0, named(crowded, number // 4), named(usual, number - number // 4 - 1))
    mixed = jax.random.permutation(jax.random.fold_in(own, 3), amount)
    giver, sink = mixed[0:amount // 2 * 2:2], mixed[1:amount // 2 * 2:2]
    slack = jnp.minimum(sizes[giver] - 1, bound - sizes[sink]) // 2
    slack = jnp.where((giver == sequence[0]) | (sink == sequence[0]) | (sizes[sink] == 0), 0, jnp.maximum(slack, 0))
    passed = jax.random.randint(jax.random.fold_in(own, 4), (amount // 2,), 0, 1 << 20) % (slack + 1)
    sizes = sizes.at[giver].add(-passed).at[sink].add(passed)
    items = jnp.searchsorted(jnp.cumsum(sizes), jnp.arange(rows * top), side="right").astype(jnp.int32)
    grid = items.reshape(top, rows).T
    grid = grid[jax.random.permutation(jax.random.fold_in(own, 1), rows)]
    offset_by = jax.random.randint(jax.random.fold_in(own, 2), (rows, 1), 0, top)
    return jnp.take_along_axis(grid, (jnp.arange(top)[None, :] + offset_by) % top, axis=1)


def load_shares(amount, total, reach, slope, full):
    weights = [(1 << 20) // math.isqrt(standing ** slope) + 1 for standing in range(1, amount + 1)]
    largest = reach if full else min(reach, max(-(-total // amount), total * weights[0] // sum(weights)))
    least = 1 if total - largest >= amount - 1 else 0
    holding, spare = [largest] + [least] * (amount - 1), total - largest - least * (amount - 1)
    while spare > 0:
        candidates = [i for i in range(1, amount) if holding[i] < largest] or [i for i in range(1, amount) if holding[i] < reach]
        whole, remaining = sum([weights[i] for i in candidates]), spare
        for i in candidates:
            addition = min(reach - holding[i], max(1, remaining * weights[i] // whole), spare)
            holding[i] = holding[i] + addition
            spare = spare - addition
    return np.array(holding)


def bell_draw(rng, extent, deviation, limit, cuts=(), held_as=jnp.bfloat16):
    level = steps_of(rng, extent, cuts, -0.22, 0.18) if cuts else 1.0
    values = jax.random.normal(rng, extent, jnp.float32) * deviation * level
    return jnp.minimum(jnp.maximum(values, -limit), limit).astype(held_as)


def setup_inputs(seed: int = 0) -> dict:
    arg_keys = jax.random.split(jax.random.key(seed), 6)
    velocity = bell_draw(arg_keys[0], (3, NX, NY, NZ), 1.0, 6.0, ((1, 128),), jnp.float32)
    node_coords = jnp.clip(1.0 * jax.random.uniform(arg_keys[1], (BLOCKS, 3, BS), jnp.float32) ** steps_of(arg_keys[1], (BLOCKS, 3, BS), ((0, 128),), -0.2, 0.2), 0.0, 1.0)
    node_force = bell_draw(arg_keys[2], (BLOCKS, 3, BS), 2.0, 12.0, ((0, 128),), jnp.float32)
    block_slab_keys = jax.random.split(jax.random.fold_in(arg_keys[3], 1), BLOCKS // BLK_DEV)
    block_slab_turns = jax.random.permutation(jax.random.fold_in(arg_keys[3], 3), BLOCKS // BLK_DEV)
    block_slab = jax.vmap(lambda own, number: deal_out(jax.random.fold_in(arg_keys[3], 2), own, number, BLK_DEV, N_SLAB, 1, CAP, 2))(block_slab_keys, block_slab_turns).reshape((BLOCKS, 1))
    block_offset = plant(jax.random.randint(arg_keys[4], (BLOCKS, 2), 1, min(NY, NZ) - 6), jax.random.fold_in(arg_keys[4], 1), 1, (min(NY, NZ) - 6) - 1).astype(jnp.int32)
    return {"velocity": velocity, "node_coords": node_coords, "node_force": node_force, "block_slab": block_slab, "block_offset": block_offset}


time_step = 0.1
viscosity = 0.2


def kernel(distance):
    return jnp.where(jnp.abs(distance) < 2.0, 0.25 * (1.0 + jnp.cos(0.5 * math.pi * distance)), 0.0)


def node_weights(coords):
    planes = jnp.arange(CX, dtype=jnp.float32)
    taps = jnp.arange(8, dtype=jnp.float32)
    weight_x = kernel(planes[None, None, :] - 1.0 - (CX - 4) * coords[:, 0, :, None])
    weight_y = kernel(taps[None, None, :] - 1.0 - 5.0 * coords[:, 1, :, None])
    weight_z = kernel(taps[None, None, :] - 1.0 - 5.0 * coords[:, 2, :, None])
    count = coords.shape[0]
    nodes = coords.shape[2]
    joint = (weight_x[:, :, :, None] * weight_y[:, :, None, :]).reshape(count, nodes, CX * 8)
    return joint, weight_z


def make_patches(coords, force):
    count = coords.shape[0]
    nodes = coords.shape[2]
    joint, weight_z = node_weights(coords)
    force_z = (jnp.transpose(force, (0, 2, 1))[:, :, :, None] * weight_z[:, :, None, :]).reshape(count, nodes, 24)
    summed = jnp.einsum("knm,knq->kmq", joint, force_z, precision=lax.Precision.HIGHEST)
    summed = jnp.transpose(summed.reshape(count, CX, 8, 3, 8), (0, 3, 1, 2, 4))
    return summed.reshape(count, 3 * CX * 64)


def interpolate(flat, coords):
    count = coords.shape[0]
    joint, weight_z = node_weights(coords)
    values = flat.reshape(count, 3, CX * 8, 8)
    partial_sum = jnp.einsum("knm,kcmj->kncj", joint, values, precision=lax.Precision.HIGHEST)
    result = jnp.sum(partial_sum * weight_z[:, :, None, :], axis=3)
    return jnp.transpose(result, (0, 2, 1))


def grouped(function, arrays):
    count = arrays[0].shape[0]
    group = min(count, 128)
    shaped = tuple(a.reshape((count // group, group) + a.shape[1:]) for a in arrays)
    result = lax.map(lambda pieces: function(*pieces), shaped)
    return result.reshape((count,) + result.shape[2:])


def fluid_step(padded, forcing):
    center = padded[:, 1:-1]
    ahead = padded[:, 2:]
    behind = padded[:, :-2]
    y_plus = jnp.roll(center, -1, 2)
    y_minus = jnp.roll(center, 1, 2)
    z_plus = jnp.roll(center, -1, 3)
    z_minus = jnp.roll(center, 1, 3)
    laplace = ahead + behind + y_plus + y_minus + z_plus + z_minus - 6.0 * center
    advect = center[0:1] * (ahead - behind) * 0.5 + center[1:2] * (y_plus - y_minus) * 0.5 + center[2:3] * (z_plus - z_minus) * 0.5
    return center + time_step * (viscosity * laplace - advect + forcing)


def reference(velocity, node_coords, node_force, block_slab, block_offset):
    count = node_coords.shape[0]
    patches = grouped(make_patches, (node_coords, node_force)).reshape(count, 3, CX, 8, 8)
    taps = jnp.arange(8, dtype=jnp.int32)
    plane_index = block_slab[:, 0:1].astype(jnp.int32) * CX + jnp.arange(CX, dtype=jnp.int32)[None, :]
    row_index = block_offset[:, 0:1].astype(jnp.int32) - 1 + taps[None, :]
    col_index = block_offset[:, 1:2].astype(jnp.int32) - 1 + taps[None, :]
    index_x = plane_index[:, :, None, None]
    index_y = row_index[:, None, :, None]
    index_z = col_index[:, None, None, :]
    force_grid = jnp.zeros_like(velocity).at[:, index_x, index_y, index_z].add(jnp.transpose(patches, (1, 0, 2, 3, 4)))
    field = velocity
    for substep in range(SUBSTEPS):
        padded = jnp.concatenate([field[:, -1:], field, field[:, :1]], axis=1)
        field = fluid_step(padded, force_grid)
    beside_all = jnp.transpose(field[:, index_x, index_y, index_z], (1, 0, 2, 3, 4)).reshape(count, 3 * CX * 64)
    node_velocity = grouped(interpolate, (beside_all, node_coords))
    return field, node_velocity
```

```python
import functools

import jax
import jax.numpy as jnp
from jax import lax
from jax.experimental import pallas as pl
from jax.experimental.pallas import tpu as pltpu
from jax.sharding import PartitionSpec as P

CX = 8
NY = 32
NZ = 128
SUBSTEPS = 3
LANES = 128
WINDOWS = 25
UNROLL = 4

time_step = 0.1
viscosity = 0.2

f32 = jnp.float32
bf16 = jnp.bfloat16

COS_TERMS = (
    0.7071067481276141,
    -0.21808909214261787,
    0.011209883548645258,
    -0.0002299265021950359,
    2.3703615380631122e-06,
)

VMEM_LIMIT = 48 * 1024 * 1024


def vmem():
    return pl.BlockSpec(memory_space=pltpu.VMEM)


def params():
    return pltpu.CompilerParams(vmem_limit_bytes=VMEM_LIMIT)


def phi(distance):
    t = jnp.minimum(distance * distance, 4.0)
    total = COS_TERMS[4] * t + COS_TERMS[3]
    for term in (COS_TERMS[2], COS_TERMS[1], COS_TERMS[0]):
        total = total * t + term
    return total * total


def split_2(values):
    high = values.astype(bf16).astype(f32)
    return high, values - high


def split_3(values):
    high = values.astype(bf16)
    rest = values - high.astype(f32)
    middle = rest.astype(bf16)
    low = (rest - middle.astype(f32)).astype(bf16)
    return high, middle, low


def dot(a, b, dims):
    return lax.dot_general(a, b, (dims, ((), ())), preferred_element_type=f32)


NN = ((1,), (0,))
NT = ((1,), (1,))


def prep_kernel(coords, force, slab, offset, out, back):
    row = lax.broadcasted_iota(jnp.int32, (LANES, LANES), 0)
    col = lax.broadcasted_iota(jnp.int32, (LANES, LANES), 1)
    hot = (jnp.broadcast_to(slab[...], (LANES, LANES)) == row).astype(f32)
    before = (row < col).astype(f32).astype(bf16)
    rank = dot(hot.astype(bf16), before, NN)
    first = jnp.where(rank < 0.5, hot, 0.0)
    second = hot - first
    back[:, :LANES] = first.T.astype(bf16)
    back[:, LANES:] = second.T.astype(bf16)
    both = jnp.concatenate([first, second], axis=0).astype(bf16)
    for quantity in range(6):
        source = coords if quantity < 3 else force
        high, middle, low = split_3(source[quantity % 3])
        placed = dot(both, high, NN) + dot(both, middle, NN) + dot(both, low, NN)
        for slot in range(2):
            start = (slot * 6 + quantity) * LANES
            out[:, 0, start : start + LANES] = placed[slot * LANES : (slot + 1) * LANES]
    offsets = offset[...].astype(f32)
    rows = lax.broadcasted_iota(jnp.int32, (8, LANES), 0)
    spread_y = jnp.broadcast_to(offsets[0:1], (8, LANES))
    spread_z = jnp.broadcast_to(offsets[1:2], (8, LANES))
    tail = jnp.zeros((LANES, LANES), f32)
    empty = jnp.zeros((LANES - 8, LANES), f32)
    for slot, chosen in ((0, first), (1, second)):
        table = jnp.where(rows == 2 * slot, spread_y, 0.0) + jnp.where(
            rows == 2 * slot + 1, spread_z, 0.0
        )
        table = jnp.concatenate([table, empty], axis=0).astype(bf16)
        tail = tail + dot(chosen.astype(bf16), table, NT)
    out[:, 0, 12 * LANES :] = tail


def prep(coords, force, slab, offset):
    return pl.pallas_call(
        prep_kernel,
        out_shape=(
            jax.ShapeDtypeStruct((LANES, 1, 13 * LANES), f32),
            jax.ShapeDtypeStruct((LANES, 2 * LANES), bf16),
        ),
        in_specs=[vmem()] * 4,
        out_specs=(vmem(), vmem()),
        compiler_params=params(),
    )(coords, force, slab, offset)


def node_weights(got, device, slot):
    taps = lax.broadcasted_iota(jnp.int32, (8, LANES), 0).astype(f32) - 1.0
    parts = []
    for dim, reach in ((0, CX - 4.0), (1, 5.0), (2, 5.0)):
        start = (slot * 6 + dim) * LANES
        place = got[device, :, start : start + LANES]
        parts.append(phi(taps - reach * place))
    weight_x, weight_y, weight_z = parts
    joint = jnp.concatenate([weight_y[i : i + 1] * weight_x for i in range(8)], axis=0)
    high, low = split_2(joint)
    stacked = jnp.concatenate([high, low], axis=0).astype(bf16)
    return stacked, weight_z


def window(offsets, device, slot):
    y = offsets[device, 0, 2 * slot].astype(jnp.int32) - 1
    z = offsets[device, 0, 2 * slot + 1].astype(jnp.int32) - 1
    return jnp.clip(y, 0, WINDOWS - 1), jnp.clip(z, 0, WINDOWS - 1)


def spread_kernel(got, grid, total, rows_yx, offsets, sem):
    copy = pltpu.make_async_copy(got.at[:, :, pl.ds(12 * LANES, LANES)], offsets, sem)
    copy.start()
    total[...] = jnp.zeros_like(total)
    copy.wait()

    def step(index, carry):
        pieces = []
        for sub in range(UNROLL):
            device = index * UNROLL + sub
            for slot in range(2):
                stacked, weight_z = node_weights(got, device, slot)
                loads = []
                for c in range(3):
                    start = (slot * 6 + 3 + c) * LANES
                    loads.append(got[device, :, start : start + LANES] * weight_z)
                high, low = split_2(jnp.concatenate(loads, axis=0))
                load = jnp.concatenate([high, low], axis=0).astype(bf16)
                out = dot(load, stacked, NT)
                pieces.append((device, slot, out[:24] + out[24:]))
        for device, slot, out in pieces:
            y, z = window(offsets, device, slot)
            for c in range(3):
                total[y, c, pl.ds(z, 8), :] += out[c * 8 : (c + 1) * 8]
        return carry

    lax.fori_loop(0, LANES // UNROLL, step, 0)
    left = jnp.zeros((96, LANES), f32)
    right = jnp.zeros((96, LANES), f32)
    lane = lax.broadcasted_iota(jnp.int32, (96, LANES), 1)
    for y in range(WINDOWS):
        part = total[y].reshape(96, LANES)
        part = part + pltpu.roll(part, 64, 1)
        part = jnp.where(lane < 64, part, 0.0)
        shift = 8 * y % LANES
        moved = pltpu.roll(part, shift, 1) if shift else part
        if 8 * y >= LANES:
            right = right + moved
        elif 8 * y + 64 <= LANES:
            left = left + moved
        else:
            left = left + jnp.where(lane >= shift, moved, 0.0)
            right = right + jnp.where(lane < shift, moved, 0.0)
    pad = jnp.zeros((32, LANES), f32)
    rows_yx[:LANES] = jnp.concatenate([left, pad], axis=0).T
    rows_yx[LANES:] = jnp.concatenate([right, pad], axis=0).T
    for a in range(CX):
        grid[a] = rows_yx[pl.ds(a, NY, stride=CX), :]


def spread(got):
    return pl.pallas_call(
        spread_kernel,
        out_shape=jax.ShapeDtypeStruct((CX, NY, LANES), f32),
        in_specs=[vmem()],
        out_specs=vmem(),
        scratch_shapes=[
            pltpu.VMEM((WINDOWS, 3, 32, LANES), f32),
            pltpu.VMEM((NY * CX, LANES), f32),
            pltpu.SMEM((LANES, 1, LANES), f32),
            pltpu.SemaphoreType.DMA,
        ],
        compiler_params=params(),
    )(got)


def fluid_kernel(velocity, behind, ahead, grid, grid_behind, grid_ahead, out, step_1, step_2):
    lane = lax.broadcasted_iota(jnp.int32, (NY, NZ), 1)

    def load_0(c, p):
        if p < 0:
            return behind[c, p + 3]
        if p >= CX:
            return ahead[c, p - CX]
        return velocity[c, p]

    def load_1(c, p):
        return step_1[c, p + 2]

    def load_2(c, p):
        return step_2[c, p + 1]

    def store_1(c, p, value):
        step_1[c, p + 2] = value

    def store_2(c, p, value):
        step_2[c, p + 1] = value

    def store_3(c, p, value):
        out[c, p] = value

    def forcing(c, p):
        if p < 0:
            cells = grid_behind[p + 2]
        elif p >= CX:
            cells = grid_ahead[p - CX]
        else:
            cells = grid[p]
        if c:
            cells = pltpu.roll(cells, LANES - 32 * c, 1)
        return jnp.where(lane < 32, cells, 0.0)

    stages = ((load_0, store_1, 2), (load_1, store_2, 1), (load_2, store_3, 0))
    for load, store, width in stages:
        for p in range(-width, CX + width):
            centers = [load(c, p) for c in range(3)]
            for c in range(3):
                center = centers[c]
                x_plus, x_minus = load(c, p + 1), load(c, p - 1)
                y_plus, y_minus = pltpu.roll(center, NY - 1, 0), pltpu.roll(center, 1, 0)
                z_plus, z_minus = pltpu.roll(center, NZ - 1, 1), pltpu.roll(center, 1, 1)
                laplace = x_plus + x_minus + y_plus + y_minus + z_plus + z_minus - 6.0 * center
                advect = 0.5 * (
                    centers[0] * (x_plus - x_minus)
                    + centers[1] * (y_plus - y_minus)
                    + centers[2] * (z_plus - z_minus)
                )
                store(
                    c, p, center + time_step * (viscosity * laplace - advect + forcing(c, p))
                )


def fluid(velocity, behind, ahead, grid, grid_behind, grid_ahead):
    return pl.pallas_call(
        fluid_kernel,
        out_shape=jax.ShapeDtypeStruct((3, CX, NY, NZ), f32),
        in_specs=[vmem()] * 6,
        out_specs=vmem(),
        scratch_shapes=[
            pltpu.VMEM((3, CX + 4, NY, NZ), f32),
            pltpu.VMEM((3, CX + 2, NY, NZ), f32),
        ],
        compiler_params=params(),
    )(velocity, behind, ahead, grid, grid_behind, grid_ahead)


def interpolate_kernel(field, got, out, rows_yx, table_high, table_low, offsets, sem):
    copy = pltpu.make_async_copy(got.at[:, :, pl.ds(12 * LANES, LANES)], offsets, sem)
    copy.start()
    lane = lax.broadcasted_iota(jnp.int32, (NY, LANES), 1)
    for a in range(CX):
        cells = jnp.where(lane < 32, field[0, a], 0.0)
        for c in (1, 2):
            moved = pltpu.roll(field[c, a], 32 * c, 1)
            cells = jnp.where((lane >= 32 * c) & (lane < 32 * c + 32), moved, cells)
        rows_yx[pl.ds(a, NY, stride=CX), :] = cells
    left = rows_yx[:LANES].T[:96]
    right = rows_yx[LANES:].T[:96]
    wide = lax.broadcasted_iota(jnp.int32, (96, LANES), 1)

    def rolled(values, shift):
        shift = shift % LANES
        return pltpu.roll(values, shift, 1) if shift else values

    for y in range(WINDOWS):
        shift = 8 * y
        if shift + 64 <= LANES:
            once, again = rolled(left, -shift), rolled(left, 64 - shift)
        elif shift >= LANES:
            once, again = rolled(right, LANES - shift), rolled(right, LANES + 64 - shift)
        else:
            edge = LANES - shift
            once = jnp.where(wide < edge, rolled(left, -shift), rolled(right, -shift))
            again = jnp.where(
                wide < 64 + edge, rolled(left, 64 - shift), rolled(right, 64 - shift)
            )
        high, low = split_2(jnp.where(wide < 64, once, again))
        table_high[y] = high.reshape(3, 32, LANES)
        table_low[y] = low.reshape(3, 32, LANES)
    copy.wait()

    def step(index, carry):
        for sub in range(UNROLL):
            device = index * UNROLL + sub
            for slot in range(2):
                stacked, weight_z = node_weights(got, device, slot)
                y, z = window(offsets, device, slot)
                cells = [table_high[y, c, pl.ds(z, 8), :] for c in range(3)]
                cells += [table_low[y, c, pl.ds(z, 8), :] for c in range(3)]
                values = dot(jnp.concatenate(cells, axis=0).astype(bf16), stacked, NN)
                values = values[:24] + values[24:]
                for c in range(3):
                    start = (slot * 3 + c) * LANES
                    out[device, :, start : start + LANES] = jnp.sum(
                        values[c * 8 : (c + 1) * 8] * weight_z, axis=0, keepdims=True
                    )
        return carry

    lax.fori_loop(0, LANES // UNROLL, step, 0)


def interpolate(field, got):
    return pl.pallas_call(
        interpolate_kernel,
        out_shape=jax.ShapeDtypeStruct((LANES, 1, 6 * LANES), f32),
        in_specs=[vmem()] * 2,
        out_specs=vmem(),
        scratch_shapes=[
            pltpu.VMEM((NY * CX, LANES), f32),
            pltpu.VMEM((WINDOWS, 3, 32, LANES), f32),
            pltpu.VMEM((WINDOWS, 3, 32, LANES), f32),
            pltpu.SMEM((LANES, 1, LANES), f32),
            pltpu.SemaphoreType.DMA,
        ],
        compiler_params=params(),
    )(field, got)


def pick_kernel(returned, back, out):
    chosen = back[...]
    for c in range(3):
        start = c * LANES
        both = jnp.concatenate(
            [
                returned[:, 0, start : start + LANES],
                returned[:, 0, 3 * LANES + start : 4 * LANES + start],
            ],
            axis=0,
        )
        high, middle, low = split_3(both)
        out[c] = dot(chosen, high, NN) + dot(chosen, middle, NN) + dot(chosen, low, NN)


def pick(returned, back):
    return pl.pallas_call(
        pick_kernel,
        out_shape=jax.ShapeDtypeStruct((3, LANES, LANES), f32),
        in_specs=[vmem()] * 2,
        out_specs=vmem(),
        compiler_params=params(),
    )(returned, back)


def exchange(values):
    return lax.all_to_all(values, "slab", split_axis=0, concat_axis=0, tiled=True)


def from_behind(values):
    count = lax.axis_size("slab")
    return lax.ppermute(values, "slab", [(i, (i + 1) % count) for i in range(count)])


def from_ahead(values):
    count = lax.axis_size("slab")
    return lax.ppermute(values, "slab", [((i + 1) % count, i) for i in range(count)])


def body(velocity, node_coords, node_force, block_slab, block_offset):
    sent, back = prep(
        jnp.transpose(node_coords, (1, 0, 2)),
        jnp.transpose(node_force, (1, 0, 2)),
        jnp.transpose(block_slab, (1, 0)),
        jnp.transpose(block_offset, (1, 0)),
    )
    got = exchange(sent)
    behind = from_behind(velocity[:, CX - 3 :])
    ahead = from_ahead(velocity[:, :3])
    grid = spread(got)
    grid_behind = from_behind(grid[CX - 2 :])
    grid_ahead = from_ahead(grid[:2])
    field = fluid(velocity, behind, ahead, grid, grid_behind, grid_ahead)
    returned = exchange(interpolate(field, got))
    node_velocity = pick(returned, back)
    return field, jnp.transpose(node_velocity, (1, 0, 2))


def solution(mesh):
    return jax.shard_map(
        body,
        mesh=mesh,
        in_specs=(
            P(None, "slab", None, None),
            P("slab", None, None),
            P("slab", None, None),
            P("slab", None),
            P("slab", None),
        ),
        out_specs=(P(None, "slab", None, None), P("slab", None, None)),
        check_vma=False,
    )
```

```python
import jax
import jax.numpy as jnp
from jax import lax
from jax.experimental import pallas as pl
from jax.experimental.pallas import tpu as pltpu
from jax.sharding import PartitionSpec as P

CX = 8
NY = 32
NZ = 128
SUBSTEPS = 3
LANES = 128
WINDOWS = 25
SPREAD_UNROLL = 16
INNER_UNROLL = 8
EDGE_UNROLL = 16

time_step = 0.1
viscosity = 0.2

f32 = jnp.float32
bf16 = jnp.bfloat16

COS_TERMS = (
    0.7071067481276141,
    -0.21808909214261787,
    0.011209883548645258,
    -0.0002299265021950359,
    2.3703615380631122e-06,
)

VMEM_LIMIT = 24 * 1024 * 1024
VMEM_ALL = 60 * 1024 * 1024


def vmem():
    return pl.BlockSpec(memory_space=pltpu.VMEM)


def anywhere():
    return pl.BlockSpec(memory_space=pl.ANY)


def params(limit=VMEM_LIMIT):
    return pltpu.CompilerParams(vmem_limit_bytes=limit)


def phi(distance):
    t = jnp.minimum(distance * distance, 4.0)
    total = COS_TERMS[4] * t + COS_TERMS[3]
    for term in (COS_TERMS[2], COS_TERMS[1], COS_TERMS[0]):
        total = total * t + term
    return total * total


def split_2(values):
    high = values.astype(bf16).astype(f32)
    return high, values - high


def split_3(values):
    high = values.astype(bf16)
    rest = values - high.astype(f32)
    middle = rest.astype(bf16)
    low = (rest - middle.astype(f32)).astype(bf16)
    return high, middle, low


def dot(a, b, dims):
    return lax.dot_general(a, b, (dims, ((), ())), preferred_element_type=f32)


NN = ((1,), (0,))
NT = ((1,), (1,))


TABLE = WINDOWS * 96
EDGES = (0, 1, 6, 7)
MIDDLE = (2, 3, 4, 5)


def picks_kernel(out):
    source = lax.broadcasted_iota(jnp.int32, (2 * LANES, LANES), 0)
    lane = lax.broadcasted_iota(jnp.int32, (2 * LANES, LANES), 1)
    wanted = (lane >> 6) * 128 + ((lane >> 3) & 3) * 32 + (lane & 7)
    apart = source - wanted
    for start in range(WINDOWS):
        chosen = jnp.where(apart == start, 1.0, 0.0)
        out[:, start * LANES : (start + 1) * LANES] = chosen.astype(bf16)


def window_picks():
    return pl.pallas_call(
        picks_kernel,
        out_shape=jax.ShapeDtypeStruct((2 * LANES, WINDOWS * LANES), bf16),
        out_specs=vmem(),
        compiler_params=params(),
        cost_estimate=pl.CostEstimate(
            flops=2_000_000_000, bytes_accessed=2_000_000, transcendentals=0
        ),
    )()


def prep_kernel(coords_in, force_in, slab_in, offset_in, out, back, coords, force, slab, offset, sems):
    copies = [
        pltpu.make_async_copy(source, target, sems.at[i])
        for i, (source, target) in enumerate(
            ((slab_in, slab), (offset_in, offset), (coords_in, coords), (force_in, force))
        )
    ]
    for copy in copies:
        copy.start()
    row = lax.broadcasted_iota(jnp.int32, (LANES, LANES), 0)
    col = lax.broadcasted_iota(jnp.int32, (LANES, LANES), 1)
    before = (row < col).astype(f32).astype(bf16)
    copies[0].wait()
    hot = (jnp.broadcast_to(slab[...], (LANES, LANES)) == row).astype(f32)
    rank = dot(hot.astype(bf16), before, NN)
    first = jnp.where(rank < 0.5, hot, 0.0)
    second = hot - first
    both = jnp.concatenate([first, second], axis=0).astype(bf16)
    copies[1].wait()
    offsets = offset[...].astype(f32)
    rows = lax.broadcasted_iota(jnp.int32, (8, LANES), 0)
    spread_y = jnp.broadcast_to(offsets[0:1], (8, LANES))
    spread_z = jnp.broadcast_to(offsets[1:2], (8, LANES))
    tail = jnp.zeros((LANES, LANES), f32)
    empty = jnp.zeros((LANES - 8, LANES), f32)
    for slot, chosen in ((0, first), (1, second)):
        table = jnp.where(rows == 2 * slot, spread_y, 0.0) + jnp.where(
            rows == 2 * slot + 1, spread_z, 0.0
        )
        table = jnp.concatenate([table, empty], axis=0).astype(bf16)
        tail = tail + dot(chosen.astype(bf16), table, NT)
    out[:, 0, 12 * LANES :] = tail
    for quantity in range(6):
        source = coords if quantity < 3 else force
        if quantity % 3 == 0:
            copies[2 + quantity // 3].wait()
        high, middle, low = split_3(source[quantity % 3])
        placed = dot(both, high, NN) + dot(both, middle, NN) + dot(both, low, NN)
        for slot in range(2):
            start = (slot * 6 + quantity) * LANES
            out[:, 0, start : start + LANES] = placed[slot * LANES : (slot + 1) * LANES]
    back[:, :LANES] = first.T.astype(bf16)
    back[:, LANES:] = second.T.astype(bf16)


def prep(coords, force, slab, offset):
    return pl.pallas_call(
        prep_kernel,
        out_shape=(
            jax.ShapeDtypeStruct((LANES, 1, 13 * LANES), f32),
            jax.ShapeDtypeStruct((LANES, 2 * LANES), bf16),
        ),
        in_specs=[anywhere()] * 4,
        out_specs=(vmem(), vmem()),
        scratch_shapes=[
            pltpu.VMEM((3, LANES, LANES), f32),
            pltpu.VMEM((3, LANES, LANES), f32),
            pltpu.VMEM((1, LANES), jnp.int32),
            pltpu.VMEM((2, LANES), jnp.int32),
            pltpu.SemaphoreType.DMA((4,)),
        ],
        compiler_params=params(VMEM_ALL),
    )(coords, force, slab, offset)


def axis_weights(got, device, slot):
    taps = lax.broadcasted_iota(jnp.int32, (8, LANES), 0).astype(f32) - 1.0
    parts = []
    for dim, reach in ((0, CX - 4.0), (1, 5.0), (2, 5.0)):
        start = (slot * 6 + dim) * LANES
        place = got[device, :, start : start + LANES]
        parts.append(phi(taps - reach * place))
    return parts


def stack_2(values):
    high, low = split_2(values)
    return jnp.concatenate([high, low], axis=0).astype(bf16)


def spread_kernel(got, grid, near, far, rows_out, total, rows_yx, rows, sem):
    tail = got[:, 0, 12 * LANES :].T
    y = jnp.concatenate([tail[0:1], tail[2:3]], axis=0)
    z = jnp.concatenate([tail[1:2], tail[3:4]], axis=0)
    y = jnp.clip(y - 1.0, 0.0, WINDOWS - 1.0)
    z = jnp.clip(z - 1.0, 0.0, WINDOWS - 1.0)
    start = (y * 96.0 + z).astype(jnp.int32)
    rows_out[...] = jnp.concatenate([start, jnp.zeros((6, LANES), jnp.int32)], axis=0)
    copy = pltpu.make_async_copy(rows_out, rows, sem)
    copy.start()
    total[...] = jnp.zeros_like(total)
    copy.wait()

    def step(index, carry):
        pieces = []
        for sub in range(SPREAD_UNROLL):
            device = index * SPREAD_UNROLL + sub
            loads, stacks = [], []
            for slot in range(2):
                weight_x, weight_y, weight_z = axis_weights(got, device, slot)
                stacks.append(
                    stack_2(
                        jnp.concatenate([weight_y[i : i + 1] * weight_x for i in range(8)], axis=0)
                    )
                )
                parts = []
                for c in range(3):
                    start = (slot * 6 + 3 + c) * LANES
                    parts.append(got[device, :, start : start + LANES] * weight_z)
                loads.append(stack_2(jnp.concatenate(parts, axis=0)))
            out = dot(jnp.concatenate(loads, axis=0), jnp.concatenate(stacks, axis=0), NT)
            pieces.append((device, 0, out[:24, :LANES] + out[24:48, :LANES]))
            pieces.append((device, 1, out[48:72, LANES:] + out[72:, LANES:]))
        for device, slot, out in pieces:
            row = rows[slot, device]
            for c in range(3):
                total[pl.ds(row + 32 * c, 8), :] += out[c * 8 : (c + 1) * 8]
        return carry

    lax.fori_loop(0, LANES // SPREAD_UNROLL, step, 0)
    left = jnp.zeros((96, LANES), f32)
    right = jnp.zeros((96, LANES), f32)
    lane = lax.broadcasted_iota(jnp.int32, (96, LANES), 1)
    for y in range(WINDOWS):
        part = total[y * 96 : (y + 1) * 96]
        part = part + pltpu.roll(part, 64, 1)
        part = jnp.where(lane < 64, part, 0.0)
        shift = 8 * y % LANES
        moved = pltpu.roll(part, shift, 1) if shift else part
        if 8 * y >= LANES:
            right = right + moved
        elif 8 * y + 64 <= LANES:
            left = left + moved
        else:
            left = left + jnp.where(lane >= shift, moved, 0.0)
            right = right + jnp.where(lane < shift, moved, 0.0)
    pad = jnp.zeros((32, LANES), f32)
    rows_yx[:LANES] = jnp.concatenate([left, pad], axis=0).T
    rows_yx[LANES:] = jnp.concatenate([right, pad], axis=0).T
    planes = [rows_yx[pl.ds(a, NY, stride=CX), :] for a in range(CX)]
    odd = lax.axis_index("slab") % 2 == 1
    for a in range(CX):
        grid[a] = planes[a]
    for a in range(2):
        near[a] = jnp.where(odd, planes[a], planes[CX - 2 + a])
        far[a] = jnp.where(odd, planes[CX - 2 + a], planes[a])


def spread(got):
    return pl.pallas_call(
        spread_kernel,
        out_shape=(
            jax.ShapeDtypeStruct((CX, NY, LANES), f32),
            jax.ShapeDtypeStruct((2, NY, LANES), f32),
            jax.ShapeDtypeStruct((2, NY, LANES), f32),
            jax.ShapeDtypeStruct((8, LANES), jnp.int32),
        ),
        in_specs=[vmem()],
        out_specs=(vmem(),) * 4,
        scratch_shapes=[
            pltpu.VMEM((TABLE, LANES), f32),
            pltpu.VMEM((NY * CX, LANES), f32),
            pltpu.SMEM((8, LANES), jnp.int32),
            pltpu.SemaphoreType.DMA,
        ],
        compiler_params=params(),
    )(got)


def forcing_of(cells, c):
    lane = lax.broadcasted_iota(jnp.int32, (NY, NZ), 1)
    if c:
        cells = pltpu.roll(cells, LANES - 32 * c, 1)
    return jnp.where(lane < 32, cells, 0.0)


def fluid_plane(load, cells, p):
    centers = [load(c, p) for c in range(3)]
    results = []
    for c in range(3):
        center = centers[c]
        x_plus, x_minus = load(c, p + 1), load(c, p - 1)
        y_plus, y_minus = pltpu.roll(center, NY - 1, 0), pltpu.roll(center, 1, 0)
        z_plus, z_minus = pltpu.roll(center, NZ - 1, 1), pltpu.roll(center, 1, 1)
        laplace = x_plus + x_minus + y_plus + y_minus + z_plus + z_minus - 6.0 * center
        advect = 0.5 * (
            centers[0] * (x_plus - x_minus)
            + centers[1] * (y_plus - y_minus)
            + centers[2] * (z_plus - z_minus)
        )
        results.append(
            center + time_step * (viscosity * laplace - advect + forcing_of(cells, c))
        )
    return results


def packed_plane(parts):
    lane = lax.broadcasted_iota(jnp.int32, (NY, LANES), 1)
    cells = jnp.where(lane < 32, parts[0], 0.0)
    for c in (1, 2):
        moved = pltpu.roll(parts[c], 32 * c, 1)
        cells = jnp.where((lane >= 32 * c) & (lane < 32 * c + 32), moved, cells)
    return cells


def fill_table(table, planes, picks):
    cells = jnp.concatenate([packed_plane(parts) for parts in planes], axis=0).T[:96]
    high, low = split_2(cells)
    split = jnp.concatenate([high, low], axis=1).astype(bf16)
    for y in range(0, WINDOWS, 2):
        wide = min(2, WINDOWS - y)
        both = dot(split, picks[:, y * LANES : (y + wide) * LANES], NN)
        for i in range(wide):
            table[(y + i) * 96 : (y + i + 1) * 96] = both[:, i * LANES : (i + 1) * LANES]


def window_sums(table, rows, device, weights, weights_z):
    cells = []
    for slot in range(2):
        row = rows[slot, device]
        for c in range(3):
            cells.append(table[pl.ds(row + 32 * c, 8), :])
    values = dot(jnp.concatenate(cells, axis=0).astype(bf16), weights, NN)
    sums = []
    for slot in range(2):
        for c in range(3):
            start = slot * 24 + c * 8
            part = values[start : start + 8, slot * LANES : (slot + 1) * LANES]
            sums.append(jnp.sum(part * weights_z[slot], axis=0, keepdims=True))
    return sums


def halo_reader(inside, same, cross, depth):
    odd = lax.axis_index("slab") % 2 == 1

    def load(c, p):
        if p < 0:
            return jnp.where(odd, same[c, p + depth], cross[c, p + depth])
        if p >= CX:
            return jnp.where(odd, cross[c, p - CX], same[c, p - CX])
        return inside[c, p]

    return load


def inner_kernel(
    velocity, same, cross, grid, got, rows_in, picks,
    step_1, step_2, middle, edge_weights, z_weights, partial, table, rows, sem
):
    copy = pltpu.make_async_copy(rows_in, rows, sem)
    copy.start()
    load_0 = halo_reader(velocity, same, cross, SUBSTEPS)
    for p in range(CX):
        for c, value in enumerate(fluid_plane(load_0, grid[p], p)):
            step_1[c, p] = value
    for p in range(1, CX - 1):
        for c, value in enumerate(fluid_plane(lambda c, p: step_1[c, p], grid[p], p)):
            step_2[c, p] = value
    planes = []
    for p in MIDDLE:
        planes.append(fluid_plane(lambda c, p: step_2[c, p], grid[p], p))
        for c in range(3):
            middle[c, p - MIDDLE[0]] = planes[-1][c]
    fill_table(table, planes, picks)
    copy.wait()

    def step(index, carry):
        for sub in range(INNER_UNROLL):
            device = index * INNER_UNROLL + sub
            weights, weights_z = [], []
            for slot in range(2):
                weight_x, weight_y, weight_z = axis_weights(got, device, slot)
                weights.append(
                    stack_2(
                        jnp.concatenate([weight_x[a : a + 1] * weight_y for a in MIDDLE], axis=0)
                    )
                )
                edge_weights[device, :, slot * LANES : (slot + 1) * LANES] = stack_2(
                    jnp.concatenate([weight_x[a : a + 1] * weight_y for a in EDGES], axis=0)
                )
                z_weights[device, :, slot * LANES : (slot + 1) * LANES] = weight_z
                weights_z.append(weight_z)
            both = jnp.concatenate(weights, axis=1)
            sums = window_sums(
                table, rows, device, jnp.concatenate([both, both], axis=0), weights_z
            )
            for i in range(6):
                partial[device, :, i * LANES : (i + 1) * LANES] = sums[i]
        return carry

    lax.fori_loop(0, LANES // INNER_UNROLL, step, 0)


def inner(velocity, same, cross, grid, got, rows, picks):
    return pl.pallas_call(
        inner_kernel,
        out_shape=(
            jax.ShapeDtypeStruct((3, CX, NY, NZ), f32),
            jax.ShapeDtypeStruct((3, CX, NY, NZ), f32),
            jax.ShapeDtypeStruct((3, len(MIDDLE), NY, NZ), f32),
            jax.ShapeDtypeStruct((LANES, 64, 2 * LANES), bf16),
            jax.ShapeDtypeStruct((LANES, 8, 2 * LANES), f32),
            jax.ShapeDtypeStruct((LANES, 1, 6 * LANES), f32),
        ),
        in_specs=[vmem()] * 7,
        out_specs=(vmem(),) * 6,
        scratch_shapes=[
            pltpu.VMEM((TABLE, LANES), f32),
            pltpu.SMEM((8, LANES), jnp.int32),
            pltpu.SemaphoreType.DMA,
        ],
        compiler_params=params(),
        cost_estimate=pl.CostEstimate(
            flops=6_000_000_000, bytes_accessed=8_000_000, transcendentals=0
        ),
    )(velocity, same, cross, grid, got, rows, picks)


def edge_kernel(
    velocity, same, cross, grid, near, far, rows_in, picks,
    step_1, step_2, middle, edge_weights, z_weights, partial,
    field, out, ends_1, ends_2, ends_3, table, rows, sems
):
    copies = [pltpu.make_async_copy(rows_in, rows, sems.at[0])]
    copies.append(
        pltpu.make_async_copy(middle, field.at[:, pl.ds(MIDDLE[0], len(MIDDLE))], sems.at[1])
    )
    for i, p in enumerate((0, CX - 2)):
        copies.append(
            pltpu.make_async_copy(ends_3.at[:, pl.ds(2 * i, 2)], field.at[:, pl.ds(p, 2)], sems.at[2 + i])
        )
    copies[0].start()
    copies[1].start()
    odd = lax.axis_index("slab") % 2 == 1

    def cells(p):
        if p < 0:
            return jnp.where(odd, near[p + 2], far[p + 2])
        if p >= CX:
            return jnp.where(odd, far[p - CX], near[p - CX])
        return grid[p]

    def reader(ends, inside, low):
        def load(c, p):
            for i, q in enumerate(low):
                if p == q:
                    return ends[c, i]
            return inside[c, p]

        return load

    planes_1 = (-2, -1, CX, CX + 1)
    planes_2 = (-1, 0, CX - 1, CX)
    load_0 = halo_reader(velocity, same, cross, SUBSTEPS)
    for i, p in enumerate(planes_1):
        for c, value in enumerate(fluid_plane(load_0, cells(p), p)):
            ends_1[c, i] = value
    load_1 = reader(ends_1, step_1, planes_1)
    for i, p in enumerate(planes_2):
        for c, value in enumerate(fluid_plane(load_1, cells(p), p)):
            ends_2[c, i] = value
    load_2 = reader(ends_2, step_2, planes_2)
    planes = []
    for i, p in enumerate(EDGES):
        planes.append(fluid_plane(load_2, cells(p), p))
        for c in range(3):
            ends_3[c, i] = planes[-1][c]
    copies[2].start()
    copies[3].start()
    fill_table(table, planes, picks)
    copies[0].wait()

    def step(index, carry):
        for sub in range(EDGE_UNROLL):
            device = index * EDGE_UNROLL + sub
            both = edge_weights[device]
            weights_z = [
                z_weights[device, :, slot * LANES : (slot + 1) * LANES] for slot in range(2)
            ]
            sums = window_sums(
                table, rows, device, jnp.concatenate([both, both], axis=0), weights_z
            )
            for i in range(6):
                lanes = slice(i * LANES, (i + 1) * LANES)
                out[device, :, lanes] = partial[device, :, lanes] + sums[i]
        return carry

    lax.fori_loop(0, LANES // EDGE_UNROLL, step, 0)
    for copy in copies[1:]:
        copy.wait()


def edge(*arguments):
    return pl.pallas_call(
        edge_kernel,
        out_shape=(
            jax.ShapeDtypeStruct((3, CX, NY, NZ), f32),
            jax.ShapeDtypeStruct((LANES, 1, 6 * LANES), f32),
        ),
        in_specs=[vmem()] * 14,
        out_specs=(anywhere(), vmem()),
        scratch_shapes=[
            pltpu.VMEM((3, 4, NY, NZ), f32),
            pltpu.VMEM((3, 4, NY, NZ), f32),
            pltpu.VMEM((3, 4, NY, NZ), f32),
            pltpu.VMEM((TABLE, LANES), f32),
            pltpu.SMEM((8, LANES), jnp.int32),
            pltpu.SemaphoreType.DMA((4,)),
        ],
        compiler_params=params(),
    )(*arguments)


def pick_kernel(returned, back, out):
    chosen = back[...]
    for c in range(3):
        start = c * LANES
        both = jnp.concatenate(
            [
                returned[:, 0, start : start + LANES],
                returned[:, 0, 3 * LANES + start : 4 * LANES + start],
            ],
            axis=0,
        )
        high, middle, low = split_3(both)
        out[c] = dot(chosen, high, NN) + dot(chosen, middle, NN) + dot(chosen, low, NN)


def pick(returned, back):
    return pl.pallas_call(
        pick_kernel,
        out_shape=jax.ShapeDtypeStruct((3, LANES, LANES), f32),
        in_specs=[vmem()] * 2,
        out_specs=vmem(),
        compiler_params=params(),
    )(returned, back)


def exchange(values):
    return lax.all_to_all(values, "slab", split_axis=0, concat_axis=0, tiled=True)


def swap(values, first):
    count = lax.axis_size("slab")
    pairs = []
    for i in range(first, count + first, 2):
        a, b = i % count, (i + 1) % count
        pairs += [(a, b), (b, a)]
    return lax.ppermute(values, "slab", pairs)


def body(velocity, node_coords, node_force, block_slab, block_offset):
    picks = window_picks()
    sent, back = prep(
        jnp.transpose(node_coords, (1, 0, 2)),
        jnp.transpose(node_force, (1, 0, 2)),
        jnp.transpose(block_slab, (1, 0)),
        jnp.transpose(block_offset, (1, 0)),
    )
    got = exchange(sent)
    odd = lax.axis_index("slab") % 2 == 1
    first, last = velocity[:, :SUBSTEPS], velocity[:, CX - SUBSTEPS :]
    cross = swap(jnp.where(odd, last, first), 1)
    same = swap(jnp.where(odd, first, last), 0)
    grid, near, far, rows = spread(got)
    far = swap(far, 1)
    near = swap(near, 0)
    inside = inner(velocity, same, cross, grid, got, rows, picks)
    field, sums = edge(velocity, same, cross, grid, near, far, rows, picks, *inside)
    node_velocity = pick(exchange(sums), back)
    return field, jnp.transpose(node_velocity, (1, 0, 2))


def solution(mesh):
    return jax.shard_map(
        body,
        mesh=mesh,
        in_specs=(
            P(None, "slab", None, None),
            P("slab", None, None),
            P("slab", None, None),
            P("slab", None),
            P("slab", None),
        ),
        out_specs=(P(None, "slab", None, None), P("slab", None, None)),
        check_vma=False,
    )
```

```python
import jax
import jax.numpy as jnp
from jax import lax
from jax.experimental import pallas as pl
from jax.experimental.pallas import tpu as pltpu
from jax.sharding import PartitionSpec as P

CX = 8
NY = 32
NZ = 128
SUBSTEPS = 3
LANES = 128
WINDOWS = 25
SPREAD_UNROLL = 32
MIDDLE_UNROLL = 32
INNER_UNROLL = 32
EDGE_UNROLL = 32

time_step = 0.1
viscosity = 0.2

f32 = jnp.float32
bf16 = jnp.bfloat16

COS_TERMS = (
    0.7071067481276141,
    -0.21808909214261787,
    0.011209883548645258,
    -0.0002299265021950359,
    2.3703615380631122e-06,
)

VMEM_LIMIT = 24 * 1024 * 1024
VMEM_ALL = 60 * 1024 * 1024


def vmem():
    return pl.BlockSpec(memory_space=pltpu.VMEM)


def anywhere():
    return pl.BlockSpec(memory_space=pl.ANY)


def params(limit=VMEM_LIMIT):
    return pltpu.CompilerParams(vmem_limit_bytes=limit)


def phi(distance):
    t = jnp.minimum(distance * distance, 4.0)
    total = COS_TERMS[4] * t + COS_TERMS[3]
    for term in (COS_TERMS[2], COS_TERMS[1], COS_TERMS[0]):
        total = total * t + term
    return total * total


def split_2(values):
    high = values.astype(bf16).astype(f32)
    return high, values - high


def split_3(values):
    high = values.astype(bf16)
    rest = values - high.astype(f32)
    middle = rest.astype(bf16)
    low = (rest - middle.astype(f32)).astype(bf16)
    return high, middle, low


def dot(a, b, dims):
    return lax.dot_general(a, b, (dims, ((), ())), preferred_element_type=f32)


NN = ((1,), (0,))
NT = ((1,), (1,))


TABLE = WINDOWS * 96
EDGES = (0, 1, 6, 7)
MIDDLE = (2, 3, 4, 5)
SENT = 13
REACH = (CX - 4.0, 5.0, 5.0)


def picks_kernel(out):
    source = lax.broadcasted_iota(jnp.int32, (LANES, LANES), 0)
    lane = lax.broadcasted_iota(jnp.int32, (LANES, LANES), 1)
    apart = source - ((lane >> 3) & 3) * 32 - (lane & 7)
    for start in range(WINDOWS):
        chosen = jnp.where(apart == start, 1.0, 0.0)
        out[:, start * LANES : (start + 1) * LANES] = chosen.astype(bf16)


def window_picks():
    return pl.pallas_call(
        picks_kernel,
        out_shape=jax.ShapeDtypeStruct((LANES, WINDOWS * LANES), bf16),
        out_specs=vmem(),
        compiler_params=params(),
        cost_estimate=pl.CostEstimate(
            flops=2_000_000_000, bytes_accessed=2_000_000, transcendentals=0
        ),
    )()


def prep_kernel(coords_in, force_in, slab_in, offset_in, out, back, coords, force, slab, offset, sems):
    copies = [
        pltpu.make_async_copy(source, target, sems.at[i])
        for i, (source, target) in enumerate(
            ((slab_in, slab), (offset_in, offset), (coords_in, coords), (force_in, force))
        )
    ]
    for copy in copies:
        copy.start()
    row = lax.broadcasted_iota(jnp.int32, (LANES, LANES), 0)
    col = lax.broadcasted_iota(jnp.int32, (LANES, LANES), 1)
    before = (row < col).astype(f32).astype(bf16)
    copies[0].wait()
    hot = (jnp.broadcast_to(slab[...], (LANES, LANES)) == row).astype(f32)
    rank = dot(hot.astype(bf16), before, NN)
    first = jnp.where(rank < 0.5, hot, 0.0)
    second = hot - first
    both = jnp.concatenate([first, second], axis=0).astype(bf16)
    copies[1].wait()
    offsets = offset[...].astype(f32)
    rows = lax.broadcasted_iota(jnp.int32, (8, LANES), 0)
    spread_y = jnp.broadcast_to(offsets[0:1], (8, LANES))
    spread_z = jnp.broadcast_to(offsets[1:2], (8, LANES))
    tail = jnp.zeros((LANES, LANES), f32)
    empty = jnp.zeros((LANES - 8, LANES), f32)
    for slot, chosen in ((0, first), (1, second)):
        table = jnp.where(rows == 2 * slot, spread_y, 0.0) + jnp.where(
            rows == 2 * slot + 1, spread_z, 0.0
        )
        table = jnp.concatenate([table, empty], axis=0).astype(bf16)
        tail = tail + dot(chosen.astype(bf16), table, NT)
    out[pl.ds(12, LANES, stride=SENT), :] = tail
    for quantity in range(6):
        if quantity % 3 == 0:
            copies[2 + quantity // 3].wait()
        if quantity < 3:
            source = coords[quantity] * REACH[quantity]
        else:
            source = force[quantity - 3]
        high, middle, low = split_3(source)
        placed = dot(both, high, NN) + dot(both, middle, NN) + dot(both, low, NN)
        for slot in range(2):
            out[pl.ds(slot * 6 + quantity, LANES, stride=SENT), :] = placed[
                slot * LANES : (slot + 1) * LANES
            ]
    back[:, :LANES] = first.T.astype(bf16)
    back[:, LANES:] = second.T.astype(bf16)


def prep(coords, force, slab, offset):
    return pl.pallas_call(
        prep_kernel,
        out_shape=(
            jax.ShapeDtypeStruct((SENT * LANES, LANES), f32),
            jax.ShapeDtypeStruct((LANES, 2 * LANES), bf16),
        ),
        in_specs=[anywhere()] * 4,
        out_specs=(vmem(), vmem()),
        scratch_shapes=[
            pltpu.VMEM((3, LANES, LANES), f32),
            pltpu.VMEM((3, LANES, LANES), f32),
            pltpu.VMEM((1, LANES), jnp.int32),
            pltpu.VMEM((2, LANES), jnp.int32),
            pltpu.SemaphoreType.DMA((4,)),
        ],
        compiler_params=params(VMEM_ALL),
    )(coords, force, slab, offset)


def stack_2(values):
    high, low = split_2(values)
    return jnp.concatenate([high, low], axis=0).astype(bf16)


def plane_stack(weight_x, weight_y, planes):
    return stack_2(jnp.concatenate([weight_x[a : a + 1] * weight_y for a in planes], axis=0))


def own_halves(out):
    row = lax.broadcasted_iota(jnp.int32, (48, LANES), 0)
    lane = lax.broadcasted_iota(jnp.int32, (48, LANES), 1)
    return jnp.where((row < 24) == (lane < 64), out, 0.0)


def spread_pair(load, stack):
    turned = stack.T
    return own_halves(dot(load, jnp.concatenate([turned, turned], axis=0), NN))


def gather_windows(total, rows, parts, index, unroll):
    for sub in range(unroll):
        for slot in range(2):
            row = rows[slot, index * unroll + sub]
            for c in range(3):
                start = slot * 24 + c * 8
                total[pl.ds(row + 32 * c, 8), :] += parts[sub, start : start + 8]


def spread_planes(total, picks):
    cells = jnp.zeros((96, LANES), f32)
    for y in range(0, WINDOWS, 2):
        wide = min(2, WINDOWS - y)
        both = [total[(y + i) * 96 : (y + i + 1) * 96] for i in range(wide)]
        both = both[0] if wide == 1 else jnp.concatenate(both, axis=1)
        chosen = picks[:, y * LANES : (y + wide) * LANES]
        high, low = split_2(both)
        cells = cells + dot(high.astype(bf16), chosen, NT) + dot(low.astype(bf16), chosen, NT)
    cells = jnp.concatenate([cells * time_step, jnp.zeros((32, LANES), f32)], axis=0).T
    return [cells[i * NY : (i + 1) * NY] for i in range(4)]


def spread_kernel(
    got, picks, grid, near, far, rows_out, weights, loads, stacks, total, parts, rows, sem
):
    tail = got[pl.ds(12, LANES, stride=SENT), :].T
    y = jnp.concatenate([tail[0:1], tail[2:3]], axis=0)
    z = jnp.concatenate([tail[1:2], tail[3:4]], axis=0)
    y = jnp.clip(y - 1.0, 0.0, WINDOWS - 1.0)
    z = jnp.clip(z - 1.0, 0.0, WINDOWS - 1.0)
    start = (y * 96.0 + z).astype(jnp.int32)
    rows_out[...] = jnp.concatenate([start, jnp.zeros((6, LANES), jnp.int32)], axis=0)
    copy = pltpu.make_async_copy(rows_out, rows, sem)
    copy.start()
    total[...] = jnp.zeros_like(total)
    taps = lax.broadcasted_iota(jnp.int32, (8, LANES), 0).astype(f32) - 1.0

    def compute(index):
        for sub in range(SPREAD_UNROLL):
            device = index * SPREAD_UNROLL + sub
            load, stack = [], []
            for slot in range(2):
                source = device * SENT + slot * 6
                weight_x, weight_y, weight_z = [
                    phi(taps - got[pl.ds(source + dim, 1), :]) for dim in range(3)
                ]
                weights[device, slot, 0:8] = weight_x
                weights[device, slot, 8:16] = weight_y
                weights[device, slot, 16:24] = weight_z
                stack.append(plane_stack(weight_x, weight_y, EDGES))
                load += [got[pl.ds(source + 3 + c, 1), :] * weight_z for c in range(3)]
            load = jnp.concatenate(split_2(jnp.concatenate(load, axis=0)), axis=1).astype(bf16)
            stack = jnp.concatenate(stack, axis=0)
            loads[device] = load
            stacks[device] = stack
            parts[sub] = spread_pair(load, stack)

    def step(index, carry):
        gather_windows(total, rows, parts, index - 1, SPREAD_UNROLL)
        compute(index)
        return carry

    compute(0)
    copy.wait()
    lax.fori_loop(1, LANES // SPREAD_UNROLL, step, 0)
    gather_windows(total, rows, parts, LANES // SPREAD_UNROLL - 1, SPREAD_UNROLL)
    planes = spread_planes(total, picks)
    odd = lax.axis_index("slab") % 2 == 1
    for i in range(4):
        grid[i] = planes[i]
    for i in range(2):
        near[i] = jnp.where(odd, planes[i], planes[2 + i])
        far[i] = jnp.where(odd, planes[2 + i], planes[i])


def spread(got, picks):
    return pl.pallas_call(
        spread_kernel,
        out_shape=(
            jax.ShapeDtypeStruct((4, NY, LANES), f32),
            jax.ShapeDtypeStruct((2, NY, LANES), f32),
            jax.ShapeDtypeStruct((2, NY, LANES), f32),
            jax.ShapeDtypeStruct((8, LANES), jnp.int32),
            jax.ShapeDtypeStruct((LANES, 2, 24, LANES), f32),
            jax.ShapeDtypeStruct((LANES, 48, 2 * LANES), bf16),
            jax.ShapeDtypeStruct((LANES, 128, LANES), bf16),
        ),
        in_specs=[vmem()] * 2,
        out_specs=(vmem(),) * 7,
        scratch_shapes=[
            pltpu.VMEM((TABLE, LANES), f32),
            pltpu.VMEM((SPREAD_UNROLL, 48, LANES), f32),
            pltpu.SMEM((8, LANES), jnp.int32),
            pltpu.SemaphoreType.DMA,
        ],
        compiler_params=params(),
    )(got, picks)


def forcing_of(cells, c):
    lane = lax.broadcasted_iota(jnp.int32, (NY, NZ), 1)
    if c:
        cells = pltpu.roll(cells, LANES - 32 * c, 1)
    return jnp.where(lane < 32, cells, 0.0)


def fluid_plane(load, cells, p):
    centers = [load(c, p) for c in range(3)]
    results = []
    for c in range(3):
        center = centers[c]
        x_plus, x_minus = load(c, p + 1), load(c, p - 1)
        y_plus, y_minus = pltpu.roll(center, NY - 1, 0), pltpu.roll(center, 1, 0)
        z_plus, z_minus = pltpu.roll(center, NZ - 1, 1), pltpu.roll(center, 1, 1)
        around = (x_plus + x_minus) + (y_plus + y_minus) + (z_plus + z_minus)
        advect = (
            centers[0] * (x_plus - x_minus)
            + centers[1] * (y_plus - y_minus)
            + centers[2] * (z_plus - z_minus)
        )
        results.append(
            (1.0 - 6.0 * time_step * viscosity) * center
            + (time_step * viscosity) * around
            - (0.5 * time_step) * advect
            + forcing_of(cells, c)
        )
    return results


def packed_plane(parts):
    lane = lax.broadcasted_iota(jnp.int32, (NY, LANES), 1)
    cells = jnp.where(lane < 32, parts[0], 0.0)
    for c in (1, 2):
        moved = pltpu.roll(parts[c], 32 * c, 1)
        cells = jnp.where((lane >= 32 * c) & (lane < 32 * c + 32), moved, cells)
    return cells


def fill_table(table, planes, picks):
    cells = jnp.concatenate([packed_plane(parts) for parts in planes], axis=0).T[:96]
    split = stack_2(cells)
    lane = lax.broadcasted_iota(jnp.int32, (96, LANES), 1)
    for y in range(0, WINDOWS, 2):
        wide = min(2, WINDOWS - y)
        both = dot(split, picks[:, y * LANES : (y + wide) * LANES], NN)
        for i in range(wide):
            part = both[:, i * LANES : (i + 1) * LANES]
            table[(y + i) * 96 : (y + i + 1) * 96] = jnp.where(lane < 64, part[:96], part[96:])


def fold(a, b, width):
    if b is None:
        return a + pltpu.roll(a, width, 0)
    bit = (lax.broadcasted_iota(jnp.int32, (8, LANES), 0) & width) == 0
    return jnp.where(bit, a, b) + pltpu.roll(jnp.where(bit, b, a), width, 0)


def window_sums(table, rows, device, stack, weights):
    cells = []
    for slot in range(2):
        row = rows[slot, device]
        for c in range(3):
            cells.append(table[pl.ds(row + 32 * c, 8), :])
    both = jnp.concatenate([stack[:64], stack[64:]], axis=1)
    both = jnp.concatenate([both, both], axis=0)
    values = dot(jnp.concatenate(cells, axis=0).astype(bf16), both, NN)
    v = []
    for slot in range(2):
        weight_z = weights[device, slot, 16:24]
        for c in range(3):
            start = slot * 24 + c * 8
            v.append(values[start : start + 8, slot * LANES : (slot + 1) * LANES] * weight_z)
    low = fold(fold(v[0], v[1], 1), fold(v[2], v[3], 1), 2)
    high = fold(fold(v[4], v[5], 1), None, 2)
    return fold(low, high, 4)[:6]


def halo_reader(inside, same, cross, depth):
    odd = lax.axis_index("slab") % 2 == 1

    def load(c, p):
        if p < 0:
            return jnp.where(odd, same[c, p + depth], cross[c, p + depth])
        if p >= CX:
            return jnp.where(odd, cross[c, p - CX], same[c, p - CX])
        return inside[c, p]

    return load


def inner_kernel(
    velocity, same, cross, grid, rows_in, weights, loads, picks,
    step_1, step_2, middle, partial, stacks, total, parts, table, rows, sem
):
    copy = pltpu.make_async_copy(rows_in, rows, sem)
    copy.start()
    total[...] = jnp.zeros_like(total)

    def compute(index):
        for sub in range(MIDDLE_UNROLL):
            device = index * MIDDLE_UNROLL + sub
            stack = jnp.concatenate(
                [
                    plane_stack(weights[device, slot, 0:8], weights[device, slot, 8:16], MIDDLE)
                    for slot in range(2)
                ],
                axis=0,
            )
            stacks[device] = stack
            parts[sub] = spread_pair(loads[device], stack)

    def spread_step(index, carry):
        gather_windows(total, rows, parts, index - 1, MIDDLE_UNROLL)
        compute(index)
        return carry

    compute(0)
    copy.wait()
    lax.fori_loop(1, LANES // MIDDLE_UNROLL, spread_step, 0)
    gather_windows(total, rows, parts, LANES // MIDDLE_UNROLL - 1, MIDDLE_UNROLL)
    forces = dict(zip(MIDDLE, spread_planes(total, picks)))
    for i, p in enumerate(EDGES):
        forces[p] = grid[i]

    load_0 = halo_reader(velocity, same, cross, SUBSTEPS)
    for p in range(CX):
        for c, value in enumerate(fluid_plane(load_0, forces[p], p)):
            step_1[c, p] = value
    for p in range(1, CX - 1):
        for c, value in enumerate(fluid_plane(lambda c, p: step_1[c, p], forces[p], p)):
            step_2[c, p] = value
    planes = []
    for p in MIDDLE:
        planes.append(fluid_plane(lambda c, p: step_2[c, p], forces[p], p))
        for c in range(3):
            middle[c, p - MIDDLE[0]] = planes[-1][c]
    fill_table(table, planes, picks)

    def step(index, carry):
        for sub in range(INNER_UNROLL):
            device = index * INNER_UNROLL + sub
            partial[pl.ds(device * 6, 6), :] = window_sums(
                table, rows, device, stacks[device], weights
            )
        return carry

    lax.fori_loop(0, LANES // INNER_UNROLL, step, 0)


def inner(*arguments):
    return pl.pallas_call(
        inner_kernel,
        out_shape=(
            jax.ShapeDtypeStruct((3, CX, NY, NZ), f32),
            jax.ShapeDtypeStruct((3, CX, NY, NZ), f32),
            jax.ShapeDtypeStruct((3, len(MIDDLE), NY, NZ), f32),
            jax.ShapeDtypeStruct((6 * LANES, LANES), f32),
        ),
        in_specs=[vmem()] * 8,
        out_specs=(vmem(),) * 4,
        scratch_shapes=[
            pltpu.VMEM((LANES, 128, LANES), bf16),
            pltpu.VMEM((TABLE, LANES), f32),
            pltpu.VMEM((MIDDLE_UNROLL, 48, LANES), f32),
            pltpu.VMEM((TABLE, LANES), f32),
            pltpu.SMEM((8, LANES), jnp.int32),
            pltpu.SemaphoreType.DMA,
        ],
        compiler_params=params(),
        cost_estimate=pl.CostEstimate(
            flops=6_000_000_000, bytes_accessed=8_000_000, transcendentals=0
        ),
    )(*arguments)


def edge_kernel(
    velocity, same, cross, grid, near, far, rows_in, weights, stacks, picks,
    step_1, step_2, middle, partial,
    field, out, ends_1, ends_2, ends_3, table, rows, sems
):
    copies = [pltpu.make_async_copy(rows_in, rows, sems.at[0])]
    copies.append(
        pltpu.make_async_copy(middle, field.at[:, pl.ds(MIDDLE[0], len(MIDDLE))], sems.at[1])
    )
    for i, p in enumerate((0, CX - 2)):
        source, target = ends_3.at[:, pl.ds(2 * i, 2)], field.at[:, pl.ds(p, 2)]
        copies.append(pltpu.make_async_copy(source, target, sems.at[2 + i]))
    copies[0].start()
    copies[1].start()
    odd = lax.axis_index("slab") % 2 == 1

    def cells(p):
        if p < 0:
            return jnp.where(odd, near[p + 2], far[p + 2])
        if p >= CX:
            return jnp.where(odd, far[p - CX], near[p - CX])
        return grid[EDGES.index(p)]

    def reader(ends, inside, low):
        def load(c, p):
            for i, q in enumerate(low):
                if p == q:
                    return ends[c, i]
            return inside[c, p]

        return load

    planes_1 = (-2, -1, CX, CX + 1)
    planes_2 = (-1, 0, CX - 1, CX)
    load_0 = halo_reader(velocity, same, cross, SUBSTEPS)
    for i, p in enumerate(planes_1):
        for c, value in enumerate(fluid_plane(load_0, cells(p), p)):
            ends_1[c, i] = value
    load_1 = reader(ends_1, step_1, planes_1)
    for i, p in enumerate(planes_2):
        for c, value in enumerate(fluid_plane(load_1, cells(p), p)):
            ends_2[c, i] = value
    load_2 = reader(ends_2, step_2, planes_2)
    planes = []
    for i, p in enumerate(EDGES):
        planes.append(fluid_plane(load_2, cells(p), p))
        for c in range(3):
            ends_3[c, i] = planes[-1][c]
    copies[2].start()
    copies[3].start()
    fill_table(table, planes, picks)
    copies[0].wait()

    def step(index, carry):
        for sub in range(EDGE_UNROLL):
            device = index * EDGE_UNROLL + sub
            own = pl.ds(device * 6, 6)
            out[own, :] = partial[own, :] + window_sums(
                table, rows, device, stacks[device], weights
            )
        return carry

    lax.fori_loop(0, LANES // EDGE_UNROLL, step, 0)
    for copy in copies[1:]:
        copy.wait()


def edge(*arguments):
    return pl.pallas_call(
        edge_kernel,
        out_shape=(
            jax.ShapeDtypeStruct((3, CX, NY, NZ), f32),
            jax.ShapeDtypeStruct((6 * LANES, LANES), f32),
        ),
        in_specs=[vmem()] * 14,
        out_specs=(anywhere(), vmem()),
        scratch_shapes=[
            pltpu.VMEM((3, 4, NY, NZ), f32),
            pltpu.VMEM((3, 4, NY, NZ), f32),
            pltpu.VMEM((3, 4, NY, NZ), f32),
            pltpu.VMEM((TABLE, LANES), f32),
            pltpu.SMEM((8, LANES), jnp.int32),
            pltpu.SemaphoreType.DMA((4,)),
        ],
        compiler_params=params(),
    )(*arguments)


def pick_kernel(returned, back, out):
    chosen = back[...]
    for c in range(3):
        both = jnp.concatenate(
            [returned[pl.ds(3 * slot + c, LANES, stride=6), :] for slot in range(2)], axis=0
        )
        high, middle, low = split_3(both)
        out[c] = dot(chosen, high, NN) + dot(chosen, middle, NN) + dot(chosen, low, NN)


def pick(returned, back):
    return pl.pallas_call(
        pick_kernel,
        out_shape=jax.ShapeDtypeStruct((3, LANES, LANES), f32),
        in_specs=[vmem()] * 2,
        out_specs=vmem(),
        compiler_params=params(),
    )(returned, back)


def exchange(values):
    shape = values.shape
    values = values.reshape(LANES, 1, -1)
    values = lax.all_to_all(values, "slab", split_axis=0, concat_axis=0, tiled=True)
    return values.reshape(shape)


def swap(values, first):
    count = lax.axis_size("slab")
    pairs = []
    for i in range(first, count + first, 2):
        a, b = i % count, (i + 1) % count
        pairs += [(a, b), (b, a)]
    return lax.ppermute(values, "slab", pairs)


def body(velocity, node_coords, node_force, block_slab, block_offset):
    picks = window_picks()
    sent, back = prep(
        jnp.transpose(node_coords, (1, 0, 2)),
        jnp.transpose(node_force, (1, 0, 2)),
        jnp.transpose(block_slab, (1, 0)),
        jnp.transpose(block_offset, (1, 0)),
    )
    got = exchange(sent)
    odd = lax.axis_index("slab") % 2 == 1
    first, last = velocity[:, :SUBSTEPS], velocity[:, CX - SUBSTEPS :]
    cross = swap(jnp.where(odd, last, first), 1)
    same = swap(jnp.where(odd, first, last), 0)
    grid, near, far, rows, weights, loads, stacks = spread(got, picks)
    far = swap(far, 1)
    near = swap(near, 0)
    inside = inner(velocity, same, cross, grid, rows, weights, loads, picks)
    field, sums = edge(
        velocity, same, cross, grid, near, far, rows, weights, stacks, picks, *inside
    )
    node_velocity = pick(exchange(sums), back)
    return field, jnp.transpose(node_velocity, (1, 0, 2))


def solution(mesh):
    return jax.shard_map(
        body,
        mesh=mesh,
        in_specs=(
            P(None, "slab", None, None),
            P("slab", None, None),
            P("slab", None, None),
            P("slab", None),
            P("slab", None),
        ),
        out_specs=(P(None, "slab", None, None), P("slab", None, None)),
        check_vma=False,
    )
```

```python
import jax
import jax.numpy as jnp
from jax import lax
from jax.experimental import pallas as pl
from jax.experimental.pallas import tpu as pltpu
from jax.sharding import PartitionSpec as P

CX = 8
NY = 32
NZ = 128
SUBSTEPS = 3
LANES = 128
WINDOWS = 25
SPREAD_UNROLL = 32
INNER_UNROLL = 32
EDGE_UNROLL = 32

time_step = 0.1
viscosity = 0.2

f32 = jnp.float32
bf16 = jnp.bfloat16

COS_TERMS = (
    0.7071067481276141,
    -0.21808909214261787,
    0.011209883548645258,
    -0.0002299265021950359,
    2.3703615380631122e-06,
)

VMEM_LIMIT = 24 * 1024 * 1024
VMEM_ALL = 60 * 1024 * 1024


def vmem():
    return pl.BlockSpec(memory_space=pltpu.VMEM)


def anywhere():
    return pl.BlockSpec(memory_space=pl.ANY)


def params(limit=VMEM_LIMIT):
    return pltpu.CompilerParams(vmem_limit_bytes=limit)


def phi(distance):
    t = jnp.minimum(distance * distance, 4.0)
    total = COS_TERMS[4] * t + COS_TERMS[3]
    for term in (COS_TERMS[2], COS_TERMS[1], COS_TERMS[0]):
        total = total * t + term
    return total * total


def split_2(values):
    high = values.astype(bf16).astype(f32)
    return high, values - high


def split_3(values):
    high = values.astype(bf16)
    rest = values - high.astype(f32)
    middle = rest.astype(bf16)
    low = (rest - middle.astype(f32)).astype(bf16)
    return high, middle, low


def dot(a, b, dims):
    return lax.dot_general(a, b, (dims, ((), ())), preferred_element_type=f32)


NN = ((1,), (0,))
NT = ((1,), (1,))


TABLE = WINDOWS * 96
EDGES = (0, 1, 6, 7)
MIDDLE = (2, 3, 4, 5)
ORDER = EDGES + MIDDLE
SENT = 13
REACH = (CX - 4.0, 5.0, 5.0)


def fill_picks(picks):
    row = lax.broadcasted_iota(jnp.int32, (LANES, LANES), 0)
    lane = lax.broadcasted_iota(jnp.int32, (LANES, LANES), 1)
    apart = row - ((lane >> 3) & 3) * 32 - (lane & 7)
    for start in range(WINDOWS):
        chosen = jnp.where(apart == start, 1.0, 0.0)
        picks[:, start * LANES : (start + 1) * LANES] = chosen.astype(bf16)


def turned_picks_kernel(turned):
    row = lax.broadcasted_iota(jnp.int32, (LANES, 2 * LANES), 0)
    lane = lax.broadcasted_iota(jnp.int32, (LANES, 2 * LANES), 1)
    apart = lane - ((row >> 3) & 7) * 32 - (row & 7)
    for start in range(WINDOWS):
        chosen = jnp.where(apart == start, 1.0, 0.0)
        turned[start * LANES : (start + 1) * LANES] = chosen.astype(bf16)


def window_picks():
    return pl.pallas_call(
        turned_picks_kernel,
        out_shape=jax.ShapeDtypeStruct((WINDOWS * LANES, 2 * LANES), bf16),
        out_specs=vmem(),
        compiler_params=params(),
        cost_estimate=pl.CostEstimate(
            flops=2_000_000_000, bytes_accessed=4_000_000, transcendentals=0
        ),
    )()


def prep_kernel(coords_in, force_in, slab_in, offset_in, out, back, coords, force, slab, offset, sems):
    copies = [
        pltpu.make_async_copy(source, target, sems.at[i])
        for i, (source, target) in enumerate(
            ((slab_in, slab), (offset_in, offset), (coords_in, coords), (force_in, force))
        )
    ]
    for copy in copies:
        copy.start()
    row = lax.broadcasted_iota(jnp.int32, (LANES, LANES), 0)
    col = lax.broadcasted_iota(jnp.int32, (LANES, LANES), 1)
    before = (row < col).astype(f32).astype(bf16)
    copies[0].wait()
    hot = (jnp.broadcast_to(slab[...], (LANES, LANES)) == row).astype(f32)
    rank = dot(hot.astype(bf16), before, NN)
    first = jnp.where(rank < 0.5, hot, 0.0)
    second = hot - first
    both = jnp.concatenate([first, second], axis=0).astype(bf16)
    copies[1].wait()
    offsets = offset[...].astype(f32)
    rows = lax.broadcasted_iota(jnp.int32, (8, LANES), 0)
    spread_y = jnp.broadcast_to(offsets[0:1], (8, LANES))
    spread_z = jnp.broadcast_to(offsets[1:2], (8, LANES))
    tail = jnp.zeros((LANES, LANES), f32)
    empty = jnp.zeros((LANES - 8, LANES), f32)
    for slot, chosen in ((0, first), (1, second)):
        table = jnp.where(rows == 2 * slot, spread_y, 0.0) + jnp.where(
            rows == 2 * slot + 1, spread_z, 0.0
        )
        table = jnp.concatenate([table, empty], axis=0).astype(bf16)
        tail = tail + dot(chosen.astype(bf16), table, NT)
    out[pl.ds(12, LANES, stride=SENT), :] = tail
    for quantity in range(6):
        if quantity % 3 == 0:
            copies[2 + quantity // 3].wait()
        if quantity < 3:
            source = coords[quantity] * REACH[quantity]
        else:
            source = force[quantity - 3]
        high, middle, low = split_3(source)
        placed = dot(both, high, NN) + dot(both, middle, NN) + dot(both, low, NN)
        for slot in range(2):
            out[pl.ds(slot * 6 + quantity, LANES, stride=SENT), :] = placed[
                slot * LANES : (slot + 1) * LANES
            ]
    back[:, :LANES] = first.T.astype(bf16)
    back[:, LANES:] = second.T.astype(bf16)


def prep(coords, force, slab, offset):
    return pl.pallas_call(
        prep_kernel,
        out_shape=(
            jax.ShapeDtypeStruct((SENT * LANES, LANES), f32),
            jax.ShapeDtypeStruct((LANES, 2 * LANES), bf16),
        ),
        in_specs=[anywhere()] * 4,
        out_specs=(vmem(), vmem()),
        scratch_shapes=[
            pltpu.VMEM((3, LANES, LANES), f32),
            pltpu.VMEM((3, LANES, LANES), f32),
            pltpu.VMEM((1, LANES), jnp.int32),
            pltpu.VMEM((2, LANES), jnp.int32),
            pltpu.SemaphoreType.DMA((4,)),
        ],
        compiler_params=params(VMEM_ALL),
    )(coords, force, slab, offset)


def stack_2(values):
    high, low = split_2(values)
    return jnp.concatenate([high, low], axis=0).astype(bf16)


def joint_stack(weight_x, weight_y):
    return stack_2(jnp.concatenate([weight_x[a : a + 1] * weight_y for a in ORDER], axis=0))


def spread_pair(load, stack):
    turned = stack.T
    out = dot(load, jnp.concatenate([turned, turned], axis=0), NN)
    return jnp.concatenate([out[:24, :LANES], out[24:, LANES:]], axis=0)


def gather_windows(total, rows, parts, index, unroll):
    for sub in range(unroll):
        for slot in range(2):
            row = rows[slot, index * unroll + sub]
            for c in range(3):
                start = slot * 24 + c * 8
                total[pl.ds(row + 32 * c, 8), :] += parts[sub, start : start + 8]


def spread_planes(total, turned_picks):
    cells = jnp.zeros((192, 2 * LANES), f32)
    for y in range(0, WINDOWS, 2):
        wide = min(2, WINDOWS - y)
        both = [total[(y + i) * 96 : (y + i + 1) * 96] for i in range(wide)]
        both = both[0] if wide == 1 else jnp.concatenate(both, axis=1)
        chosen = turned_picks[y * LANES : (y + wide) * LANES]
        cells = cells + dot(stack_2(both), chosen, NN)
    cells = (cells[:96] + cells[96:]) * time_step
    cells = jnp.concatenate([cells, jnp.zeros((32, 2 * LANES), f32)], axis=0).T
    return {p: cells[i * NY : (i + 1) * NY] for i, p in enumerate(ORDER)}


def spread_kernel(
    got, turned_picks, grid, near, far, rows_out, weights_z, stacks, total, parts, rows, sem
):
    tail = got[pl.ds(12, LANES, stride=SENT), :].T
    y = jnp.concatenate([tail[0:1], tail[2:3]], axis=0)
    z = jnp.concatenate([tail[1:2], tail[3:4]], axis=0)
    y = jnp.clip(y - 1.0, 0.0, WINDOWS - 1.0)
    z = jnp.clip(z - 1.0, 0.0, WINDOWS - 1.0)
    start = (y * 96.0 + z).astype(jnp.int32)
    rows_out[...] = jnp.concatenate([start, jnp.zeros((6, LANES), jnp.int32)], axis=0)
    copy = pltpu.make_async_copy(rows_out, rows, sem)
    copy.start()
    total[...] = jnp.zeros_like(total)
    taps = lax.broadcasted_iota(jnp.int32, (8, LANES), 0).astype(f32) - 1.0

    def compute(index):
        for sub in range(SPREAD_UNROLL):
            device = index * SPREAD_UNROLL + sub
            load, stack = [], []
            for slot in range(2):
                source = device * SENT + slot * 6
                weight_x, weight_y, weight_z = [
                    phi(taps - got[pl.ds(source + dim, 1), :]) for dim in range(3)
                ]
                weights_z[device, slot] = weight_z
                stack.append(joint_stack(weight_x, weight_y))
                load += [got[pl.ds(source + 3 + c, 1), :] * weight_z for c in range(3)]
            load = jnp.concatenate(split_2(jnp.concatenate(load, axis=0)), axis=1).astype(bf16)
            stack = jnp.concatenate(stack, axis=0)
            stacks[device] = stack
            parts[sub] = spread_pair(load, stack)

    def step(index, carry):
        gather_windows(total, rows, parts, index - 1, SPREAD_UNROLL)
        compute(index)
        return carry

    compute(0)
    copy.wait()
    lax.fori_loop(1, LANES // SPREAD_UNROLL, step, 0)
    gather_windows(total, rows, parts, LANES // SPREAD_UNROLL - 1, SPREAD_UNROLL)
    planes = spread_planes(total, turned_picks)
    odd = lax.axis_index("slab") % 2 == 1
    for a in range(CX):
        grid[a] = planes[a]
    for a in range(2):
        near[a] = jnp.where(odd, planes[a], planes[CX - 2 + a])
        far[a] = jnp.where(odd, planes[CX - 2 + a], planes[a])


def spread(got, turned_picks):
    return pl.pallas_call(
        spread_kernel,
        out_shape=(
            jax.ShapeDtypeStruct((CX, NY, LANES), f32),
            jax.ShapeDtypeStruct((2, NY, LANES), f32),
            jax.ShapeDtypeStruct((2, NY, LANES), f32),
            jax.ShapeDtypeStruct((8, LANES), jnp.int32),
            jax.ShapeDtypeStruct((LANES, 2, 8, LANES), f32),
            jax.ShapeDtypeStruct((LANES, 256, LANES), bf16),
        ),
        in_specs=[vmem()] * 2,
        out_specs=(vmem(),) * 6,
        scratch_shapes=[
            pltpu.VMEM((TABLE, LANES), f32),
            pltpu.VMEM((SPREAD_UNROLL, 48, LANES), f32),
            pltpu.SMEM((8, LANES), jnp.int32),
            pltpu.SemaphoreType.DMA,
        ],
        compiler_params=params(),
    )(got, turned_picks)


def forcing_of(cells, c):
    lane = lax.broadcasted_iota(jnp.int32, (NY, NZ), 1)
    if c:
        cells = pltpu.roll(cells, LANES - 32 * c, 1)
    return jnp.where(lane < 32, cells, 0.0)


def fluid_plane(load, cells, p):
    centers = [load(c, p) for c in range(3)]
    results = []
    for c in range(3):
        center = centers[c]
        x_plus, x_minus = load(c, p + 1), load(c, p - 1)
        y_plus, y_minus = pltpu.roll(center, NY - 1, 0), pltpu.roll(center, 1, 0)
        z_plus, z_minus = pltpu.roll(center, NZ - 1, 1), pltpu.roll(center, 1, 1)
        around = (x_plus + x_minus) + (y_plus + y_minus) + (z_plus + z_minus)
        advect = (
            centers[0] * (x_plus - x_minus)
            + centers[1] * (y_plus - y_minus)
            + centers[2] * (z_plus - z_minus)
        )
        results.append(
            (1.0 - 6.0 * time_step * viscosity) * center
            + (time_step * viscosity) * around
            - (0.5 * time_step) * advect
            + forcing_of(cells, c)
        )
    return results


def packed_plane(parts):
    lane = lax.broadcasted_iota(jnp.int32, (NY, LANES), 1)
    cells = jnp.where(lane < 32, parts[0], 0.0)
    for c in (1, 2):
        moved = pltpu.roll(parts[c], 32 * c, 1)
        cells = jnp.where((lane >= 32 * c) & (lane < 32 * c + 32), moved, cells)
    return cells


def fill_table(table, planes, picks):
    cells = jnp.concatenate([packed_plane(parts) for parts in planes], axis=0).T[:96]
    split = stack_2(cells)
    lane = lax.broadcasted_iota(jnp.int32, (96, LANES), 1)
    for y in range(0, WINDOWS, 2):
        wide = min(2, WINDOWS - y)
        both = dot(split, picks[:, y * LANES : (y + wide) * LANES], NN)
        for i in range(wide):
            part = both[:, i * LANES : (i + 1) * LANES]
            table[(y + i) * 96 : (y + i + 1) * 96] = jnp.where(lane < 64, part[:96], part[96:])


def fold(a, b, width):
    if b is None:
        return a + pltpu.roll(a, width, 0)
    bit = (lax.broadcasted_iota(jnp.int32, (8, LANES), 0) & width) == 0
    return jnp.where(bit, a, b) + pltpu.roll(jnp.where(bit, b, a), width, 0)


def window_sums(table, rows, device, stack, weights_z, first):
    cells = []
    for slot in range(2):
        row = rows[slot, device]
        for c in range(3):
            cells.append(table[pl.ds(row + 32 * c, 8), :])
    high = jnp.concatenate([stack[first : first + 32], stack[128 + first : 160 + first]], axis=1)
    low = jnp.concatenate([stack[64 + first : 96 + first], stack[192 + first : 224 + first]], axis=1)
    both = jnp.concatenate([high, low, high, low], axis=0)
    values = dot(jnp.concatenate(cells, axis=0).astype(bf16), both, NN)
    v = []
    for slot in range(2):
        weight_z = weights_z[device, slot]
        for c in range(3):
            start = slot * 24 + c * 8
            v.append(values[start : start + 8, slot * LANES : (slot + 1) * LANES] * weight_z)
    low = fold(fold(v[0], v[1], 1), fold(v[2], v[3], 1), 2)
    high = fold(fold(v[4], v[5], 1), None, 2)
    return fold(low, high, 4)[:6]


def halo_reader(inside, same, cross, depth):
    odd = lax.axis_index("slab") % 2 == 1

    def load(c, p):
        if p < 0:
            return jnp.where(odd, same[c, p + depth], cross[c, p + depth])
        if p >= CX:
            return jnp.where(odd, cross[c, p - CX], same[c, p - CX])
        return inside[c, p]

    return load


def inner_kernel(
    velocity, same, cross, grid, rows_in, weights_z, stacks,
    step_1, step_2, middle, partial, picks, table, rows, sem
):
    copy = pltpu.make_async_copy(rows_in, rows, sem)
    copy.start()
    fill_picks(picks)
    load_0 = halo_reader(velocity, same, cross, SUBSTEPS)
    for p in range(CX):
        for c, value in enumerate(fluid_plane(load_0, grid[p], p)):
            step_1[c, p] = value
    for p in range(1, CX - 1):
        for c, value in enumerate(fluid_plane(lambda c, p: step_1[c, p], grid[p], p)):
            step_2[c, p] = value
    planes = []
    for p in MIDDLE:
        planes.append(fluid_plane(lambda c, p: step_2[c, p], grid[p], p))
        for c in range(3):
            middle[c, p - MIDDLE[0]] = planes[-1][c]
    fill_table(table, planes, picks)
    copy.wait()

    def step(index, carry):
        for sub in range(INNER_UNROLL):
            device = index * INNER_UNROLL + sub
            partial[pl.ds(device * 6, 6), :] = window_sums(
                table, rows, device, stacks[device], weights_z, 32
            )
        return carry

    lax.fori_loop(0, LANES // INNER_UNROLL, step, 0)


def inner(*arguments):
    return pl.pallas_call(
        inner_kernel,
        out_shape=(
            jax.ShapeDtypeStruct((3, CX, NY, NZ), f32),
            jax.ShapeDtypeStruct((3, CX, NY, NZ), f32),
            jax.ShapeDtypeStruct((3, len(MIDDLE), NY, NZ), f32),
            jax.ShapeDtypeStruct((6 * LANES, LANES), f32),
            jax.ShapeDtypeStruct((LANES, WINDOWS * LANES), bf16),
        ),
        in_specs=[vmem()] * 7,
        out_specs=(vmem(),) * 5,
        scratch_shapes=[
            pltpu.VMEM((TABLE, LANES), f32),
            pltpu.SMEM((8, LANES), jnp.int32),
            pltpu.SemaphoreType.DMA,
        ],
        compiler_params=params(),
        cost_estimate=pl.CostEstimate(
            flops=6_000_000_000, bytes_accessed=8_000_000, transcendentals=0
        ),
    )(*arguments)


def edge_kernel(
    velocity, same, cross, grid, near, far, rows_in, weights_z, stacks,
    step_1, step_2, middle, partial, picks,
    field, out, ends_1, ends_2, ends_3, table, rows, sems
):
    copies = [pltpu.make_async_copy(rows_in, rows, sems.at[0])]
    copies.append(
        pltpu.make_async_copy(middle, field.at[:, pl.ds(MIDDLE[0], len(MIDDLE))], sems.at[1])
    )
    for i, p in enumerate((0, CX - 2)):
        source, target = ends_3.at[:, pl.ds(2 * i, 2)], field.at[:, pl.ds(p, 2)]
        copies.append(pltpu.make_async_copy(source, target, sems.at[2 + i]))
    copies[0].start()
    copies[1].start()
    odd = lax.axis_index("slab") % 2 == 1

    def cells(p):
        if p < 0:
            return jnp.where(odd, near[p + 2], far[p + 2])
        if p >= CX:
            return jnp.where(odd, far[p - CX], near[p - CX])
        return grid[p]

    def reader(ends, inside, low):
        def load(c, p):
            for i, q in enumerate(low):
                if p == q:
                    return ends[c, i]
            return inside[c, p]

        return load

    planes_1 = (-2, -1, CX, CX + 1)
    planes_2 = (-1, 0, CX - 1, CX)
    load_0 = halo_reader(velocity, same, cross, SUBSTEPS)
    for i, p in enumerate(planes_1):
        for c, value in enumerate(fluid_plane(load_0, cells(p), p)):
            ends_1[c, i] = value
    load_1 = reader(ends_1, step_1, planes_1)
    for i, p in enumerate(planes_2):
        for c, value in enumerate(fluid_plane(load_1, cells(p), p)):
            ends_2[c, i] = value
    load_2 = reader(ends_2, step_2, planes_2)
    planes = []
    for i, p in enumerate(EDGES):
        planes.append(fluid_plane(load_2, cells(p), p))
        for c in range(3):
            ends_3[c, i] = planes[-1][c]
    copies[2].start()
    copies[3].start()
    fill_table(table, planes, picks)
    copies[0].wait()

    def step(index, carry):
        for sub in range(EDGE_UNROLL):
            device = index * EDGE_UNROLL + sub
            own = pl.ds(device * 6, 6)
            out[own, :] = partial[own, :] + window_sums(
                table, rows, device, stacks[device], weights_z, 0
            )
        return carry

    lax.fori_loop(0, LANES // EDGE_UNROLL, step, 0)
    for copy in copies[1:]:
        copy.wait()


def edge(*arguments):
    return pl.pallas_call(
        edge_kernel,
        out_shape=(
            jax.ShapeDtypeStruct((3, CX, NY, NZ), f32),
            jax.ShapeDtypeStruct((6 * LANES, LANES), f32),
        ),
        in_specs=[vmem()] * 14,
        out_specs=(anywhere(), vmem()),
        scratch_shapes=[
            pltpu.VMEM((3, 4, NY, NZ), f32),
            pltpu.VMEM((3, 4, NY, NZ), f32),
            pltpu.VMEM((3, 4, NY, NZ), f32),
            pltpu.VMEM((TABLE, LANES), f32),
            pltpu.SMEM((8, LANES), jnp.int32),
            pltpu.SemaphoreType.DMA((4,)),
        ],
        compiler_params=params(),
    )(*arguments)


def pick_kernel(returned, back, out):
    chosen = back[...]
    for c in range(3):
        both = jnp.concatenate(
            [returned[pl.ds(3 * slot + c, LANES, stride=6), :] for slot in range(2)], axis=0
        )
        high, middle, low = split_3(both)
        out[c] = dot(chosen, high, NN) + dot(chosen, middle, NN) + dot(chosen, low, NN)


def pick(returned, back):
    return pl.pallas_call(
        pick_kernel,
        out_shape=jax.ShapeDtypeStruct((3, LANES, LANES), f32),
        in_specs=[vmem()] * 2,
        out_specs=vmem(),
        compiler_params=params(),
    )(returned, back)


def exchange(values):
    shape = values.shape
    values = values.reshape(LANES, 1, -1)
    values = lax.all_to_all(values, "slab", split_axis=0, concat_axis=0, tiled=True)
    return values.reshape(shape)


def swap(values, first):
    count = lax.axis_size("slab")
    pairs = []
    for i in range(first, count + first, 2):
        a, b = i % count, (i + 1) % count
        pairs += [(a, b), (b, a)]
    return lax.ppermute(values, "slab", pairs)


def body(velocity, node_coords, node_force, block_slab, block_offset):
    turned_picks = window_picks()
    sent, back = prep(
        jnp.transpose(node_coords, (1, 0, 2)),
        jnp.transpose(node_force, (1, 0, 2)),
        jnp.transpose(block_slab, (1, 0)),
        jnp.transpose(block_offset, (1, 0)),
    )
    got = exchange(sent)
    odd = lax.axis_index("slab") % 2 == 1
    first, last = velocity[:, :SUBSTEPS], velocity[:, CX - SUBSTEPS :]
    cross = swap(jnp.where(odd, last, first), 1)
    same = swap(jnp.where(odd, first, last), 0)
    grid, near, far, rows, weights_z, stacks = spread(got, turned_picks)
    near = swap(near, 0)
    far = swap(far, 1)
    inside = inner(velocity, same, cross, grid, rows, weights_z, stacks)
    field, sums = edge(
        velocity, same, cross, grid, near, far, rows, weights_z, stacks, *inside
    )
    node_velocity = pick(exchange(sums), back)
    return field, jnp.transpose(node_velocity, (1, 0, 2))


def solution(mesh):
    return jax.shard_map(
        body,
        mesh=mesh,
        in_specs=(
            P(None, "slab", None, None),
            P("slab", None, None),
            P("slab", None, None),
            P("slab", None),
            P("slab", None),
        ),
        out_specs=(P(None, "slab", None, None), P("slab", None, None)),
        check_vma=False,
    )
```

```python
import jax
import jax.numpy as jnp
from jax import lax
from jax.experimental import pallas as pl
from jax.experimental.pallas import tpu as pltpu
from jax.sharding import PartitionSpec as P

CX = 8
NY = 32
NZ = 128
SUBSTEPS = 3
LANES = 128
WINDOWS = 25
GROUP = 16

time_step = 0.1
viscosity = 0.2

f32 = jnp.float32
bf16 = jnp.bfloat16

COS_TERMS = (
    0.7071067481276141,
    -0.21808909214261787,
    0.011209883548645258,
    -0.0002299265021950359,
    2.3703615380631122e-06,
)

VMEM_LIMIT = 24 * 1024 * 1024
VMEM_ALL = 60 * 1024 * 1024


def vmem():
    return pl.BlockSpec(memory_space=pltpu.VMEM)


def anywhere():
    return pl.BlockSpec(memory_space=pl.ANY)


def params(limit=VMEM_LIMIT):
    return pltpu.CompilerParams(vmem_limit_bytes=limit)


def phi(distance):
    t = jnp.minimum(distance * distance, 4.0)
    total = COS_TERMS[4] * t + COS_TERMS[3]
    for term in (COS_TERMS[2], COS_TERMS[1], COS_TERMS[0]):
        total = total * t + term
    return total * total


def split_2(values):
    high = values.astype(bf16).astype(f32)
    return high, values - high


def split_3(values):
    high = values.astype(bf16)
    rest = values - high.astype(f32)
    middle = rest.astype(bf16)
    low = (rest - middle.astype(f32)).astype(bf16)
    return high, middle, low


def dot(a, b, dims):
    return lax.dot_general(a, b, (dims, ((), ())), preferred_element_type=f32)


NN = ((1,), (0,))
NT = ((1,), (1,))


TABLE = WINDOWS * 96
EDGES = (0, 1, 6, 7)
MIDDLE = (2, 3, 4, 5)
ORDER = EDGES + MIDDLE
SENT = 13
REACH = (CX - 4.0, 5.0, 5.0)


def fill_picks(picks):
    row = lax.broadcasted_iota(jnp.int32, (LANES, LANES), 0)
    lane = lax.broadcasted_iota(jnp.int32, (LANES, LANES), 1)
    apart = row - ((lane >> 3) & 3) * 32 - (lane & 7)
    for start in range(WINDOWS):
        chosen = jnp.where(apart == start, 1.0, 0.0)
        picks[:, start * LANES : (start + 1) * LANES] = chosen.astype(bf16)


def turned_picks_kernel(turned):
    row = lax.broadcasted_iota(jnp.int32, (LANES, 2 * LANES), 0)
    lane = lax.broadcasted_iota(jnp.int32, (LANES, 2 * LANES), 1)
    apart = lane - ((row >> 3) & 7) * 32 - (row & 7)
    for start in range(WINDOWS):
        chosen = jnp.where(apart == start, 1.0, 0.0)
        turned[start * LANES : (start + 1) * LANES] = chosen.astype(bf16)


def window_picks():
    return pl.pallas_call(
        turned_picks_kernel,
        out_shape=jax.ShapeDtypeStruct((WINDOWS * LANES, 2 * LANES), bf16),
        out_specs=vmem(),
        compiler_params=params(),
        cost_estimate=pl.CostEstimate(
            flops=2_000_000_000, bytes_accessed=4_000_000, transcendentals=0
        ),
    )()


def prep_kernel(coords_in, force_in, slab_in, offset_in, out, back, coords, force, slab, offset, sems):
    copies = [
        pltpu.make_async_copy(source, target, sems.at[i])
        for i, (source, target) in enumerate(
            ((slab_in, slab), (offset_in, offset), (coords_in, coords), (force_in, force))
        )
    ]
    for copy in copies:
        copy.start()
    row = lax.broadcasted_iota(jnp.int32, (LANES, LANES), 0)
    col = lax.broadcasted_iota(jnp.int32, (LANES, LANES), 1)
    before = (row < col).astype(f32).astype(bf16)
    copies[0].wait()
    hot = (jnp.broadcast_to(slab[...], (LANES, LANES)) == row).astype(f32)
    rank = dot(hot.astype(bf16), before, NN)
    first = jnp.where(rank < 0.5, hot, 0.0)
    second = hot - first
    both = jnp.concatenate([first, second], axis=0).astype(bf16)
    copies[1].wait()
    offsets = offset[...].astype(f32)
    rows = lax.broadcasted_iota(jnp.int32, (8, LANES), 0)
    spread_y = jnp.broadcast_to(offsets[0:1], (8, LANES))
    spread_z = jnp.broadcast_to(offsets[1:2], (8, LANES))
    tail = jnp.zeros((LANES, LANES), f32)
    empty = jnp.zeros((LANES - 8, LANES), f32)
    for slot, chosen in ((0, first), (1, second)):
        table = jnp.where(rows == 2 * slot, spread_y, 0.0) + jnp.where(
            rows == 2 * slot + 1, spread_z, 0.0
        )
        table = jnp.concatenate([table, empty], axis=0).astype(bf16)
        tail = tail + dot(chosen.astype(bf16), table, NT)
    out[pl.ds(12, LANES, stride=SENT), :] = tail
    for quantity in range(6):
        if quantity % 3 == 0:
            copies[2 + quantity // 3].wait()
        if quantity < 3:
            source = coords[quantity] * REACH[quantity]
        else:
            source = force[quantity - 3]
        high, middle, low = split_3(source)
        placed = dot(both, high, NN) + dot(both, middle, NN) + dot(both, low, NN)
        for slot in range(2):
            out[pl.ds(slot * 6 + quantity, LANES, stride=SENT), :] = placed[
                slot * LANES : (slot + 1) * LANES
            ]
    back[:, :LANES] = first.T.astype(bf16)
    back[:, LANES:] = second.T.astype(bf16)


def prep(coords, force, slab, offset):
    return pl.pallas_call(
        prep_kernel,
        out_shape=(
            jax.ShapeDtypeStruct((SENT * LANES, LANES), f32),
            jax.ShapeDtypeStruct((LANES, 2 * LANES), bf16),
        ),
        in_specs=[anywhere()] * 4,
        out_specs=(vmem(), vmem()),
        scratch_shapes=[
            pltpu.VMEM((3, LANES, LANES), f32),
            pltpu.VMEM((3, LANES, LANES), f32),
            pltpu.VMEM((1, LANES), jnp.int32),
            pltpu.VMEM((2, LANES), jnp.int32),
            pltpu.SemaphoreType.DMA((4,)),
        ],
        compiler_params=params(VMEM_ALL),
    )(coords, force, slab, offset)


def stack_2(values):
    high, low = split_2(values)
    return jnp.concatenate([high, low], axis=0).astype(bf16)


def joint_stack(weight_x, weight_y):
    return stack_2(jnp.concatenate([weight_x[a : a + 1] * weight_y for a in ORDER], axis=0))


def spread_pair(load, stack):
    turned = stack.T
    out = dot(load, jnp.concatenate([turned, turned], axis=0), NN)
    return jnp.concatenate([out[:24, :LANES], out[24:, LANES:]], axis=0)


def gather_windows(total, rows, parts, index):
    for sub in range(GROUP):
        for slot in range(2):
            row = rows[slot, index * GROUP + sub]
            for c in range(3):
                start = slot * 24 + c * 8
                total[pl.ds(row + 32 * c, 8), :] += parts[sub, start : start + 8]


def spread_planes(total, turned_picks):
    cells = jnp.zeros((192, 2 * LANES), f32)
    for y in range(0, WINDOWS, 2):
        wide = min(2, WINDOWS - y)
        both = [total[(y + i) * 96 : (y + i + 1) * 96] for i in range(wide)]
        both = both[0] if wide == 1 else jnp.concatenate(both, axis=1)
        chosen = turned_picks[y * LANES : (y + wide) * LANES]
        cells = cells + dot(stack_2(both), chosen, NN)
    cells = (cells[:96] + cells[96:]) * time_step
    cells = jnp.concatenate([cells, jnp.zeros((32, 2 * LANES), f32)], axis=0).T
    return {p: cells[i * NY : (i + 1) * NY] for i, p in enumerate(ORDER)}


def spread_kernel(
    got, turned_picks, grid, near, far, rows_out, weights_z, stacks, total, parts, rows, sem
):
    tail = got[pl.ds(12, LANES, stride=SENT), :].T
    y = jnp.concatenate([tail[0:1], tail[2:3]], axis=0)
    z = jnp.concatenate([tail[1:2], tail[3:4]], axis=0)
    y = jnp.clip(y - 1.0, 0.0, WINDOWS - 1.0)
    z = jnp.clip(z - 1.0, 0.0, WINDOWS - 1.0)
    start = (y * 96.0 + z).astype(jnp.int32)
    rows_out[...] = jnp.concatenate([start, jnp.zeros((6, LANES), jnp.int32)], axis=0)
    copy = pltpu.make_async_copy(rows_out, rows, sem)
    copy.start()
    total[...] = jnp.zeros_like(total)
    taps = lax.broadcasted_iota(jnp.int32, (8, LANES), 0).astype(f32) - 1.0

    def compute(index):
        for sub in range(GROUP):
            device = index * GROUP + sub
            load, stack = [], []
            for slot in range(2):
                source = device * SENT + slot * 6
                weight_x, weight_y, weight_z = [
                    phi(taps - got[pl.ds(source + dim, 1), :]) for dim in range(3)
                ]
                weights_z[device, slot] = weight_z
                stack.append(joint_stack(weight_x, weight_y))
                load += [got[pl.ds(source + 3 + c, 1), :] * weight_z for c in range(3)]
            load = jnp.concatenate(split_2(jnp.concatenate(load, axis=0)), axis=1).astype(bf16)
            stack = jnp.concatenate(stack, axis=0)
            stacks[device] = stack
            parts[sub] = spread_pair(load, stack)

    compute(0)
    copy.wait()
    for index in range(1, LANES // GROUP):
        gather_windows(total, rows, parts, index - 1)
        compute(index)
    gather_windows(total, rows, parts, LANES // GROUP - 1)
    planes = spread_planes(total, turned_picks)
    odd = lax.axis_index("slab") % 2 == 1
    for a in range(CX):
        grid[a] = planes[a]
    for a in range(2):
        near[a] = jnp.where(odd, planes[a], planes[CX - 2 + a])
        far[a] = jnp.where(odd, planes[CX - 2 + a], planes[a])


def spread(got, turned_picks):
    return pl.pallas_call(
        spread_kernel,
        out_shape=(
            jax.ShapeDtypeStruct((CX, NY, LANES), f32),
            jax.ShapeDtypeStruct((2, NY, LANES), f32),
            jax.ShapeDtypeStruct((2, NY, LANES), f32),
            jax.ShapeDtypeStruct((8, LANES), jnp.int32),
            jax.ShapeDtypeStruct((LANES, 2, 8, LANES), f32),
            jax.ShapeDtypeStruct((LANES, 256, LANES), bf16),
        ),
        in_specs=[vmem()] * 2,
        out_specs=(vmem(),) * 6,
        scratch_shapes=[
            pltpu.VMEM((TABLE, LANES), f32),
            pltpu.VMEM((GROUP, 48, LANES), f32),
            pltpu.SMEM((8, LANES), jnp.int32),
            pltpu.SemaphoreType.DMA,
        ],
        compiler_params=params(),
    )(got, turned_picks)


def forcing_of(cells, c):
    lane = lax.broadcasted_iota(jnp.int32, (NY, NZ), 1)
    if c:
        cells = pltpu.roll(cells, LANES - 32 * c, 1)
    return jnp.where(lane < 32, cells, 0.0)


def fluid_plane(load, cells, p):
    centers = [load(c, p) for c in range(3)]
    results = []
    for c in range(3):
        center = centers[c]
        x_plus, x_minus = load(c, p + 1), load(c, p - 1)
        y_plus, y_minus = pltpu.roll(center, NY - 1, 0), pltpu.roll(center, 1, 0)
        z_plus, z_minus = pltpu.roll(center, NZ - 1, 1), pltpu.roll(center, 1, 1)
        around = (x_plus + x_minus) + (y_plus + y_minus) + (z_plus + z_minus)
        advect = (
            centers[0] * (x_plus - x_minus)
            + centers[1] * (y_plus - y_minus)
            + centers[2] * (z_plus - z_minus)
        )
        results.append(
            (1.0 - 6.0 * time_step * viscosity) * center
            + (time_step * viscosity) * around
            - (0.5 * time_step) * advect
            + forcing_of(cells, c)
        )
    return results


def packed_plane(parts):
    lane = lax.broadcasted_iota(jnp.int32, (NY, LANES), 1)
    cells = jnp.where(lane < 32, parts[0], 0.0)
    for c in (1, 2):
        moved = pltpu.roll(parts[c], 32 * c, 1)
        cells = jnp.where((lane >= 32 * c) & (lane < 32 * c + 32), moved, cells)
    return cells


def fill_table(table, planes, picks):
    cells = jnp.concatenate([packed_plane(parts) for parts in planes], axis=0).T[:96]
    split = stack_2(cells)
    lane = lax.broadcasted_iota(jnp.int32, (96, LANES), 1)
    for y in range(0, WINDOWS, 2):
        wide = min(2, WINDOWS - y)
        both = dot(split, picks[:, y * LANES : (y + wide) * LANES], NN)
        for i in range(wide):
            part = both[:, i * LANES : (i + 1) * LANES]
            table[(y + i) * 96 : (y + i + 1) * 96] = jnp.where(lane < 64, part[:96], part[96:])


def fold(a, b, width):
    if b is None:
        return a + pltpu.roll(a, width, 0)
    bit = (lax.broadcasted_iota(jnp.int32, (8, LANES), 0) & width) == 0
    return jnp.where(bit, a, b) + pltpu.roll(jnp.where(bit, b, a), width, 0)


def window_sums(table, rows, device, stack, weights_z, first):
    cells = []
    for slot in range(2):
        row = rows[slot, device]
        for c in range(3):
            cells.append(table[pl.ds(row + 32 * c, 8), :])
    high = jnp.concatenate([stack[first : first + 32], stack[128 + first : 160 + first]], axis=1)
    low = jnp.concatenate([stack[64 + first : 96 + first], stack[192 + first : 224 + first]], axis=1)
    both = jnp.concatenate([high, low, high, low], axis=0)
    values = dot(jnp.concatenate(cells, axis=0).astype(bf16), both, NN)
    v = []
    for slot in range(2):
        weight_z = weights_z[device, slot]
        for c in range(3):
            start = slot * 24 + c * 8
            v.append(values[start : start + 8, slot * LANES : (slot + 1) * LANES] * weight_z)
    low = fold(fold(v[0], v[1], 1), fold(v[2], v[3], 1), 2)
    high = fold(fold(v[4], v[5], 1), None, 2)
    return fold(low, high, 4)[:6]


def halo_reader(inside, same, cross, depth):
    odd = lax.axis_index("slab") % 2 == 1

    def load(c, p):
        if p < 0:
            return jnp.where(odd, same[c, p + depth], cross[c, p + depth])
        if p >= CX:
            return jnp.where(odd, cross[c, p - CX], same[c, p - CX])
        return inside[c, p]

    return load


def inner_kernel(
    velocity, same, cross, grid, rows_in, weights_z, stacks,
    step_1, step_2, middle, partial, picks, table, rows, sem
):
    copy = pltpu.make_async_copy(rows_in, rows, sem)
    copy.start()
    fill_picks(picks)
    load_0 = halo_reader(velocity, same, cross, SUBSTEPS)
    for p in range(CX):
        for c, value in enumerate(fluid_plane(load_0, grid[p], p)):
            step_1[c, p] = value
    for p in range(1, CX - 1):
        for c, value in enumerate(fluid_plane(lambda c, p: step_1[c, p], grid[p], p)):
            step_2[c, p] = value
    planes = []
    for p in MIDDLE:
        planes.append(fluid_plane(lambda c, p: step_2[c, p], grid[p], p))
        for c in range(3):
            middle[c, p - MIDDLE[0]] = planes[-1][c]
    fill_table(table, planes, picks)
    copy.wait()

    for device in range(LANES):
        partial[device * 6 : device * 6 + 6] = window_sums(
            table, rows, device, stacks[device], weights_z, 32
        )


def inner(*arguments):
    return pl.pallas_call(
        inner_kernel,
        out_shape=(
            jax.ShapeDtypeStruct((3, CX, NY, NZ), f32),
            jax.ShapeDtypeStruct((3, CX, NY, NZ), f32),
            jax.ShapeDtypeStruct((3, len(MIDDLE), NY, NZ), f32),
            jax.ShapeDtypeStruct((6 * LANES, LANES), f32),
            jax.ShapeDtypeStruct((LANES, WINDOWS * LANES), bf16),
        ),
        in_specs=[vmem()] * 7,
        out_specs=(vmem(),) * 5,
        scratch_shapes=[
            pltpu.VMEM((TABLE, LANES), f32),
            pltpu.SMEM((8, LANES), jnp.int32),
            pltpu.SemaphoreType.DMA,
        ],
        compiler_params=params(),
        cost_estimate=pl.CostEstimate(
            flops=6_000_000_000, bytes_accessed=8_000_000, transcendentals=0
        ),
    )(*arguments)


def edge_kernel(
    velocity, same, cross, grid, near, far, rows_in, weights_z, stacks,
    step_1, step_2, middle, partial, picks,
    field, out, ends_1, ends_2, ends_3, table, rows, sems
):
    copies = [pltpu.make_async_copy(rows_in, rows, sems.at[0])]
    copies.append(
        pltpu.make_async_copy(middle, field.at[:, pl.ds(MIDDLE[0], len(MIDDLE))], sems.at[1])
    )
    for i, p in enumerate((0, CX - 2)):
        source, target = ends_3.at[:, pl.ds(2 * i, 2)], field.at[:, pl.ds(p, 2)]
        copies.append(pltpu.make_async_copy(source, target, sems.at[2 + i]))
    copies[0].start()
    copies[1].start()
    odd = lax.axis_index("slab") % 2 == 1

    def cells(p):
        if p < 0:
            return jnp.where(odd, near[p + 2], far[p + 2])
        if p >= CX:
            return jnp.where(odd, far[p - CX], near[p - CX])
        return grid[p]

    def reader(ends, inside, low):
        def load(c, p):
            for i, q in enumerate(low):
                if p == q:
                    return ends[c, i]
            return inside[c, p]

        return load

    planes_1 = (-2, -1, CX, CX + 1)
    planes_2 = (-1, 0, CX - 1, CX)
    load_0 = halo_reader(velocity, same, cross, SUBSTEPS)
    for i, p in enumerate(planes_1):
        for c, value in enumerate(fluid_plane(load_0, cells(p), p)):
            ends_1[c, i] = value
    load_1 = reader(ends_1, step_1, planes_1)
    for i, p in enumerate(planes_2):
        for c, value in enumerate(fluid_plane(load_1, cells(p), p)):
            ends_2[c, i] = value
    load_2 = reader(ends_2, step_2, planes_2)
    planes = []
    for i, p in enumerate(EDGES):
        planes.append(fluid_plane(load_2, cells(p), p))
        for c in range(3):
            ends_3[c, i] = planes[-1][c]
    copies[2].start()
    copies[3].start()
    fill_table(table, planes, picks)
    copies[0].wait()

    for device in range(LANES):
        own = slice(device * 6, device * 6 + 6)
        out[own] = partial[own] + window_sums(
            table, rows, device, stacks[device], weights_z, 0
        )
    for copy in copies[1:]:
        copy.wait()


def edge(*arguments):
    return pl.pallas_call(
        edge_kernel,
        out_shape=(
            jax.ShapeDtypeStruct((3, CX, NY, NZ), f32),
            jax.ShapeDtypeStruct((6 * LANES, LANES), f32),
        ),
        in_specs=[vmem()] * 14,
        out_specs=(anywhere(), vmem()),
        scratch_shapes=[
            pltpu.VMEM((3, 4, NY, NZ), f32),
            pltpu.VMEM((3, 4, NY, NZ), f32),
            pltpu.VMEM((3, 4, NY, NZ), f32),
            pltpu.VMEM((TABLE, LANES), f32),
            pltpu.SMEM((8, LANES), jnp.int32),
            pltpu.SemaphoreType.DMA((4,)),
        ],
        compiler_params=params(),
    )(*arguments)


def pick_kernel(returned, back, out):
    chosen = back[...]
    for c in range(3):
        both = jnp.concatenate(
            [returned[pl.ds(3 * slot + c, LANES, stride=6), :] for slot in range(2)], axis=0
        )
        high, middle, low = split_3(both)
        out[c] = dot(chosen, high, NN) + dot(chosen, middle, NN) + dot(chosen, low, NN)


def pick(returned, back):
    return pl.pallas_call(
        pick_kernel,
        out_shape=jax.ShapeDtypeStruct((3, LANES, LANES), f32),
        in_specs=[vmem()] * 2,
        out_specs=vmem(),
        compiler_params=params(),
    )(returned, back)


def exchange(values):
    shape = values.shape
    values = values.reshape(LANES, 1, -1)
    values = lax.all_to_all(values, "slab", split_axis=0, concat_axis=0, tiled=True)
    return values.reshape(shape)


def swap(values, first):
    count = lax.axis_size("slab")
    pairs = []
    for i in range(first, count + first, 2):
        a, b = i % count, (i + 1) % count
        pairs += [(a, b), (b, a)]
    return lax.ppermute(values, "slab", pairs)


def body(velocity, node_coords, node_force, block_slab, block_offset):
    turned_picks = window_picks()
    sent, back = prep(
        jnp.transpose(node_coords, (1, 0, 2)),
        jnp.transpose(node_force, (1, 0, 2)),
        jnp.transpose(block_slab, (1, 0)),
        jnp.transpose(block_offset, (1, 0)),
    )
    got = exchange(sent)
    odd = lax.axis_index("slab") % 2 == 1
    first, last = velocity[:, :SUBSTEPS], velocity[:, CX - SUBSTEPS :]
    cross = swap(jnp.where(odd, last, first), 1)
    same = swap(jnp.where(odd, first, last), 0)
    grid, near, far, rows, weights_z, stacks = spread(got, turned_picks)
    near = swap(near, 0)
    far = swap(far, 1)
    inside = inner(velocity, same, cross, grid, rows, weights_z, stacks)
    field, sums = edge(
        velocity, same, cross, grid, near, far, rows, weights_z, stacks, *inside
    )
    node_velocity = pick(exchange(sums), back)
    return field, jnp.transpose(node_velocity, (1, 0, 2))


def solution(mesh):
    return jax.shard_map(
        body,
        mesh=mesh,
        in_specs=(
            P(None, "slab", None, None),
            P("slab", None, None),
            P("slab", None, None),
            P("slab", None),
            P("slab", None),
        ),
        out_specs=(P(None, "slab", None, None), P("slab", None, None)),
        check_vma=False,
    )
```

```python
import jax
import jax.numpy as jnp
from jax import lax
from jax.experimental import pallas as pl
from jax.experimental.pallas import tpu as pltpu
from jax.sharding import PartitionSpec as P

CX = 8
NY = 32
NZ = 128
SUBSTEPS = 3
LANES = 128
WINDOWS = 25
GROUP = 16

time_step = 0.1
viscosity = 0.2

f32 = jnp.float32
bf16 = jnp.bfloat16

COS_TERMS = (
    0.7071067481276141,
    -0.21808909214261787,
    0.011209883548645258,
    -0.0002299265021950359,
    2.3703615380631122e-06,
)

VMEM_LIMIT = 24 * 1024 * 1024
VMEM_ALL = 60 * 1024 * 1024


def vmem():
    return pl.BlockSpec(memory_space=pltpu.VMEM)


def anywhere():
    return pl.BlockSpec(memory_space=pl.ANY)


def params(limit=VMEM_LIMIT):
    return pltpu.CompilerParams(vmem_limit_bytes=limit)


def phi(distance):
    t = jnp.minimum(distance * distance, 4.0)
    total = COS_TERMS[4] * t + COS_TERMS[3]
    for term in (COS_TERMS[2], COS_TERMS[1], COS_TERMS[0]):
        total = total * t + term
    return total * total


def split_2(values):
    high = values.astype(bf16).astype(f32)
    return high, values - high


def split_3(values):
    high = values.astype(bf16)
    rest = values - high.astype(f32)
    middle = rest.astype(bf16)
    low = (rest - middle.astype(f32)).astype(bf16)
    return high, middle, low


def dot(a, b, dims):
    return lax.dot_general(a, b, (dims, ((), ())), preferred_element_type=f32)


NN = ((1,), (0,))
NT = ((1,), (1,))


TABLE = WINDOWS * 96
EDGES = (0, 1, 6, 7)
HALO = (-2, -1, CX, CX + 1)
MIDDLE = (2, 3, 4, 5)
ORDER = EDGES + MIDDLE
SENT = 13
REACH = (CX - 4.0, 5.0, 5.0)


def fill_picks(picks):
    row = lax.broadcasted_iota(jnp.int32, (LANES, LANES), 0)
    lane = lax.broadcasted_iota(jnp.int32, (LANES, LANES), 1)
    apart = row - ((lane >> 3) & 3) * 32 - (lane & 7)
    for start in range(WINDOWS):
        chosen = jnp.where(apart == start, 1.0, 0.0)
        picks[:, start * LANES : (start + 1) * LANES] = chosen.astype(bf16)


def turned_picks_kernel(turned):
    row = lax.broadcasted_iota(jnp.int32, (LANES, 2 * LANES), 0)
    lane = lax.broadcasted_iota(jnp.int32, (LANES, 2 * LANES), 1)
    apart = lane - ((row >> 3) & 7) * 32 - (row & 7)
    for start in range(WINDOWS):
        chosen = jnp.where(apart == start, 1.0, 0.0)
        turned[start * LANES : (start + 1) * LANES] = chosen.astype(bf16)


def window_picks():
    return pl.pallas_call(
        turned_picks_kernel,
        out_shape=jax.ShapeDtypeStruct((WINDOWS * LANES, 2 * LANES), bf16),
        out_specs=vmem(),
        compiler_params=params(),
        cost_estimate=pl.CostEstimate(
            flops=2_000_000_000, bytes_accessed=4_000_000, transcendentals=0
        ),
    )()


def prep_kernel(coords_in, force_in, slab_in, offset_in, out, back, coords, force, slab, offset, sems):
    copies = [
        pltpu.make_async_copy(source, target, sems.at[i])
        for i, (source, target) in enumerate(
            ((slab_in, slab), (offset_in, offset), (coords_in, coords), (force_in, force))
        )
    ]
    for copy in copies:
        copy.start()
    row = lax.broadcasted_iota(jnp.int32, (LANES, LANES), 0)
    col = lax.broadcasted_iota(jnp.int32, (LANES, LANES), 1)
    before = (row < col).astype(f32).astype(bf16)
    copies[0].wait()
    hot = (jnp.broadcast_to(slab[...], (LANES, LANES)) == row).astype(f32)
    rank = dot(hot.astype(bf16), before, NN)
    first = jnp.where(rank < 0.5, hot, 0.0)
    second = hot - first
    both = jnp.concatenate([first, second], axis=0).astype(bf16)
    copies[1].wait()
    offsets = offset[...].astype(f32)
    rows = lax.broadcasted_iota(jnp.int32, (8, LANES), 0)
    spread_y = jnp.broadcast_to(offsets[0:1], (8, LANES))
    spread_z = jnp.broadcast_to(offsets[1:2], (8, LANES))
    tail = jnp.zeros((LANES, LANES), f32)
    empty = jnp.zeros((LANES - 8, LANES), f32)
    for slot, chosen in ((0, first), (1, second)):
        table = jnp.where(rows == 2 * slot, spread_y, 0.0) + jnp.where(
            rows == 2 * slot + 1, spread_z, 0.0
        )
        table = jnp.concatenate([table, empty], axis=0).astype(bf16)
        tail = tail + dot(chosen.astype(bf16), table, NT)
    out[pl.ds(12, LANES, stride=SENT), :] = tail
    for quantity in range(6):
        if quantity % 3 == 0:
            copies[2 + quantity // 3].wait()
        if quantity < 3:
            source = coords[quantity] * REACH[quantity]
        else:
            source = force[quantity - 3]
        high, middle, low = split_3(source)
        placed = dot(both, high, NN) + dot(both, middle, NN) + dot(both, low, NN)
        for slot in range(2):
            out[pl.ds(slot * 6 + quantity, LANES, stride=SENT), :] = placed[
                slot * LANES : (slot + 1) * LANES
            ]
    back[:, :LANES] = first.T.astype(bf16)
    back[:, LANES:] = second.T.astype(bf16)


def prep(coords, force, slab, offset):
    return pl.pallas_call(
        prep_kernel,
        out_shape=(
            jax.ShapeDtypeStruct((SENT * LANES, LANES), f32),
            jax.ShapeDtypeStruct((LANES, 2 * LANES), bf16),
        ),
        in_specs=[anywhere()] * 4,
        out_specs=(vmem(), vmem()),
        scratch_shapes=[
            pltpu.VMEM((3, LANES, LANES), f32),
            pltpu.VMEM((3, LANES, LANES), f32),
            pltpu.VMEM((1, LANES), jnp.int32),
            pltpu.VMEM((2, LANES), jnp.int32),
            pltpu.SemaphoreType.DMA((4,)),
        ],
        compiler_params=params(VMEM_ALL),
    )(coords, force, slab, offset)


def stack_2(values):
    high, low = split_2(values)
    return jnp.concatenate([high, low], axis=0).astype(bf16)


def joint_stack(weight_x, weight_y):
    return stack_2(jnp.concatenate([weight_x[a : a + 1] * weight_y for a in ORDER], axis=0))


def spread_pair(load, stack):
    turned = stack.T
    out = dot(load, jnp.concatenate([turned, turned], axis=0), NN)
    return jnp.concatenate([out[:24, :LANES], out[24:, LANES:]], axis=0)


def gather_windows(total, rows, parts, index):
    for sub in range(GROUP):
        for slot in range(2):
            row = rows[slot, index * GROUP + sub]
            for c in range(3):
                start = slot * 24 + c * 8
                total[pl.ds(row + 32 * c, 8), :] += parts[sub, start : start + 8]


def spread_planes(total, turned_picks):
    cells = jnp.zeros((192, 2 * LANES), f32)
    for y in range(0, WINDOWS, 2):
        wide = min(2, WINDOWS - y)
        both = [total[(y + i) * 96 : (y + i + 1) * 96] for i in range(wide)]
        both = both[0] if wide == 1 else jnp.concatenate(both, axis=1)
        chosen = turned_picks[y * LANES : (y + wide) * LANES]
        cells = cells + dot(stack_2(both), chosen, NN)
    cells = (cells[:96] + cells[96:]) * time_step
    cells = jnp.concatenate([cells, jnp.zeros((32, 2 * LANES), f32)], axis=0).T
    return {p: cells[i * NY : (i + 1) * NY] for i, p in enumerate(ORDER)}


def spread_kernel(
    got, turned_picks, far, near, grid, rows_out, weights_z, stacks, total, parts, rows, sem
):
    tail = got[pl.ds(12, LANES, stride=SENT), :].T
    y = jnp.concatenate([tail[0:1], tail[2:3]], axis=0)
    z = jnp.concatenate([tail[1:2], tail[3:4]], axis=0)
    y = jnp.clip(y - 1.0, 0.0, WINDOWS - 1.0)
    z = jnp.clip(z - 1.0, 0.0, WINDOWS - 1.0)
    start = (y * 96.0 + z).astype(jnp.int32)
    rows_out[...] = jnp.concatenate([start, jnp.zeros((6, LANES), jnp.int32)], axis=0)
    copy = pltpu.make_async_copy(rows_out, rows, sem)
    copy.start()
    total[...] = jnp.zeros_like(total)
    taps = lax.broadcasted_iota(jnp.int32, (8, LANES), 0).astype(f32) - 1.0

    def compute(index):
        for sub in range(GROUP):
            device = index * GROUP + sub
            load, stack = [], []
            for slot in range(2):
                source = device * SENT + slot * 6
                weight_x, weight_y, weight_z = [
                    phi(taps - got[pl.ds(source + dim, 1), :]) for dim in range(3)
                ]
                weights_z[device, slot] = weight_z
                stack.append(joint_stack(weight_x, weight_y))
                load += [got[pl.ds(source + 3 + c, 1), :] * weight_z for c in range(3)]
            load = jnp.concatenate(split_2(jnp.concatenate(load, axis=0)), axis=1).astype(bf16)
            stack = jnp.concatenate(stack, axis=0)
            stacks[device] = stack
            parts[sub] = spread_pair(load, stack)

    compute(0)
    copy.wait()
    for index in range(1, LANES // GROUP):
        gather_windows(total, rows, parts, index - 1)
        compute(index)
    gather_windows(total, rows, parts, LANES // GROUP - 1)
    planes = spread_planes(total, turned_picks)
    odd = lax.axis_index("slab") % 2 == 1
    for a in range(CX):
        grid[a] = planes[a]
    for a in range(2):
        near[a] = jnp.where(odd, planes[a], planes[CX - 2 + a])
        far[a] = jnp.where(odd, planes[CX - 2 + a], planes[a])


def spread(got, turned_picks):
    return pl.pallas_call(
        spread_kernel,
        out_shape=(
            jax.ShapeDtypeStruct((2, NY, LANES), f32),
            jax.ShapeDtypeStruct((2, NY, LANES), f32),
            jax.ShapeDtypeStruct((CX, NY, LANES), f32),
            jax.ShapeDtypeStruct((8, LANES), jnp.int32),
            jax.ShapeDtypeStruct((LANES, 2, 8, LANES), f32),
            jax.ShapeDtypeStruct((LANES, 256, LANES), bf16),
        ),
        in_specs=[vmem()] * 2,
        out_specs=(vmem(),) * 6,
        scratch_shapes=[
            pltpu.VMEM((TABLE, LANES), f32),
            pltpu.VMEM((GROUP, 48, LANES), f32),
            pltpu.SMEM((8, LANES), jnp.int32),
            pltpu.SemaphoreType.DMA,
        ],
        compiler_params=params(),
    )(got, turned_picks)


def forcing_of(cells, c):
    lane = lax.broadcasted_iota(jnp.int32, (NY, NZ), 1)
    if c:
        cells = pltpu.roll(cells, LANES - 32 * c, 1)
    return jnp.where(lane < 32, cells, 0.0)


def fluid_plane(load, cells, p):
    centers = [load(c, p) for c in range(3)]
    results = []
    for c in range(3):
        center = centers[c]
        x_plus, x_minus = load(c, p + 1), load(c, p - 1)
        y_plus, y_minus = pltpu.roll(center, NY - 1, 0), pltpu.roll(center, 1, 0)
        z_plus, z_minus = pltpu.roll(center, NZ - 1, 1), pltpu.roll(center, 1, 1)
        around = (x_plus + x_minus) + (y_plus + y_minus) + (z_plus + z_minus)
        advect = (
            centers[0] * (x_plus - x_minus)
            + centers[1] * (y_plus - y_minus)
            + centers[2] * (z_plus - z_minus)
        )
        moved = (
            (1.0 - 6.0 * time_step * viscosity) * center
            + (time_step * viscosity) * around
            - (0.5 * time_step) * advect
        )
        results.append(moved if cells is None else moved + forcing_of(cells, c))
    return results


def packed_plane(parts):
    lane = lax.broadcasted_iota(jnp.int32, (NY, LANES), 1)
    cells = jnp.where(lane < 32, parts[0], 0.0)
    for c in (1, 2):
        moved = pltpu.roll(parts[c], 32 * c, 1)
        cells = jnp.where((lane >= 32 * c) & (lane < 32 * c + 32), moved, cells)
    return cells


def fill_table(table, planes, picks):
    cells = jnp.concatenate([packed_plane(parts) for parts in planes], axis=0).T[:96]
    split = stack_2(cells)
    lane = lax.broadcasted_iota(jnp.int32, (96, LANES), 1)
    for y in range(0, WINDOWS, 2):
        wide = min(2, WINDOWS - y)
        both = dot(split, picks[:, y * LANES : (y + wide) * LANES], NN)
        for i in range(wide):
            part = both[:, i * LANES : (i + 1) * LANES]
            table[(y + i) * 96 : (y + i + 1) * 96] = jnp.where(lane < 64, part[:96], part[96:])


def fold(a, b, width):
    if b is None:
        return a + pltpu.roll(a, width, 0)
    bit = (lax.broadcasted_iota(jnp.int32, (8, LANES), 0) & width) == 0
    return jnp.where(bit, a, b) + pltpu.roll(jnp.where(bit, b, a), width, 0)


def window_sums(table, rows, device, stack, weights_z, first):
    cells = []
    for slot in range(2):
        row = rows[slot, device]
        for c in range(3):
            cells.append(table[pl.ds(row + 32 * c, 8), :])
    high = jnp.concatenate([stack[first : first + 32], stack[128 + first : 160 + first]], axis=1)
    low = jnp.concatenate([stack[64 + first : 96 + first], stack[192 + first : 224 + first]], axis=1)
    both = jnp.concatenate([high, low, high, low], axis=0)
    values = dot(jnp.concatenate(cells, axis=0).astype(bf16), both, NN)
    v = []
    for slot in range(2):
        weight_z = weights_z[device, slot]
        for c in range(3):
            start = slot * 24 + c * 8
            v.append(values[start : start + 8, slot * LANES : (slot + 1) * LANES] * weight_z)
    low = fold(fold(v[0], v[1], 1), fold(v[2], v[3], 1), 2)
    high = fold(fold(v[4], v[5], 1), None, 2)
    return fold(low, high, 4)[:6]


def halo_reader(inside, same, cross, depth):
    odd = lax.axis_index("slab") % 2 == 1

    def load(c, p):
        if p < 0:
            return jnp.where(odd, same[c, p + depth], cross[c, p + depth])
        if p >= CX:
            return jnp.where(odd, cross[c, p - CX], same[c, p - CX])
        return inside[c, p]

    return load


def inner_kernel(
    velocity, same, cross, grid, rows_in, weights_z, stacks,
    step_1, step_2, middle, partial, picks, unforced, table, rows, sem
):
    copy = pltpu.make_async_copy(rows_in, rows, sem)
    copy.start()
    fill_picks(picks)
    load_0 = halo_reader(velocity, same, cross, SUBSTEPS)
    for i, p in enumerate(HALO):
        for c, value in enumerate(fluid_plane(load_0, None, p)):
            unforced[c, i] = value
    for p in range(CX):
        for c, value in enumerate(fluid_plane(load_0, grid[p], p)):
            step_1[c, p] = value
    for p in range(1, CX - 1):
        for c, value in enumerate(fluid_plane(lambda c, p: step_1[c, p], grid[p], p)):
            step_2[c, p] = value
    planes = []
    for p in MIDDLE:
        planes.append(fluid_plane(lambda c, p: step_2[c, p], grid[p], p))
        for c in range(3):
            middle[c, p - MIDDLE[0]] = planes[-1][c]
    fill_table(table, planes, picks)
    copy.wait()

    for device in range(LANES):
        partial[device * 6 : device * 6 + 6] = window_sums(
            table, rows, device, stacks[device], weights_z, 32
        )


def inner(*arguments):
    return pl.pallas_call(
        inner_kernel,
        out_shape=(
            jax.ShapeDtypeStruct((3, CX, NY, NZ), f32),
            jax.ShapeDtypeStruct((3, CX, NY, NZ), f32),
            jax.ShapeDtypeStruct((3, len(MIDDLE), NY, NZ), f32),
            jax.ShapeDtypeStruct((6 * LANES, LANES), f32),
            jax.ShapeDtypeStruct((LANES, WINDOWS * LANES), bf16),
            jax.ShapeDtypeStruct((3, len(HALO), NY, NZ), f32),
        ),
        in_specs=[vmem()] * 7,
        out_specs=(vmem(),) * 6,
        scratch_shapes=[
            pltpu.VMEM((TABLE, LANES), f32),
            pltpu.SMEM((8, LANES), jnp.int32),
            pltpu.SemaphoreType.DMA,
        ],
        compiler_params=params(),
        cost_estimate=pl.CostEstimate(
            flops=6_000_000_000, bytes_accessed=8_000_000, transcendentals=0
        ),
    )(*arguments)


def edge_kernel(
    far, near, grid, rows_in, weights_z, stacks,
    step_1, step_2, middle, partial, picks, unforced,
    field, out, ends_1, ends_2, ends_3, table, rows, sems
):
    copies = [pltpu.make_async_copy(rows_in, rows, sems.at[0])]
    copies.append(
        pltpu.make_async_copy(middle, field.at[:, pl.ds(MIDDLE[0], len(MIDDLE))], sems.at[1])
    )
    for i, p in enumerate((0, CX - 2)):
        source, target = ends_3.at[:, pl.ds(2 * i, 2)], field.at[:, pl.ds(p, 2)]
        copies.append(pltpu.make_async_copy(source, target, sems.at[2 + i]))
    copies[0].start()
    copies[1].start()
    odd = lax.axis_index("slab") % 2 == 1

    def cells(p):
        if p < 0:
            return jnp.where(odd, near[p + 2], far[p + 2])
        if p >= CX:
            return jnp.where(odd, far[p - CX], near[p - CX])
        return grid[p]

    def reader(ends, inside, low):
        def load(c, p):
            for i, q in enumerate(low):
                if p == q:
                    return ends[c, i]
            return inside[c, p]

        return load

    planes_2 = (-1, 0, CX - 1, CX)
    for i, p in enumerate(HALO):
        for c in range(3):
            ends_1[c, i] = unforced[c, i] + forcing_of(cells(p), c)
    load_1 = reader(ends_1, step_1, HALO)
    for i, p in enumerate(planes_2):
        for c, value in enumerate(fluid_plane(load_1, cells(p), p)):
            ends_2[c, i] = value
    load_2 = reader(ends_2, step_2, planes_2)
    planes = []
    for i, p in enumerate(EDGES):
        planes.append(fluid_plane(load_2, cells(p), p))
        for c in range(3):
            ends_3[c, i] = planes[-1][c]
    copies[2].start()
    copies[3].start()
    fill_table(table, planes, picks)
    copies[0].wait()

    for device in range(LANES):
        own = slice(device * 6, device * 6 + 6)
        out[own] = partial[own] + window_sums(
            table, rows, device, stacks[device], weights_z, 0
        )
    for copy in copies[1:]:
        copy.wait()


def edge(*arguments):
    return pl.pallas_call(
        edge_kernel,
        out_shape=(
            jax.ShapeDtypeStruct((3, CX, NY, NZ), f32),
            jax.ShapeDtypeStruct((6 * LANES, LANES), f32),
        ),
        in_specs=[vmem()] * 12,
        out_specs=(anywhere(), vmem()),
        scratch_shapes=[
            pltpu.VMEM((3, 4, NY, NZ), f32),
            pltpu.VMEM((3, 4, NY, NZ), f32),
            pltpu.VMEM((3, 4, NY, NZ), f32),
            pltpu.VMEM((TABLE, LANES), f32),
            pltpu.SMEM((8, LANES), jnp.int32),
            pltpu.SemaphoreType.DMA((4,)),
        ],
        compiler_params=params(),
    )(*arguments)


def pick_kernel(returned, back, out):
    chosen = back[...]
    for c in range(3):
        both = jnp.concatenate(
            [returned[pl.ds(3 * slot + c, LANES, stride=6), :] for slot in range(2)], axis=0
        )
        high, middle, low = split_3(both)
        out[c] = dot(chosen, high, NN) + dot(chosen, middle, NN) + dot(chosen, low, NN)


def pick(returned, back):
    return pl.pallas_call(
        pick_kernel,
        out_shape=jax.ShapeDtypeStruct((3, LANES, LANES), f32),
        in_specs=[vmem()] * 2,
        out_specs=vmem(),
        compiler_params=params(),
    )(returned, back)


def exchange(values):
    shape = values.shape
    values = values.reshape(LANES, 1, -1)
    values = lax.all_to_all(values, "slab", split_axis=0, concat_axis=0, tiled=True)
    return values.reshape(shape)


def swap(values, first):
    count = lax.axis_size("slab")
    pairs = []
    for i in range(first, count + first, 2):
        a, b = i % count, (i + 1) % count
        pairs += [(a, b), (b, a)]
    return lax.ppermute(values, "slab", pairs)


def body(velocity, node_coords, node_force, block_slab, block_offset):
    turned_picks = window_picks()
    sent, back = prep(
        jnp.transpose(node_coords, (1, 0, 2)),
        jnp.transpose(node_force, (1, 0, 2)),
        jnp.transpose(block_slab, (1, 0)),
        jnp.transpose(block_offset, (1, 0)),
    )
    got = exchange(sent)
    odd = lax.axis_index("slab") % 2 == 1
    first, last = velocity[:, :SUBSTEPS], velocity[:, CX - SUBSTEPS :]
    cross = swap(jnp.where(odd, last, first), 1)
    same = swap(jnp.where(odd, first, last), 0)
    far, near, grid, rows, weights_z, stacks = spread(got, turned_picks)
    far = swap(far, 1)
    near = swap(near, 0)
    inside = inner(velocity, same, cross, grid, rows, weights_z, stacks)
    field, sums = edge(far, near, grid, rows, weights_z, stacks, *inside)
    node_velocity = pick(exchange(sums), back)
    return field, jnp.transpose(node_velocity, (1, 0, 2))


def solution(mesh):
    return jax.shard_map(
        body,
        mesh=mesh,
        in_specs=(
            P(None, "slab", None, None),
            P("slab", None, None),
            P("slab", None, None),
            P("slab", None),
            P("slab", None),
        ),
        out_specs=(P(None, "slab", None, None), P("slab", None, None)),
        check_vma=False,
    )
```

```python
import jax
import jax.numpy as jnp
from jax import lax
from jax.experimental import pallas as pl
from jax.experimental.pallas import tpu as pltpu
from jax.sharding import PartitionSpec as P

CX = 8
NY = 32
NZ = 128
SUBSTEPS = 3
LANES = 128
WINDOWS = 25
GROUP = 16

time_step = 0.1
viscosity = 0.2

f32 = jnp.float32
bf16 = jnp.bfloat16

COS_TERMS = (
    0.7071067481276141,
    -0.21808909214261787,
    0.011209883548645258,
    -0.0002299265021950359,
    2.3703615380631122e-06,
)

VMEM_LIMIT = 24 * 1024 * 1024
VMEM_ALL = 60 * 1024 * 1024


def vmem():
    return pl.BlockSpec(memory_space=pltpu.VMEM)


def anywhere():
    return pl.BlockSpec(memory_space=pl.ANY)


def params(limit=VMEM_LIMIT):
    return pltpu.CompilerParams(vmem_limit_bytes=limit)


def phi(distance):
    t = jnp.minimum(distance * distance, 4.0)
    total = COS_TERMS[4] * t + COS_TERMS[3]
    for term in (COS_TERMS[2], COS_TERMS[1], COS_TERMS[0]):
        total = total * t + term
    return total * total


def split_2(values):
    high = values.astype(bf16).astype(f32)
    return high, values - high


def split_3(values):
    high = values.astype(bf16)
    rest = values - high.astype(f32)
    middle = rest.astype(bf16)
    low = (rest - middle.astype(f32)).astype(bf16)
    return high, middle, low


def dot(a, b, dims):
    return lax.dot_general(a, b, (dims, ((), ())), preferred_element_type=f32)


NN = ((1,), (0,))
NT = ((1,), (1,))


TABLE = WINDOWS * 96
EDGES = (0, 1, 6, 7)
HALO = (-2, -1, CX, CX + 1)
MIDDLE = (2, 3, 4, 5)
ORDER = EDGES + MIDDLE
SENT = 13
REACH = (CX - 4.0, 5.0, 5.0)


def fill_picks(picks):
    row = lax.broadcasted_iota(jnp.int32, (2 * LANES, LANES), 0)
    lane = lax.broadcasted_iota(jnp.int32, (2 * LANES, LANES), 1)
    apart = row - (lane >> 6) * 128 - ((lane >> 3) & 3) * 32 - (lane & 7)
    for start in range(WINDOWS):
        chosen = jnp.where(apart == start, 1.0, 0.0)
        picks[:, start * LANES : (start + 1) * LANES] = chosen.astype(bf16)


def turned_picks_kernel(turned):
    row = lax.broadcasted_iota(jnp.int32, (LANES, 2 * LANES), 0)
    lane = lax.broadcasted_iota(jnp.int32, (LANES, 2 * LANES), 1)
    apart = lane - ((row >> 3) & 7) * 32 - (row & 7)
    for start in range(WINDOWS):
        chosen = jnp.where(apart == start, 1.0, 0.0)
        turned[start * LANES : (start + 1) * LANES] = chosen.astype(bf16)


def window_picks():
    return pl.pallas_call(
        turned_picks_kernel,
        out_shape=jax.ShapeDtypeStruct((WINDOWS * LANES, 2 * LANES), bf16),
        out_specs=vmem(),
        compiler_params=params(),
        cost_estimate=pl.CostEstimate(
            flops=2_000_000_000, bytes_accessed=4_000_000, transcendentals=0
        ),
    )()


def prep_kernel(coords_in, force_in, slab_in, offset_in, out, back, coords, force, slab, offset, sems):
    copies = [
        pltpu.make_async_copy(source, target, sems.at[i])
        for i, (source, target) in enumerate(
            ((slab_in, slab), (offset_in, offset), (coords_in, coords), (force_in, force))
        )
    ]
    for copy in copies:
        copy.start()
    row = lax.broadcasted_iota(jnp.int32, (LANES, LANES), 0)
    col = lax.broadcasted_iota(jnp.int32, (LANES, LANES), 1)
    before = (row < col).astype(f32).astype(bf16)
    copies[0].wait()
    hot = (jnp.broadcast_to(slab[...], (LANES, LANES)) == row).astype(f32)
    rank = dot(hot.astype(bf16), before, NN)
    first = jnp.where(rank < 0.5, hot, 0.0)
    second = hot - first
    both = jnp.concatenate([first, second], axis=0).astype(bf16)
    copies[1].wait()
    offsets = offset[...].astype(f32)
    rows = lax.broadcasted_iota(jnp.int32, (8, LANES), 0)
    spread_y = jnp.broadcast_to(offsets[0:1], (8, LANES))
    spread_z = jnp.broadcast_to(offsets[1:2], (8, LANES))
    tail = jnp.zeros((LANES, LANES), f32)
    empty = jnp.zeros((LANES - 8, LANES), f32)
    for slot, chosen in ((0, first), (1, second)):
        table = jnp.where(rows == 2 * slot, spread_y, 0.0) + jnp.where(
            rows == 2 * slot + 1, spread_z, 0.0
        )
        table = jnp.concatenate([table, empty], axis=0).astype(bf16)
        tail = tail + dot(chosen.astype(bf16), table, NT)
    out[pl.ds(12, LANES, stride=SENT), :] = tail
    for quantity in range(6):
        if quantity % 3 == 0:
            copies[2 + quantity // 3].wait()
        if quantity < 3:
            source = coords[quantity] * REACH[quantity]
        else:
            source = force[quantity - 3]
        high, middle, low = split_3(source)
        placed = dot(both, high, NN) + dot(both, middle, NN) + dot(both, low, NN)
        for slot in range(2):
            out[pl.ds(slot * 6 + quantity, LANES, stride=SENT), :] = placed[
                slot * LANES : (slot + 1) * LANES
            ]
    back[:, :LANES] = first.T.astype(bf16)
    back[:, LANES:] = second.T.astype(bf16)


def prep(coords, force, slab, offset):
    return pl.pallas_call(
        prep_kernel,
        out_shape=(
            jax.ShapeDtypeStruct((SENT * LANES, LANES), f32),
            jax.ShapeDtypeStruct((LANES, 2 * LANES), bf16),
        ),
        in_specs=[anywhere()] * 4,
        out_specs=(vmem(), vmem()),
        scratch_shapes=[
            pltpu.VMEM((3, LANES, LANES), f32),
            pltpu.VMEM((3, LANES, LANES), f32),
            pltpu.VMEM((1, LANES), jnp.int32),
            pltpu.VMEM((2, LANES), jnp.int32),
            pltpu.SemaphoreType.DMA((4,)),
        ],
        compiler_params=params(VMEM_ALL),
    )(coords, force, slab, offset)


def stack_2(values):
    high, low = split_2(values)
    return jnp.concatenate([high, low], axis=0).astype(bf16)


def joint_stack(weight_x, weight_y):
    return stack_2(jnp.concatenate([weight_x[a : a + 1] * weight_y for a in ORDER], axis=0))


def spread_pair(load, stack):
    turned = stack.T
    out = dot(load, jnp.concatenate([turned, turned], axis=0), NN)
    return jnp.concatenate([out[:24, :LANES], out[24:, LANES:]], axis=0)


def gather_windows(total, rows, parts, index):
    for sub in range(GROUP):
        for slot in range(2):
            row = rows[slot, index * GROUP + sub]
            for c in range(3):
                start = slot * 24 + c * 8
                total[pl.ds(row + 32 * c, 8), :] += parts[sub, start : start + 8]


def spread_planes(total, turned_picks):
    cells = jnp.zeros((192, 2 * LANES), f32)
    for y in range(0, WINDOWS, 2):
        wide = min(2, WINDOWS - y)
        both = [total[(y + i) * 96 : (y + i + 1) * 96] for i in range(wide)]
        both = both[0] if wide == 1 else jnp.concatenate(both, axis=1)
        chosen = turned_picks[y * LANES : (y + wide) * LANES]
        cells = cells + dot(stack_2(both), chosen, NN)
    cells = (cells[:96] + cells[96:]) * time_step
    cells = jnp.concatenate([cells, jnp.zeros((32, 2 * LANES), f32)], axis=0).T
    return {p: cells[i * NY : (i + 1) * NY] for i, p in enumerate(ORDER)}


def pack_planes(planes):
    rows = jnp.concatenate(planes, axis=0)
    rest = rows[48:]
    moved = jnp.concatenate([pltpu.roll(rest, shift, 1) for shift in (96, 64, 32)], axis=0)
    lane = lax.broadcasted_iota(jnp.int32, (48, LANES), 1)
    return jnp.where(lane < 96, rows[:48], moved)


def unpack_planes(packed):
    lane = lax.broadcasted_iota(jnp.int32, (16, LANES), 1)
    parts = [pltpu.roll(packed[16 * i : 16 * i + 16], 32 * i + 32, 1) for i in range(3)]
    rest = jnp.where(lane < 32, parts[0], jnp.where(lane < 64, parts[1], parts[2]))
    rows = jnp.concatenate([packed, rest], axis=0)
    return rows[:NY], rows[NY:]


def spread_kernel(
    got, turned_picks, far, near, grid, rows_out, weights_z, stacks, total, parts, rows, sem
):
    tail = got[pl.ds(12, LANES, stride=SENT), :].T
    y = jnp.concatenate([tail[0:1], tail[2:3]], axis=0)
    z = jnp.concatenate([tail[1:2], tail[3:4]], axis=0)
    y = jnp.clip(y - 1.0, 0.0, WINDOWS - 1.0)
    z = jnp.clip(z - 1.0, 0.0, WINDOWS - 1.0)
    start = (y * 96.0 + z).astype(jnp.int32)
    rows_out[...] = jnp.concatenate([start, jnp.zeros((6, LANES), jnp.int32)], axis=0)
    copy = pltpu.make_async_copy(rows_out, rows, sem)
    copy.start()
    total[...] = jnp.zeros_like(total)
    taps = lax.broadcasted_iota(jnp.int32, (8, LANES), 0).astype(f32) - 1.0

    def compute(index):
        for sub in range(GROUP):
            device = index * GROUP + sub
            load, stack = [], []
            for slot in range(2):
                source = device * SENT + slot * 6
                weight_x, weight_y, weight_z = [
                    phi(taps - got[pl.ds(source + dim, 1), :]) for dim in range(3)
                ]
                weights_z[device, slot] = weight_z
                stack.append(joint_stack(weight_x, weight_y))
                load += [got[pl.ds(source + 3 + c, 1), :] * weight_z for c in range(3)]
            load = jnp.concatenate(split_2(jnp.concatenate(load, axis=0)), axis=1).astype(bf16)
            stack = jnp.concatenate(stack, axis=0)
            stacks[device] = stack
            parts[sub] = spread_pair(load, stack)

    compute(0)
    copy.wait()
    for index in range(1, LANES // GROUP):
        gather_windows(total, rows, parts, index - 1)
        compute(index)
    gather_windows(total, rows, parts, LANES // GROUP - 1)
    planes = spread_planes(total, turned_picks)
    odd = lax.axis_index("slab") % 2 == 1
    for a in range(CX):
        grid[a] = planes[a]
    first = pack_planes([planes[0], planes[1]])
    last = pack_planes([planes[CX - 2], planes[CX - 1]])
    near[...] = jnp.where(odd, first, last)
    far[...] = jnp.where(odd, last, first)


def spread(got, turned_picks):
    return pl.pallas_call(
        spread_kernel,
        out_shape=(
            jax.ShapeDtypeStruct((48, LANES), f32),
            jax.ShapeDtypeStruct((48, LANES), f32),
            jax.ShapeDtypeStruct((CX, NY, LANES), f32),
            jax.ShapeDtypeStruct((8, LANES), jnp.int32),
            jax.ShapeDtypeStruct((LANES, 2, 8, LANES), f32),
            jax.ShapeDtypeStruct((LANES, 256, LANES), bf16),
        ),
        in_specs=[vmem()] * 2,
        out_specs=(vmem(),) * 6,
        scratch_shapes=[
            pltpu.VMEM((TABLE, LANES), f32),
            pltpu.VMEM((GROUP, 48, LANES), f32),
            pltpu.SMEM((8, LANES), jnp.int32),
            pltpu.SemaphoreType.DMA,
        ],
        compiler_params=params(),
    )(got, turned_picks)


def forcing_of(cells, c):
    lane = lax.broadcasted_iota(jnp.int32, (NY, NZ), 1)
    if c:
        cells = pltpu.roll(cells, LANES - 32 * c, 1)
    return jnp.where(lane < 32, cells, 0.0)


def fluid_plane(load, cells, p):
    centers = [load(c, p) for c in range(3)]
    results = []
    for c in range(3):
        center = centers[c]
        x_plus, x_minus = load(c, p + 1), load(c, p - 1)
        y_plus, y_minus = pltpu.roll(center, NY - 1, 0), pltpu.roll(center, 1, 0)
        z_plus, z_minus = pltpu.roll(center, NZ - 1, 1), pltpu.roll(center, 1, 1)
        around = (x_plus + x_minus) + (y_plus + y_minus) + (z_plus + z_minus)
        advect = (
            centers[0] * (x_plus - x_minus)
            + centers[1] * (y_plus - y_minus)
            + centers[2] * (z_plus - z_minus)
        )
        moved = (
            (1.0 - 6.0 * time_step * viscosity) * center
            + (time_step * viscosity) * around
            - (0.5 * time_step) * advect
        )
        results.append(moved if cells is None else moved + forcing_of(cells, c))
    return results


def packed_plane(parts):
    lane = lax.broadcasted_iota(jnp.int32, (NY, LANES), 1)
    cells = jnp.where(lane < 32, parts[0], 0.0)
    for c in (1, 2):
        moved = pltpu.roll(parts[c], 32 * c, 1)
        cells = jnp.where((lane >= 32 * c) & (lane < 32 * c + 32), moved, cells)
    return cells


def fill_table(table, planes, picks):
    cells = jnp.concatenate([packed_plane(parts) for parts in planes], axis=0).T[:96]
    split = jnp.concatenate(split_2(cells), axis=1).astype(bf16)
    for y in range(0, WINDOWS, 2):
        wide = min(2, WINDOWS - y)
        both = dot(split, picks[:, y * LANES : (y + wide) * LANES], NN)
        for i in range(wide):
            table[(y + i) * 96 : (y + i + 1) * 96] = both[:, i * LANES : (i + 1) * LANES]


def fold(a, b, width):
    if b is None:
        return a + pltpu.roll(a, width, 0)
    bit = (lax.broadcasted_iota(jnp.int32, (8, LANES), 0) & width) == 0
    return jnp.where(bit, a, b) + pltpu.roll(jnp.where(bit, b, a), width, 0)


def window_sums(table, rows, device, stack, weights_z, first):
    cells = []
    for slot in range(2):
        row = rows[slot, device]
        for c in range(3):
            cells.append(table[pl.ds(row + 32 * c, 8), :])
    high = jnp.concatenate([stack[first : first + 32], stack[128 + first : 160 + first]], axis=1)
    low = jnp.concatenate([stack[64 + first : 96 + first], stack[192 + first : 224 + first]], axis=1)
    both = jnp.concatenate([high, low, high, low], axis=0)
    values = dot(jnp.concatenate(cells, axis=0).astype(bf16), both, NN)
    v = []
    for slot in range(2):
        weight_z = weights_z[device, slot]
        for c in range(3):
            start = slot * 24 + c * 8
            v.append(values[start : start + 8, slot * LANES : (slot + 1) * LANES] * weight_z)
    low = fold(fold(v[0], v[1], 1), fold(v[2], v[3], 1), 2)
    high = fold(fold(v[4], v[5], 1), None, 2)
    return fold(low, high, 4)[:6]


def halo_reader(inside, same, cross, depth):
    odd = lax.axis_index("slab") % 2 == 1

    def load(c, p):
        if p < 0:
            return jnp.where(odd, same[c, p + depth], cross[c, p + depth])
        if p >= CX:
            return jnp.where(odd, cross[c, p - CX], same[c, p - CX])
        return inside[c, p]

    return load


def inner_kernel(
    velocity, same, cross, grid, rows_in, weights_z, stacks,
    step_1, step_2, middle, partial, picks, unforced, table, rows, sem
):
    copy = pltpu.make_async_copy(rows_in, rows, sem)
    copy.start()
    fill_picks(picks)
    load_0 = halo_reader(velocity, same, cross, SUBSTEPS)
    for i, p in enumerate(HALO):
        for c, value in enumerate(fluid_plane(load_0, None, p)):
            unforced[c, i] = value
    for p in range(CX):
        for c, value in enumerate(fluid_plane(load_0, grid[p], p)):
            step_1[c, p] = value
    for p in range(1, CX - 1):
        for c, value in enumerate(fluid_plane(lambda c, p: step_1[c, p], grid[p], p)):
            step_2[c, p] = value
    planes = []
    for p in MIDDLE:
        planes.append(fluid_plane(lambda c, p: step_2[c, p], grid[p], p))
        for c in range(3):
            middle[c, p - MIDDLE[0]] = planes[-1][c]
    fill_table(table, planes, picks)
    copy.wait()

    for device in range(LANES):
        partial[device * 6 : device * 6 + 6] = window_sums(
            table, rows, device, stacks[device], weights_z, 32
        )


def inner(*arguments):
    return pl.pallas_call(
        inner_kernel,
        out_shape=(
            jax.ShapeDtypeStruct((3, CX, NY, NZ), f32),
            jax.ShapeDtypeStruct((3, CX, NY, NZ), f32),
            jax.ShapeDtypeStruct((3, len(MIDDLE), NY, NZ), f32),
            jax.ShapeDtypeStruct((6 * LANES, LANES), f32),
            jax.ShapeDtypeStruct((2 * LANES, WINDOWS * LANES), bf16),
            jax.ShapeDtypeStruct((3, len(HALO), NY, NZ), f32),
        ),
        in_specs=[vmem()] * 7,
        out_specs=(vmem(),) * 6,
        scratch_shapes=[
            pltpu.VMEM((TABLE, LANES), f32),
            pltpu.SMEM((8, LANES), jnp.int32),
            pltpu.SemaphoreType.DMA,
        ],
        compiler_params=params(),
        cost_estimate=pl.CostEstimate(
            flops=6_000_000_000, bytes_accessed=8_000_000, transcendentals=0
        ),
    )(*arguments)


def edge_kernel(
    far, near, grid, rows_in, weights_z, stacks,
    step_1, step_2, middle, partial, picks, unforced,
    field, out, ends_1, ends_2, ends_3, table, rows, sems
):
    copies = [pltpu.make_async_copy(rows_in, rows, sems.at[0])]
    copies.append(
        pltpu.make_async_copy(middle, field.at[:, pl.ds(MIDDLE[0], len(MIDDLE))], sems.at[1])
    )
    for i, p in enumerate((0, CX - 2)):
        source, target = ends_3.at[:, pl.ds(2 * i, 2)], field.at[:, pl.ds(p, 2)]
        copies.append(pltpu.make_async_copy(source, target, sems.at[2 + i]))
    copies[0].start()
    copies[1].start()
    odd = lax.axis_index("slab") % 2 == 1

    behind = unpack_planes(jnp.where(odd, near[...], far[...]))
    ahead = unpack_planes(jnp.where(odd, far[...], near[...]))

    def cells(p):
        if p < 0:
            return behind[p + 2]
        if p >= CX:
            return ahead[p - CX]
        return grid[p]

    def reader(ends, inside, low):
        def load(c, p):
            for i, q in enumerate(low):
                if p == q:
                    return ends[c, i]
            return inside[c, p]

        return load

    planes_2 = (-1, 0, CX - 1, CX)
    for i, p in enumerate(HALO):
        for c in range(3):
            ends_1[c, i] = unforced[c, i] + forcing_of(cells(p), c)
    load_1 = reader(ends_1, step_1, HALO)
    for i, p in enumerate(planes_2):
        for c, value in enumerate(fluid_plane(load_1, cells(p), p)):
            ends_2[c, i] = value
    load_2 = reader(ends_2, step_2, planes_2)
    planes = []
    for i, p in enumerate(EDGES):
        planes.append(fluid_plane(load_2, cells(p), p))
        for c in range(3):
            ends_3[c, i] = planes[-1][c]
    copies[2].start()
    copies[3].start()
    fill_table(table, planes, picks)
    copies[0].wait()

    for device in range(LANES):
        own = slice(device * 6, device * 6 + 6)
        out[own] = partial[own] + window_sums(
            table, rows, device, stacks[device], weights_z, 0
        )
    for copy in copies[1:]:
        copy.wait()


def edge(*arguments):
    return pl.pallas_call(
        edge_kernel,
        out_shape=(
            jax.ShapeDtypeStruct((3, CX, NY, NZ), f32),
            jax.ShapeDtypeStruct((6 * LANES, LANES), f32),
        ),
        in_specs=[vmem()] * 12,
        out_specs=(anywhere(), vmem()),
        scratch_shapes=[
            pltpu.VMEM((3, 4, NY, NZ), f32),
            pltpu.VMEM((3, 4, NY, NZ), f32),
            pltpu.VMEM((3, 4, NY, NZ), f32),
            pltpu.VMEM((TABLE, LANES), f32),
            pltpu.SMEM((8, LANES), jnp.int32),
            pltpu.SemaphoreType.DMA((4,)),
        ],
        compiler_params=params(),
    )(*arguments)


def pick_kernel(returned, back, out):
    chosen = back[...]
    for c in range(3):
        both = jnp.concatenate(
            [returned[pl.ds(3 * slot + c, LANES, stride=6), :] for slot in range(2)], axis=0
        )
        high, middle, low = split_3(both)
        out[c] = dot(chosen, high, NN) + dot(chosen, middle, NN) + dot(chosen, low, NN)


def pick(returned, back):
    return pl.pallas_call(
        pick_kernel,
        out_shape=jax.ShapeDtypeStruct((3, LANES, LANES), f32),
        in_specs=[vmem()] * 2,
        out_specs=vmem(),
        compiler_params=params(),
    )(returned, back)


def exchange(values):
    shape = values.shape
    values = values.reshape(LANES, 1, -1)
    values = lax.all_to_all(values, "slab", split_axis=0, concat_axis=0, tiled=True)
    return values.reshape(shape)


def swap(values, first):
    count = lax.axis_size("slab")
    pairs = []
    for i in range(first, count + first, 2):
        a, b = i % count, (i + 1) % count
        pairs += [(a, b), (b, a)]
    return lax.ppermute(values, "slab", pairs)


def body(velocity, node_coords, node_force, block_slab, block_offset):
    turned_picks = window_picks()
    sent, back = prep(
        jnp.transpose(node_coords, (1, 0, 2)),
        jnp.transpose(node_force, (1, 0, 2)),
        jnp.transpose(block_slab, (1, 0)),
        jnp.transpose(block_offset, (1, 0)),
    )
    got = exchange(sent)
    odd = lax.axis_index("slab") % 2 == 1
    first, last = velocity[:, :SUBSTEPS], velocity[:, CX - SUBSTEPS :]
    cross = swap(jnp.where(odd, last, first), 1)
    same = swap(jnp.where(odd, first, last), 0)
    far, near, grid, rows, weights_z, stacks = spread(got, turned_picks)
    far = swap(far, 1)
    near = swap(near, 0)
    inside = inner(velocity, same, cross, grid, rows, weights_z, stacks)
    field, sums = edge(far, near, grid, rows, weights_z, stacks, *inside)
    node_velocity = pick(exchange(sums), back)
    return field, jnp.transpose(node_velocity, (1, 0, 2))


def solution(mesh):
    return jax.shard_map(
        body,
        mesh=mesh,
        in_specs=(
            P(None, "slab", None, None),
            P("slab", None, None),
            P("slab", None, None),
            P("slab", None),
            P("slab", None),
        ),
        out_specs=(P(None, "slab", None, None), P("slab", None, None)),
        check_vma=False,
    )
```

```python
import jax
import jax.numpy as jnp
from jax import lax
from jax.experimental import pallas as pl
from jax.experimental.pallas import tpu as pltpu
from jax.sharding import PartitionSpec as P

CX = 8
NY = 32
NZ = 128
SUBSTEPS = 3
LANES = 128
WINDOWS = 25
GROUP = 16

time_step = 0.1
viscosity = 0.2

f32 = jnp.float32
bf16 = jnp.bfloat16

COS_TERMS = (
    0.7071067481276141,
    -0.21808909214261787,
    0.011209883548645258,
    -0.0002299265021950359,
    2.3703615380631122e-06,
)

VMEM_LIMIT = 24 * 1024 * 1024
VMEM_ALL = 60 * 1024 * 1024


def vmem():
    return pl.BlockSpec(memory_space=pltpu.VMEM)


def anywhere():
    return pl.BlockSpec(memory_space=pl.ANY)


def params(limit=VMEM_LIMIT):
    return pltpu.CompilerParams(vmem_limit_bytes=limit)


def phi(distance):
    t = jnp.minimum(distance * distance, 4.0)
    total = COS_TERMS[4] * t + COS_TERMS[3]
    for term in (COS_TERMS[2], COS_TERMS[1], COS_TERMS[0]):
        total = total * t + term
    return total * total


def split_2(values):
    high = values.astype(bf16).astype(f32)
    return high, values - high


def split_3(values):
    high = values.astype(bf16)
    rest = values - high.astype(f32)
    middle = rest.astype(bf16)
    low = (rest - middle.astype(f32)).astype(bf16)
    return high, middle, low


def dot(a, b, dims):
    return lax.dot_general(a, b, (dims, ((), ())), preferred_element_type=f32)


NN = ((1,), (0,))
NT = ((1,), (1,))


TABLE = WINDOWS * 96
EDGES = (0, 1, 6, 7)
HALO = (-2, -1, CX, CX + 1)
MIDDLE = (2, 3, 4, 5)
ORDER = EDGES + MIDDLE
SENT = 12
REACH = (CX - 4.0, 5.0, 5.0)


def fill_picks(picks):
    row = lax.broadcasted_iota(jnp.int32, (2 * LANES, LANES), 0)
    lane = lax.broadcasted_iota(jnp.int32, (2 * LANES, LANES), 1)
    apart = row - (lane >> 6) * 128 - ((lane >> 3) & 3) * 32 - (lane & 7)
    for start in range(WINDOWS):
        chosen = jnp.where(apart == start, 1.0, 0.0)
        picks[:, start * LANES : (start + 1) * LANES] = chosen.astype(bf16)


def turned_picks_kernel(turned):
    row = lax.broadcasted_iota(jnp.int32, (LANES, 2 * LANES), 0)
    lane = lax.broadcasted_iota(jnp.int32, (LANES, 2 * LANES), 1)
    apart = lane - ((row >> 3) & 7) * 32 - (row & 7)
    for start in range(WINDOWS):
        chosen = jnp.where(apart == start, 1.0, 0.0)
        turned[start * LANES : (start + 1) * LANES] = chosen.astype(bf16)


def window_picks():
    return pl.pallas_call(
        turned_picks_kernel,
        out_shape=jax.ShapeDtypeStruct((WINDOWS * LANES, 2 * LANES), bf16),
        out_specs=vmem(),
        compiler_params=params(),
        cost_estimate=pl.CostEstimate(
            flops=2_000_000_000, bytes_accessed=4_000_000, transcendentals=0
        ),
    )()


def prep_kernel(coords_in, force_in, slab_in, offset_in, out, back, coords, force, slab, offset, sems):
    copies = [
        pltpu.make_async_copy(source, target, sems.at[i])
        for i, (source, target) in enumerate(
            ((slab_in, slab), (offset_in, offset), (coords_in, coords), (force_in, force))
        )
    ]
    for copy in copies:
        copy.start()
    row = lax.broadcasted_iota(jnp.int32, (LANES, LANES), 0)
    col = lax.broadcasted_iota(jnp.int32, (LANES, LANES), 1)
    before = (row < col).astype(f32).astype(bf16)
    copies[0].wait()
    hot = (jnp.broadcast_to(slab[...], (LANES, LANES)) == row).astype(f32)
    rank = dot(hot.astype(bf16), before, NN)
    first = jnp.where(rank < 0.5, hot, 0.0)
    second = hot - first
    both = jnp.concatenate([first, second], axis=0).astype(bf16)
    copies[1].wait()
    offsets = offset[...].astype(f32)
    corners = [None] + [
        jnp.broadcast_to(offsets[i : i + 1], (LANES, LANES)).T for i in range(2)
    ]
    for quantity in range(6):
        if quantity % 3 == 0:
            copies[2 + quantity // 3].wait()
        if quantity < 3:
            source = coords[quantity] * REACH[quantity]
            if quantity:
                source = source + corners[quantity]
        else:
            source = force[quantity - 3]
        high, middle, low = split_3(source)
        placed = dot(both, high, NN) + dot(both, middle, NN) + dot(both, low, NN)
        for slot in range(2):
            out[pl.ds(slot * 6 + quantity, LANES, stride=SENT), :] = placed[
                slot * LANES : (slot + 1) * LANES
            ]
    back[:, :LANES] = first.T.astype(bf16)
    back[:, LANES:] = second.T.astype(bf16)


def prep(coords, force, slab, offset):
    return pl.pallas_call(
        prep_kernel,
        out_shape=(
            jax.ShapeDtypeStruct((SENT * LANES, LANES), f32),
            jax.ShapeDtypeStruct((LANES, 2 * LANES), bf16),
        ),
        in_specs=[anywhere()] * 4,
        out_specs=(vmem(), vmem()),
        scratch_shapes=[
            pltpu.VMEM((3, LANES, LANES), f32),
            pltpu.VMEM((3, LANES, LANES), f32),
            pltpu.VMEM((1, LANES), jnp.int32),
            pltpu.VMEM((2, LANES), jnp.int32),
            pltpu.SemaphoreType.DMA((4,)),
        ],
        compiler_params=params(VMEM_ALL),
    )(coords, force, slab, offset)


def stack_2(values):
    high, low = split_2(values)
    return jnp.concatenate([high, low], axis=0).astype(bf16)


def joint_stack(weight_x, weight_y):
    return stack_2(jnp.concatenate([weight_x[a : a + 1] * weight_y for a in ORDER], axis=0))


def spread_pair(load, stack):
    turned = stack.T
    out = dot(load, jnp.concatenate([turned, turned], axis=0), NN)
    return jnp.concatenate([out[:24, :LANES], out[24:, LANES:]], axis=0)


def gather_windows(total, rows, parts, index):
    for sub in range(GROUP):
        for slot in range(2):
            row = rows[slot, index * GROUP + sub]
            for c in range(3):
                start = slot * 24 + c * 8
                total[pl.ds(row + 32 * c, 8), :] += parts[sub, start : start + 8]


def spread_planes(total, turned_picks):
    cells = jnp.zeros((192, 2 * LANES), f32)
    for y in range(0, WINDOWS, 2):
        wide = min(2, WINDOWS - y)
        both = [total[(y + i) * 96 : (y + i + 1) * 96] for i in range(wide)]
        both = both[0] if wide == 1 else jnp.concatenate(both, axis=1)
        chosen = turned_picks[y * LANES : (y + wide) * LANES]
        cells = cells + dot(stack_2(both), chosen, NN)
    cells = (cells[:96] + cells[96:]) * time_step
    cells = jnp.concatenate([cells, jnp.zeros((32, 2 * LANES), f32)], axis=0).T
    return {p: cells[i * NY : (i + 1) * NY] for i, p in enumerate(ORDER)}


def pack_planes(planes):
    rows = jnp.concatenate(planes, axis=0)
    rest = rows[48:]
    moved = jnp.concatenate([pltpu.roll(rest, shift, 1) for shift in (96, 64, 32)], axis=0)
    lane = lax.broadcasted_iota(jnp.int32, (48, LANES), 1)
    return jnp.where(lane < 96, rows[:48], moved)


def unpack_planes(packed):
    lane = lax.broadcasted_iota(jnp.int32, (16, LANES), 1)
    parts = [pltpu.roll(packed[16 * i : 16 * i + 16], 32 * i + 32, 1) for i in range(3)]
    rest = jnp.where(lane < 32, parts[0], jnp.where(lane < 64, parts[1], parts[2]))
    rows = jnp.concatenate([packed, rest], axis=0)
    return rows[:NY], rows[NY:]


def spread_kernel(
    got, turned_picks, far, near, grid, rows_out, weights_z, stacks, total, places, parts, rows, sem
):
    lane = lax.broadcasted_iota(jnp.int32, (LANES, LANES), 1)
    start = jnp.zeros((LANES, LANES), f32)
    for slot in range(2):
        firsts = []
        for dim in (1, 2):
            place = got[pl.ds(slot * 6 + dim, LANES, stride=SENT), :]
            least = jnp.floor(jnp.min(place, axis=1, keepdims=True)) - 1.0
            firsts.append(jnp.clip(least, 0.0, WINDOWS - 1.0))
            places[slot * 2 + dim - 1] = place - firsts[-1]
        start = jnp.where(lane == slot, firsts[0] * 96.0 + firsts[1], start)
    rows_out[...] = start.T[:8].astype(jnp.int32)
    copy = pltpu.make_async_copy(rows_out, rows, sem)
    copy.start()
    total[...] = jnp.zeros_like(total)
    taps = lax.broadcasted_iota(jnp.int32, (8, LANES), 0).astype(f32)

    def compute(index):
        for sub in range(GROUP):
            device = index * GROUP + sub
            load, stack = [], []
            for slot in range(2):
                source = device * SENT + slot * 6
                weight_x = phi(taps - 1.0 - got[pl.ds(source, 1), :])
                weight_y = phi(taps - places[slot * 2, pl.ds(device, 1), :])
                weight_z = phi(taps - places[slot * 2 + 1, pl.ds(device, 1), :])
                weights_z[device, slot] = weight_z
                stack.append(joint_stack(weight_x, weight_y))
                load += [got[pl.ds(source + 3 + c, 1), :] * weight_z for c in range(3)]
            load = jnp.concatenate(split_2(jnp.concatenate(load, axis=0)), axis=1).astype(bf16)
            stack = jnp.concatenate(stack, axis=0)
            stacks[device] = stack
            parts[sub] = spread_pair(load, stack)

    compute(0)
    copy.wait()
    for index in range(1, LANES // GROUP):
        gather_windows(total, rows, parts, index - 1)
        compute(index)
    gather_windows(total, rows, parts, LANES // GROUP - 1)
    planes = spread_planes(total, turned_picks)
    odd = lax.axis_index("slab") % 2 == 1
    for a in range(CX):
        grid[a] = planes[a]
    first = pack_planes([planes[0], planes[1]])
    last = pack_planes([planes[CX - 2], planes[CX - 1]])
    near[...] = jnp.where(odd, first, last)
    far[...] = jnp.where(odd, last, first)


def spread(got, turned_picks):
    return pl.pallas_call(
        spread_kernel,
        out_shape=(
            jax.ShapeDtypeStruct((48, LANES), f32),
            jax.ShapeDtypeStruct((48, LANES), f32),
            jax.ShapeDtypeStruct((CX, NY, LANES), f32),
            jax.ShapeDtypeStruct((8, LANES), jnp.int32),
            jax.ShapeDtypeStruct((LANES, 2, 8, LANES), f32),
            jax.ShapeDtypeStruct((LANES, 256, LANES), bf16),
        ),
        in_specs=[vmem()] * 2,
        out_specs=(vmem(),) * 6,
        scratch_shapes=[
            pltpu.VMEM((TABLE, LANES), f32),
            pltpu.VMEM((4, LANES, LANES), f32),
            pltpu.VMEM((GROUP, 48, LANES), f32),
            pltpu.SMEM((8, LANES), jnp.int32),
            pltpu.SemaphoreType.DMA,
        ],
        compiler_params=params(),
    )(got, turned_picks)


def forcing_of(cells, c):
    lane = lax.broadcasted_iota(jnp.int32, (NY, NZ), 1)
    if c:
        cells = pltpu.roll(cells, LANES - 32 * c, 1)
    return jnp.where(lane < 32, cells, 0.0)


def fluid_plane(load, cells, p):
    centers = [load(c, p) for c in range(3)]
    results = []
    for c in range(3):
        center = centers[c]
        x_plus, x_minus = load(c, p + 1), load(c, p - 1)
        y_plus, y_minus = pltpu.roll(center, NY - 1, 0), pltpu.roll(center, 1, 0)
        z_plus, z_minus = pltpu.roll(center, NZ - 1, 1), pltpu.roll(center, 1, 1)
        around = (x_plus + x_minus) + (y_plus + y_minus) + (z_plus + z_minus)
        advect = (
            centers[0] * (x_plus - x_minus)
            + centers[1] * (y_plus - y_minus)
            + centers[2] * (z_plus - z_minus)
        )
        moved = (
            (1.0 - 6.0 * time_step * viscosity) * center
            + (time_step * viscosity) * around
            - (0.5 * time_step) * advect
        )
        results.append(moved if cells is None else moved + forcing_of(cells, c))
    return results


def packed_plane(parts):
    lane = lax.broadcasted_iota(jnp.int32, (NY, LANES), 1)
    cells = jnp.where(lane < 32, parts[0], 0.0)
    for c in (1, 2):
        moved = pltpu.roll(parts[c], 32 * c, 1)
        cells = jnp.where((lane >= 32 * c) & (lane < 32 * c + 32), moved, cells)
    return cells


def fill_table(table, planes, picks):
    cells = jnp.concatenate([packed_plane(parts) for parts in planes], axis=0).T[:96]
    split = jnp.concatenate(split_2(cells), axis=1).astype(bf16)
    for y in range(0, WINDOWS, 2):
        wide = min(2, WINDOWS - y)
        both = dot(split, picks[:, y * LANES : (y + wide) * LANES], NN)
        for i in range(wide):
            table[(y + i) * 96 : (y + i + 1) * 96] = both[:, i * LANES : (i + 1) * LANES]


def fold(a, b, width):
    if b is None:
        return a + pltpu.roll(a, width, 0)
    bit = (lax.broadcasted_iota(jnp.int32, (8, LANES), 0) & width) == 0
    return jnp.where(bit, a, b) + pltpu.roll(jnp.where(bit, b, a), width, 0)


def window_sums(table, rows, device, stack, weights_z, first):
    cells = []
    for slot in range(2):
        row = rows[slot, device]
        for c in range(3):
            cells.append(table[pl.ds(row + 32 * c, 8), :])
    high = jnp.concatenate([stack[first : first + 32], stack[128 + first : 160 + first]], axis=1)
    low = jnp.concatenate([stack[64 + first : 96 + first], stack[192 + first : 224 + first]], axis=1)
    both = jnp.concatenate([high, low, high, low], axis=0)
    values = dot(jnp.concatenate(cells, axis=0).astype(bf16), both, NN)
    v = []
    for slot in range(2):
        weight_z = weights_z[device, slot]
        for c in range(3):
            start = slot * 24 + c * 8
            v.append(values[start : start + 8, slot * LANES : (slot + 1) * LANES] * weight_z)
    low = fold(fold(v[0], v[1], 1), fold(v[2], v[3], 1), 2)
    high = fold(fold(v[4], v[5], 1), None, 2)
    return fold(low, high, 4)[:6]


def halo_reader(inside, same, cross, depth):
    odd = lax.axis_index("slab") % 2 == 1

    def load(c, p):
        if p < 0:
            return jnp.where(odd, same[c, p + depth], cross[c, p + depth])
        if p >= CX:
            return jnp.where(odd, cross[c, p - CX], same[c, p - CX])
        return inside[c, p]

    return load


def inner_kernel(
    velocity, same, cross, grid, rows_in, weights_z, stacks,
    step_1, step_2, middle, partial, picks, unforced, table, rows, sem
):
    copy = pltpu.make_async_copy(rows_in, rows, sem)
    copy.start()
    fill_picks(picks)
    load_0 = halo_reader(velocity, same, cross, SUBSTEPS)
    for i, p in enumerate(HALO):
        for c, value in enumerate(fluid_plane(load_0, None, p)):
            unforced[c, i] = value
    for p in range(CX):
        for c, value in enumerate(fluid_plane(load_0, grid[p], p)):
            step_1[c, p] = value
    for p in range(1, CX - 1):
        for c, value in enumerate(fluid_plane(lambda c, p: step_1[c, p], grid[p], p)):
            step_2[c, p] = value
    planes = []
    for p in MIDDLE:
        planes.append(fluid_plane(lambda c, p: step_2[c, p], grid[p], p))
        for c in range(3):
            middle[c, p - MIDDLE[0]] = planes[-1][c]
    fill_table(table, planes, picks)
    copy.wait()

    for device in range(LANES):
        partial[device * 6 : device * 6 + 6] = window_sums(
            table, rows, device, stacks[device], weights_z, 32
        )


def inner(*arguments):
    return pl.pallas_call(
        inner_kernel,
        out_shape=(
            jax.ShapeDtypeStruct((3, CX, NY, NZ), f32),
            jax.ShapeDtypeStruct((3, CX, NY, NZ), f32),
            jax.ShapeDtypeStruct((3, len(MIDDLE), NY, NZ), f32),
            jax.ShapeDtypeStruct((6 * LANES, LANES), f32),
            jax.ShapeDtypeStruct((2 * LANES, WINDOWS * LANES), bf16),
            jax.ShapeDtypeStruct((3, len(HALO), NY, NZ), f32),
        ),
        in_specs=[vmem()] * 7,
        out_specs=(vmem(),) * 6,
        scratch_shapes=[
            pltpu.VMEM((TABLE, LANES), f32),
            pltpu.SMEM((8, LANES), jnp.int32),
            pltpu.SemaphoreType.DMA,
        ],
        compiler_params=params(),
        cost_estimate=pl.CostEstimate(
            flops=6_000_000_000, bytes_accessed=8_000_000, transcendentals=0
        ),
    )(*arguments)


def edge_kernel(
    far, near, grid, rows_in, weights_z, stacks,
    step_1, step_2, middle, partial, picks, unforced,
    field, out, ends_1, ends_2, ends_3, table, rows, sems
):
    copies = [pltpu.make_async_copy(rows_in, rows, sems.at[0])]
    copies.append(
        pltpu.make_async_copy(middle, field.at[:, pl.ds(MIDDLE[0], len(MIDDLE))], sems.at[1])
    )
    for i, p in enumerate((0, CX - 2)):
        source, target = ends_3.at[:, pl.ds(2 * i, 2)], field.at[:, pl.ds(p, 2)]
        copies.append(pltpu.make_async_copy(source, target, sems.at[2 + i]))
    copies[0].start()
    copies[1].start()
    odd = lax.axis_index("slab") % 2 == 1

    behind = unpack_planes(jnp.where(odd, near[...], far[...]))
    ahead = unpack_planes(jnp.where(odd, far[...], near[...]))

    def cells(p):
        if p < 0:
            return behind[p + 2]
        if p >= CX:
            return ahead[p - CX]
        return grid[p]

    def reader(ends, inside, low):
        def load(c, p):
            for i, q in enumerate(low):
                if p == q:
                    return ends[c, i]
            return inside[c, p]

        return load

    planes_2 = (-1, 0, CX - 1, CX)
    for i, p in enumerate(HALO):
        for c in range(3):
            ends_1[c, i] = unforced[c, i] + forcing_of(cells(p), c)
    load_1 = reader(ends_1, step_1, HALO)
    for i, p in enumerate(planes_2):
        for c, value in enumerate(fluid_plane(load_1, cells(p), p)):
            ends_2[c, i] = value
    load_2 = reader(ends_2, step_2, planes_2)
    planes = []
    for i, p in enumerate(EDGES):
        planes.append(fluid_plane(load_2, cells(p), p))
        for c in range(3):
            ends_3[c, i] = planes[-1][c]
    copies[2].start()
    copies[3].start()
    fill_table(table, planes, picks)
    copies[0].wait()

    for device in range(LANES):
        own = slice(device * 6, device * 6 + 6)
        out[own] = partial[own] + window_sums(
            table, rows, device, stacks[device], weights_z, 0
        )
    for copy in copies[1:]:
        copy.wait()


def edge(*arguments):
    return pl.pallas_call(
        edge_kernel,
        out_shape=(
            jax.ShapeDtypeStruct((3, CX, NY, NZ), f32),
            jax.ShapeDtypeStruct((6 * LANES, LANES), f32),
        ),
        in_specs=[vmem()] * 12,
        out_specs=(anywhere(), vmem()),
        scratch_shapes=[
            pltpu.VMEM((3, 4, NY, NZ), f32),
            pltpu.VMEM((3, 4, NY, NZ), f32),
            pltpu.VMEM((3, 4, NY, NZ), f32),
            pltpu.VMEM((TABLE, LANES), f32),
            pltpu.SMEM((8, LANES), jnp.int32),
            pltpu.SemaphoreType.DMA((4,)),
        ],
        compiler_params=params(),
    )(*arguments)


def pick_kernel(returned, back, out):
    chosen = back[...]
    for c in range(3):
        both = jnp.concatenate(
            [returned[pl.ds(3 * slot + c, LANES, stride=6), :] for slot in range(2)], axis=0
        )
        high, middle, low = split_3(both)
        out[c] = dot(chosen, high, NN) + dot(chosen, middle, NN) + dot(chosen, low, NN)


def pick(returned, back):
    return pl.pallas_call(
        pick_kernel,
        out_shape=jax.ShapeDtypeStruct((3, LANES, LANES), f32),
        in_specs=[vmem()] * 2,
        out_specs=vmem(),
        compiler_params=params(),
    )(returned, back)


def exchange(values):
    shape = values.shape
    values = values.reshape(LANES, 1, -1)
    values = lax.all_to_all(values, "slab", split_axis=0, concat_axis=0, tiled=True)
    return values.reshape(shape)


def swap(values, first):
    count = lax.axis_size("slab")
    pairs = []
    for i in range(first, count + first, 2):
        a, b = i % count, (i + 1) % count
        pairs += [(a, b), (b, a)]
    return lax.ppermute(values, "slab", pairs)


def body(velocity, node_coords, node_force, block_slab, block_offset):
    turned_picks = window_picks()
    sent, back = prep(
        jnp.transpose(node_coords, (1, 0, 2)),
        jnp.transpose(node_force, (1, 0, 2)),
        jnp.transpose(block_slab, (1, 0)),
        jnp.transpose(block_offset, (1, 0)),
    )
    got = exchange(sent)
    odd = lax.axis_index("slab") % 2 == 1
    first, last = velocity[:, :SUBSTEPS], velocity[:, CX - SUBSTEPS :]
    cross = swap(jnp.where(odd, last, first), 1)
    same = swap(jnp.where(odd, first, last), 0)
    far, near, grid, rows, weights_z, stacks = spread(got, turned_picks)
    far = swap(far, 1)
    near = swap(near, 0)
    inside = inner(velocity, same, cross, grid, rows, weights_z, stacks)
    field, sums = edge(far, near, grid, rows, weights_z, stacks, *inside)
    node_velocity = pick(exchange(sums), back)
    return field, jnp.transpose(node_velocity, (1, 0, 2))


def solution(mesh):
    return jax.shard_map(
        body,
        mesh=mesh,
        in_specs=(
            P(None, "slab", None, None),
            P("slab", None, None),
            P("slab", None, None),
            P("slab", None),
            P("slab", None),
        ),
        out_specs=(P(None, "slab", None, None), P("slab", None, None)),
        check_vma=False,
    )
```

```python
import jax
import jax.numpy as jnp
from jax import lax
from jax.experimental import pallas as pl
from jax.experimental.pallas import tpu as pltpu
from jax.sharding import PartitionSpec as P

CX = 8
NY = 32
NZ = 128
SUBSTEPS = 3
LANES = 128
WINDOWS = 25
GROUP = 16

time_step = 0.1
viscosity = 0.2

f32 = jnp.float32
bf16 = jnp.bfloat16

COS_TERMS = (
    0.7071067481276141,
    -0.21808909214261787,
    0.011209883548645258,
    -0.0002299265021950359,
    2.3703615380631122e-06,
)

VMEM_LIMIT = 24 * 1024 * 1024
VMEM_ALL = 60 * 1024 * 1024


def vmem():
    return pl.BlockSpec(memory_space=pltpu.VMEM)


def anywhere():
    return pl.BlockSpec(memory_space=pl.ANY)


def params(limit=VMEM_LIMIT):
    return pltpu.CompilerParams(vmem_limit_bytes=limit)


def phi(distance):
    t = jnp.minimum(distance * distance, 4.0)
    total = COS_TERMS[4] * t + COS_TERMS[3]
    for term in (COS_TERMS[2], COS_TERMS[1], COS_TERMS[0]):
        total = total * t + term
    return total * total


def split_2(values):
    high = values.astype(bf16).astype(f32)
    return high, values - high


def split_3(values):
    high = values.astype(bf16)
    rest = values - high.astype(f32)
    middle = rest.astype(bf16)
    low = (rest - middle.astype(f32)).astype(bf16)
    return high, middle, low


def dot(a, b, dims):
    return lax.dot_general(a, b, (dims, ((), ())), preferred_element_type=f32)


NN = ((1,), (0,))
NT = ((1,), (1,))


TABLE = WINDOWS * 96
EDGES = (0, 1, 6, 7)
HALO = (-2, -1, CX, CX + 1)
MIDDLE = (2, 3, 4, 5)
ORDER = EDGES + MIDDLE
SENT = 12
REACH = (CX - 4.0, 5.0, 5.0)


def fill_picks(picks):
    row = lax.broadcasted_iota(jnp.int32, (2 * LANES, LANES), 0)
    lane = lax.broadcasted_iota(jnp.int32, (2 * LANES, LANES), 1)
    apart = row - (lane >> 6) * 128 - ((lane >> 3) & 3) * 32 - (lane & 7)
    for start in range(WINDOWS):
        chosen = jnp.where(apart == start, 1.0, 0.0)
        picks[:, start * LANES : (start + 1) * LANES] = chosen.astype(bf16)


def turned_picks_kernel(turned):
    row = lax.broadcasted_iota(jnp.int32, (LANES, 2 * LANES), 0)
    lane = lax.broadcasted_iota(jnp.int32, (LANES, 2 * LANES), 1)
    apart = lane - ((row >> 3) & 7) * 32 - (row & 7)
    for start in range(WINDOWS):
        chosen = jnp.where(apart == start, 1.0, 0.0)
        turned[start * LANES : (start + 1) * LANES] = chosen.astype(bf16)


def window_picks():
    return pl.pallas_call(
        turned_picks_kernel,
        out_shape=jax.ShapeDtypeStruct((WINDOWS * LANES, 2 * LANES), bf16),
        out_specs=vmem(),
        compiler_params=params(),
        cost_estimate=pl.CostEstimate(
            flops=2_000_000_000, bytes_accessed=4_000_000, transcendentals=0
        ),
    )()


def prep_kernel(coords_in, force_in, slab_in, offset_in, out, back, coords, force, slab, offset, sems):
    copies = [
        pltpu.make_async_copy(source, target, sems.at[i])
        for i, (source, target) in enumerate(
            ((slab_in, slab), (offset_in, offset), (coords_in, coords), (force_in, force))
        )
    ]
    for copy in copies:
        copy.start()
    row = lax.broadcasted_iota(jnp.int32, (LANES, LANES), 0)
    col = lax.broadcasted_iota(jnp.int32, (LANES, LANES), 1)
    before = (row < col).astype(f32).astype(bf16)
    copies[0].wait()
    hot = (jnp.broadcast_to(slab[...], (LANES, LANES)) == row).astype(f32)
    rank = dot(hot.astype(bf16), before, NN)
    first = jnp.where(rank < 0.5, hot, 0.0)
    second = hot - first
    both = jnp.concatenate([first, second], axis=0).astype(bf16)
    copies[1].wait()
    offsets = offset[...].astype(f32)
    corners = [None] + [
        jnp.broadcast_to(offsets[i : i + 1], (LANES, LANES)).T for i in range(2)
    ]
    for quantity in range(6):
        if quantity % 3 == 0:
            copies[2 + quantity // 3].wait()
        if quantity < 3:
            source = coords[quantity] * REACH[quantity]
            if quantity:
                source = source + corners[quantity]
        else:
            source = force[quantity - 3]
        high, middle, low = split_3(source)
        placed = dot(both, high, NN) + dot(both, middle, NN) + dot(both, low, NN)
        for slot in range(2):
            out[pl.ds(slot * 6 + quantity, LANES, stride=SENT), :] = placed[
                slot * LANES : (slot + 1) * LANES
            ]
    back[:, :LANES] = first.T.astype(bf16)
    back[:, LANES:] = second.T.astype(bf16)


def prep(coords, force, slab, offset):
    return pl.pallas_call(
        prep_kernel,
        out_shape=(
            jax.ShapeDtypeStruct((SENT * LANES, LANES), f32),
            jax.ShapeDtypeStruct((LANES, 2 * LANES), bf16),
        ),
        in_specs=[anywhere()] * 4,
        out_specs=(vmem(), vmem()),
        scratch_shapes=[
            pltpu.VMEM((3, LANES, LANES), f32),
            pltpu.VMEM((3, LANES, LANES), f32),
            pltpu.VMEM((1, LANES), jnp.int32),
            pltpu.VMEM((2, LANES), jnp.int32),
            pltpu.SemaphoreType.DMA((4,)),
        ],
        compiler_params=params(VMEM_ALL),
    )(coords, force, slab, offset)


def stack_2(values):
    high, low = split_2(values)
    return jnp.concatenate([high, low], axis=0).astype(bf16)


def joint_stack(weight_x, weight_y):
    return stack_2(jnp.concatenate([weight_x[a : a + 1] * weight_y for a in ORDER], axis=0))


def spread_pair(load, stack):
    turned = stack.T
    out = dot(load, jnp.concatenate([turned, turned], axis=0), NN)
    return jnp.concatenate([out[:24, :LANES], out[24:, LANES:]], axis=0)


def gather_windows(total, rows, parts, index):
    for sub in range(GROUP):
        for slot in range(2):
            row = rows[slot, index * GROUP + sub]
            for c in range(3):
                start = slot * 24 + c * 8
                total[pl.ds(row + 32 * c, 8), :] += parts[sub, start : start + 8]


def spread_planes(total, turned_picks):
    cells = jnp.zeros((192, 2 * LANES), f32)
    for y in range(0, WINDOWS, 2):
        wide = min(2, WINDOWS - y)
        both = [total[(y + i) * 96 : (y + i + 1) * 96] for i in range(wide)]
        both = both[0] if wide == 1 else jnp.concatenate(both, axis=1)
        chosen = turned_picks[y * LANES : (y + wide) * LANES]
        cells = cells + dot(stack_2(both), chosen, NN)
    cells = (cells[:96] + cells[96:]) * time_step
    cells = jnp.concatenate([cells, jnp.zeros((32, 2 * LANES), f32)], axis=0).T
    return {p: cells[i * NY : (i + 1) * NY] for i, p in enumerate(ORDER)}


def spread_kernel(
    got, turned_picks, far, near, grid, rows_out, weights_z, stacks, total, places, parts, rows, sem
):
    lane = lax.broadcasted_iota(jnp.int32, (LANES, LANES), 1)
    start = jnp.zeros((LANES, LANES), f32)
    for slot in range(2):
        firsts = []
        for dim in (1, 2):
            place = got[pl.ds(slot * 6 + dim, LANES, stride=SENT), :]
            least = jnp.floor(jnp.min(place, axis=1, keepdims=True)) - 1.0
            firsts.append(jnp.clip(least, 0.0, WINDOWS - 1.0))
            places[slot * 2 + dim - 1] = place - firsts[-1]
        start = jnp.where(lane == slot, firsts[0] * 96.0 + firsts[1], start)
    rows_out[...] = start.T[:8].astype(jnp.int32)
    copy = pltpu.make_async_copy(rows_out, rows, sem)
    copy.start()
    total[...] = jnp.zeros_like(total)
    taps = lax.broadcasted_iota(jnp.int32, (8, LANES), 0).astype(f32)

    def compute(index):
        for sub in range(GROUP):
            device = index * GROUP + sub
            load, stack = [], []
            for slot in range(2):
                source = device * SENT + slot * 6
                weight_x = phi(taps - 1.0 - got[pl.ds(source, 1), :])
                weight_y = phi(taps - places[slot * 2, pl.ds(device, 1), :])
                weight_z = phi(taps - places[slot * 2 + 1, pl.ds(device, 1), :])
                weights_z[device, slot] = weight_z
                stack.append(joint_stack(weight_x, weight_y))
                load += [got[pl.ds(source + 3 + c, 1), :] * weight_z for c in range(3)]
            load = jnp.concatenate(split_2(jnp.concatenate(load, axis=0)), axis=1).astype(bf16)
            stack = jnp.concatenate(stack, axis=0)
            stacks[device] = stack
            parts[sub] = spread_pair(load, stack)

    compute(0)
    copy.wait()
    for index in range(1, LANES // GROUP):
        gather_windows(total, rows, parts, index - 1)
        compute(index)
    gather_windows(total, rows, parts, LANES // GROUP - 1)
    planes = spread_planes(total, turned_picks)
    odd = lax.axis_index("slab") % 2 == 1
    for a in range(CX):
        grid[a] = planes[a]
    for a in range(2):
        near[a] = jnp.where(odd, planes[a], planes[CX - 2 + a])
        far[a] = jnp.where(odd, planes[CX - 2 + a], planes[a])


def spread(got, turned_picks):
    return pl.pallas_call(
        spread_kernel,
        out_shape=(
            jax.ShapeDtypeStruct((2, NY, LANES), f32),
            jax.ShapeDtypeStruct((2, NY, LANES), f32),
            jax.ShapeDtypeStruct((CX, NY, LANES), f32),
            jax.ShapeDtypeStruct((8, LANES), jnp.int32),
            jax.ShapeDtypeStruct((LANES, 2, 8, LANES), f32),
            jax.ShapeDtypeStruct((LANES, 256, LANES), bf16),
        ),
        in_specs=[vmem()] * 2,
        out_specs=(vmem(),) * 6,
        scratch_shapes=[
            pltpu.VMEM((TABLE, LANES), f32),
            pltpu.VMEM((4, LANES, LANES), f32),
            pltpu.VMEM((GROUP, 48, LANES), f32),
            pltpu.SMEM((8, LANES), jnp.int32),
            pltpu.SemaphoreType.DMA,
        ],
        compiler_params=params(),
    )(got, turned_picks)


def forcing_of(cells, c):
    lane = lax.broadcasted_iota(jnp.int32, (NY, NZ), 1)
    if c:
        cells = pltpu.roll(cells, LANES - 32 * c, 1)
    return jnp.where(lane < 32, cells, 0.0)


def fluid_plane(load, cells, p):
    centers = [load(c, p) for c in range(3)]
    results = []
    for c in range(3):
        center = centers[c]
        x_plus, x_minus = load(c, p + 1), load(c, p - 1)
        y_plus, y_minus = pltpu.roll(center, NY - 1, 0), pltpu.roll(center, 1, 0)
        z_plus, z_minus = pltpu.roll(center, NZ - 1, 1), pltpu.roll(center, 1, 1)
        around = (x_plus + x_minus) + (y_plus + y_minus) + (z_plus + z_minus)
        advect = (
            centers[0] * (x_plus - x_minus)
            + centers[1] * (y_plus - y_minus)
            + centers[2] * (z_plus - z_minus)
        )
        moved = (
            (1.0 - 6.0 * time_step * viscosity) * center
            + (time_step * viscosity) * around
            - (0.5 * time_step) * advect
        )
        results.append(moved if cells is None else moved + forcing_of(cells, c))
    return results


def packed_plane(parts):
    lane = lax.broadcasted_iota(jnp.int32, (NY, LANES), 1)
    cells = jnp.where(lane < 32, parts[0], 0.0)
    for c in (1, 2):
        moved = pltpu.roll(parts[c], 32 * c, 1)
        cells = jnp.where((lane >= 32 * c) & (lane < 32 * c + 32), moved, cells)
    return cells


def fill_table(table, planes, picks):
    cells = jnp.concatenate([packed_plane(parts) for parts in planes], axis=0).T[:96]
    split = jnp.concatenate(split_2(cells), axis=1).astype(bf16)
    for y in range(0, WINDOWS, 2):
        wide = min(2, WINDOWS - y)
        both = dot(split, picks[:, y * LANES : (y + wide) * LANES], NN)
        for i in range(wide):
            table[(y + i) * 96 : (y + i + 1) * 96] = both[:, i * LANES : (i + 1) * LANES]


def fold(a, b, width):
    if b is None:
        return a + pltpu.roll(a, width, 0)
    bit = (lax.broadcasted_iota(jnp.int32, (8, LANES), 0) & width) == 0
    return jnp.where(bit, a, b) + pltpu.roll(jnp.where(bit, b, a), width, 0)


def window_sums(table, rows, device, stack, weights_z, first):
    cells = []
    for slot in range(2):
        row = rows[slot, device]
        for c in range(3):
            cells.append(table[pl.ds(row + 32 * c, 8), :])
    high = jnp.concatenate([stack[first : first + 32], stack[128 + first : 160 + first]], axis=1)
    low = jnp.concatenate([stack[64 + first : 96 + first], stack[192 + first : 224 + first]], axis=1)
    both = jnp.concatenate([high, low, high, low], axis=0)
    values = dot(jnp.concatenate(cells, axis=0).astype(bf16), both, NN)
    v = []
    for slot in range(2):
        weight_z = weights_z[device, slot]
        for c in range(3):
            start = slot * 24 + c * 8
            v.append(values[start : start + 8, slot * LANES : (slot + 1) * LANES] * weight_z)
    low = fold(fold(v[0], v[1], 1), fold(v[2], v[3], 1), 2)
    high = fold(fold(v[4], v[5], 1), None, 2)
    return fold(low, high, 4)[:6]


def halo_reader(inside, same, cross, depth):
    odd = lax.axis_index("slab") % 2 == 1

    def load(c, p):
        if p < 0:
            return jnp.where(odd, same[c, p + depth], cross[c, p + depth])
        if p >= CX:
            return jnp.where(odd, cross[c, p - CX], same[c, p - CX])
        return inside[c, p]

    return load


def inner_kernel(
    velocity, same, cross, grid, rows_in, weights_z, stacks,
    step_1, step_2, middle, partial, picks, unforced, table, rows, sem
):
    copy = pltpu.make_async_copy(rows_in, rows, sem)
    copy.start()
    fill_picks(picks)
    load_0 = halo_reader(velocity, same, cross, SUBSTEPS)
    for i, p in enumerate(HALO):
        for c, value in enumerate(fluid_plane(load_0, None, p)):
            unforced[c, i] = value
    for p in range(CX):
        for c, value in enumerate(fluid_plane(load_0, grid[p], p)):
            step_1[c, p] = value
    for p in range(1, CX - 1):
        for c, value in enumerate(fluid_plane(lambda c, p: step_1[c, p], grid[p], p)):
            step_2[c, p] = value
    planes = []
    for p in MIDDLE:
        planes.append(fluid_plane(lambda c, p: step_2[c, p], grid[p], p))
        for c in range(3):
            middle[c, p - MIDDLE[0]] = planes[-1][c]
    fill_table(table, planes, picks)
    copy.wait()

    for device in range(LANES):
        partial[device * 6 : device * 6 + 6] = window_sums(
            table, rows, device, stacks[device], weights_z, 32
        )


def inner(*arguments):
    return pl.pallas_call(
        inner_kernel,
        out_shape=(
            jax.ShapeDtypeStruct((3, CX, NY, NZ), f32),
            jax.ShapeDtypeStruct((3, CX, NY, NZ), f32),
            jax.ShapeDtypeStruct((3, len(MIDDLE), NY, NZ), f32),
            jax.ShapeDtypeStruct((6 * LANES, LANES), f32),
            jax.ShapeDtypeStruct((2 * LANES, WINDOWS * LANES), bf16),
            jax.ShapeDtypeStruct((3, len(HALO), NY, NZ), f32),
        ),
        in_specs=[vmem()] * 7,
        out_specs=(vmem(),) * 6,
        scratch_shapes=[
            pltpu.VMEM((TABLE, LANES), f32),
            pltpu.SMEM((8, LANES), jnp.int32),
            pltpu.SemaphoreType.DMA,
        ],
        compiler_params=params(),
        cost_estimate=pl.CostEstimate(
            flops=6_000_000_000, bytes_accessed=8_000_000, transcendentals=0
        ),
    )(*arguments)


def edge_kernel(
    far, near, grid, rows_in, weights_z, stacks,
    step_1, step_2, middle, partial, picks, unforced,
    field, out, ends_1, ends_2, ends_3, table, rows, sems
):
    copies = [pltpu.make_async_copy(rows_in, rows, sems.at[0])]
    copies.append(
        pltpu.make_async_copy(middle, field.at[:, pl.ds(MIDDLE[0], len(MIDDLE))], sems.at[1])
    )
    for i, p in enumerate((0, CX - 2)):
        source, target = ends_3.at[:, pl.ds(2 * i, 2)], field.at[:, pl.ds(p, 2)]
        copies.append(pltpu.make_async_copy(source, target, sems.at[2 + i]))
    copies[0].start()
    copies[1].start()
    odd = lax.axis_index("slab") % 2 == 1

    def cells(p):
        if p < 0:
            return jnp.where(odd, near[p + 2], far[p + 2])
        if p >= CX:
            return jnp.where(odd, far[p - CX], near[p - CX])
        return grid[p]

    def reader(ends, inside, low):
        def load(c, p):
            for i, q in enumerate(low):
                if p == q:
                    return ends[c, i]
            return inside[c, p]

        return load

    planes_2 = (-1, 0, CX - 1, CX)
    for i, p in enumerate(HALO):
        for c in range(3):
            ends_1[c, i] = unforced[c, i] + forcing_of(cells(p), c)
    load_1 = reader(ends_1, step_1, HALO)
    for i, p in enumerate(planes_2):
        for c, value in enumerate(fluid_plane(load_1, cells(p), p)):
            ends_2[c, i] = value
    load_2 = reader(ends_2, step_2, planes_2)
    planes = []
    for i, p in enumerate(EDGES):
        planes.append(fluid_plane(load_2, cells(p), p))
        for c in range(3):
            ends_3[c, i] = planes[-1][c]
    copies[2].start()
    copies[3].start()
    fill_table(table, planes, picks)
    copies[0].wait()

    for device in range(LANES):
        own = slice(device * 6, device * 6 + 6)
        out[own] = partial[own] + window_sums(
            table, rows, device, stacks[device], weights_z, 0
        )
    for copy in copies[1:]:
        copy.wait()


def edge(*arguments):
    return pl.pallas_call(
        edge_kernel,
        out_shape=(
            jax.ShapeDtypeStruct((3, CX, NY, NZ), f32),
            jax.ShapeDtypeStruct((6 * LANES, LANES), f32),
        ),
        in_specs=[vmem()] * 12,
        out_specs=(anywhere(), vmem()),
        scratch_shapes=[
            pltpu.VMEM((3, 4, NY, NZ), f32),
            pltpu.VMEM((3, 4, NY, NZ), f32),
            pltpu.VMEM((3, 4, NY, NZ), f32),
            pltpu.VMEM((TABLE, LANES), f32),
            pltpu.SMEM((8, LANES), jnp.int32),
            pltpu.SemaphoreType.DMA((4,)),
        ],
        compiler_params=params(),
    )(*arguments)


def pick_kernel(returned, back, out):
    chosen = back[...]
    for c in range(3):
        both = jnp.concatenate(
            [returned[pl.ds(3 * slot + c, LANES, stride=6), :] for slot in range(2)], axis=0
        )
        high, middle, low = split_3(both)
        out[c] = dot(chosen, high, NN) + dot(chosen, middle, NN) + dot(chosen, low, NN)


def pick(returned, back):
    return pl.pallas_call(
        pick_kernel,
        out_shape=jax.ShapeDtypeStruct((3, LANES, LANES), f32),
        in_specs=[vmem()] * 2,
        out_specs=vmem(),
        compiler_params=params(),
    )(returned, back)


def exchange(values):
    shape = values.shape
    values = values.reshape(LANES, 1, -1)
    values = lax.all_to_all(values, "slab", split_axis=0, concat_axis=0, tiled=True)
    return values.reshape(shape)


def swap(values, first):
    count = lax.axis_size("slab")
    pairs = []
    for i in range(first, count + first, 2):
        a, b = i % count, (i + 1) % count
        pairs += [(a, b), (b, a)]
    return lax.ppermute(values, "slab", pairs)


def body(velocity, node_coords, node_force, block_slab, block_offset):
    turned_picks = window_picks()
    sent, back = prep(
        jnp.transpose(node_coords, (1, 0, 2)),
        jnp.transpose(node_force, (1, 0, 2)),
        jnp.transpose(block_slab, (1, 0)),
        jnp.transpose(block_offset, (1, 0)),
    )
    got = exchange(sent)
    odd = lax.axis_index("slab") % 2 == 1
    first, last = velocity[:, :SUBSTEPS], velocity[:, CX - SUBSTEPS :]
    cross = swap(jnp.where(odd, last, first), 1)
    same = swap(jnp.where(odd, first, last), 0)
    far, near, grid, rows, weights_z, stacks = spread(got, turned_picks)
    far = swap(far, 1)
    near = swap(near, 0)
    inside = inner(velocity, same, cross, grid, rows, weights_z, stacks)
    field, sums = edge(far, near, grid, rows, weights_z, stacks, *inside)
    node_velocity = pick(exchange(sums), back)
    return field, jnp.transpose(node_velocity, (1, 0, 2))


def solution(mesh):
    return jax.shard_map(
        body,
        mesh=mesh,
        in_specs=(
            P(None, "slab", None, None),
            P("slab", None, None),
            P("slab", None, None),
            P("slab", None),
            P("slab", None),
        ),
        out_specs=(P(None, "slab", None, None), P("slab", None, None)),
        check_vma=False,
    )
```
